32 devices in a mesh: dp: 2 (over y), ctx: 16 (over z, x, core).
Axes of the slice: x: 2, y: 2, z: 4, core: 2. Of those that a mesh axis runs over, the one named last changes fastest.
Arguments:
- embeds: bfloat16 [2, 65536, 128], P('dp', 'ctx'), may hold values from -6 to 6
- perturb: bfloat16 [2, 65536, 128], P('dp', 'ctx'), may hold values from -1.5 to 1.5
- cotangent: bfloat16 [2, 65536, 128], P('dp', 'ctx'), may hold values from -6 to 6
- filter_spectrum: float32 [2, 256, 256, 128], P(None, 'ctx'), may hold values from -4.2 to 4.2
- skip_gain: float32 [128], replicated, may hold values from 0.25 to 1.75
Outputs:
- clean_output: bfloat16 [2, 65536, 128], P('dp', 'ctx')
- filter_grad: float32 [2, 256, 256, 128], P(None, 'ctx', 'dp')
The draws below stay inside these ranges and needn't reach their ends.
All inputs are finite; a program needn't handle non-finite values.
Results may differ from the reference program's by a relative error of at most 0.022.
Values may be sent and summed in bfloat16 or wider, within the bound.
No kernel may reach another device: no remote copies, remote signals or barrier semaphores. Data moves between devices by JAX's collectives and lax.ppermute only.
A program may use at most 128 MiB of HBM per device.

```python
import jax
import jax.numpy as jnp
from jax import lax

N1 = 256
N2 = 256
CH = 128
BATCH = 2
SEQLEN = 65536


def shard_levels(stream_key, shape, cuts, low, high):
    def one(dim, blocks):
        draws = jax.random.uniform(jax.random.fold_in(jax.random.fold_in(stream_key, 6), dim), (blocks,), jnp.float32, low / len(cuts), high / len(cuts))
        return jnp.repeat(jnp.exp(draws), shape[dim] // blocks).reshape((-1,) + (1,) * (len(shape) - dim - 1))

    gain = one(*cuts[0])
    for cut in cuts[1:]:
        gain = gain * one(*cut)
    return gain


def gaussian(rng, shape, spread, most, shards=(), kind=jnp.bfloat16):
    level = shard_levels(rng, shape, shards, -0.22, 0.18) if shards else 1.0
    array = jax.random.normal(rng, shape, jnp.float32) * spread * level
    return jnp.minimum(jnp.maximum(array, -most), most).astype(kind)


def setup_inputs(seed: int = 0) -> dict:
    seeds = jax.random.split(jax.random.key(seed), 6)
    embeds = gaussian(seeds[0], (BATCH, SEQLEN, CH), 1.0, 6.0, ((0, 2), (1, 16)))
    perturb = gaussian(seeds[1], (BATCH, SEQLEN, CH), 0.25, 1.5, ((0, 2), (1, 16)))
    cotangent = gaussian(seeds[2], (BATCH, SEQLEN, CH), 1.0, 6.0, ((0, 2), (1, 16)))
    filter_spectrum = gaussian(seeds[3], (2, N1, N2, CH), 0.7, 4.2, ((1, 16),), jnp.float32)
    skip_gain = jnp.clip(1.0 + 0.15 * jax.random.normal(seeds[4], (CH,), jnp.float32), 0.25, 1.75)
    return dict(embeds=embeds, perturb=perturb, cotangent=cotangent, filter_spectrum=filter_spectrum, skip_gain=skip_gain)


two_pi = 6.283185307179586
smart_weight = 2.0


def trig_table(period):
    row_ids = jnp.arange(period, dtype=jnp.int32)
    exponent = (row_ids[:, None] * row_ids[None, :]) % period
    phase_angle = exponent.astype(jnp.float32) * (two_pi / period)
    return jnp.cos(phase_angle).astype(jnp.bfloat16), jnp.sin(phase_angle).astype(jnp.bfloat16)


def left_mul(table, values):
    flat = values.reshape(values.shape[0], -1)
    return jnp.dot(table, flat, preferred_element_type=jnp.float32).reshape(values.shape)


def right_mul(values, table):
    return jnp.einsum("knc,mn->kmc", values.astype(jnp.float32), table.astype(jnp.float32))


def reference(embeds, perturb, cotangent, filter_spectrum, skip_gain):
    cos_one, sin_one = trig_table(N1)
    cos_two, sin_two = trig_table(N2)
    k_ids = jnp.arange(N1, dtype=jnp.int32)
    n_ids = jnp.arange(N2, dtype=jnp.int32)
    exponent = (k_ids[:, None] * n_ids[None, :]) % (N1 * N2)
    phase_angle = exponent.astype(jnp.float32) * (two_pi / (N1 * N2))
    tw_cos = jnp.cos(phase_angle)[:, :, None]
    tw_sin = jnp.sin(phase_angle)[:, :, None]
    inv_len = 1.0 / (N1 * N2)
    filter_real = filter_spectrum[0]
    filter_imag = filter_spectrum[1]

    def forward(signal):
        part_real = left_mul(cos_one, signal)
        part_imag = -left_mul(sin_one, signal)
        half_real = (part_real * tw_cos + part_imag * tw_sin).astype(jnp.bfloat16)
        half_imag = (part_imag * tw_cos - part_real * tw_sin).astype(jnp.bfloat16)
        spec_real = right_mul(half_real, cos_two) + right_mul(half_imag, sin_two)
        spec_imag = right_mul(half_imag, cos_two) - right_mul(half_real, sin_two)
        return spec_real, spec_imag

    def filtered_by(spec_real, spec_imag):
        prod_real = (filter_real * spec_real - filter_imag * spec_imag).astype(jnp.bfloat16)
        prod_imag = (filter_real * spec_imag + filter_imag * spec_real).astype(jnp.bfloat16)
        part_real = right_mul(prod_real, cos_two) - right_mul(prod_imag, sin_two)
        part_imag = right_mul(prod_imag, cos_two) + right_mul(prod_real, sin_two)
        half_real = (part_real * tw_cos - part_imag * tw_sin).astype(jnp.bfloat16)
        half_imag = (part_imag * tw_cos + part_real * tw_sin).astype(jnp.bfloat16)
        filtered = ((left_mul(cos_one, half_real) - left_mul(sin_one, half_imag)) * inv_len).astype(jnp.bfloat16)
        return lax.optimization_barrier(filtered).astype(jnp.float32)

    seq_count = embeds.shape[0]
    channels = embeds.shape[2]
    outputs = []
    grad_total = jnp.zeros((2, N1, N2, channels), jnp.float32)
    for seq_index in range(seq_count):
        clean_rows = embeds[seq_index].reshape(N1, N2, channels)
        clean_wide = clean_rows.astype(jnp.float32)
        shifted = (clean_wide + perturb[seq_index].reshape(N1, N2, channels).astype(jnp.float32)).astype(jnp.bfloat16)
        shifted_wide = shifted.astype(jnp.float32)
        clean_real, clean_imag = forward(clean_rows)
        shift_real, shift_imag = forward(shifted)
        conv_clean = filtered_by(clean_real, clean_imag)
        conv_shift = filtered_by(shift_real, shift_imag)
        clean_y = clean_wide * conv_clean + skip_gain * clean_wide
        shifted_y = shifted_wide * conv_shift + skip_gain * shifted_wide
        outputs.append(clean_y.astype(jnp.bfloat16).reshape(N1 * N2, channels))
        smooth_gap = shifted_y - clean_y
        cot_wide = cotangent[seq_index].reshape(N1, N2, channels).astype(jnp.float32)
        err_clean = (clean_wide * (cot_wide - smart_weight * smooth_gap)).astype(jnp.bfloat16)
        err_shift = (shifted_wide * (smart_weight * smooth_gap)).astype(jnp.bfloat16)
        errc_real, errc_imag = forward(err_clean)
        errs_real, errs_imag = forward(err_shift)
        grad_real = ((errc_real * clean_real + errc_imag * clean_imag) + (errs_real * shift_real + errs_imag * shift_imag)) * inv_len
        grad_imag = ((errc_imag * clean_real - errc_real * clean_imag) + (errs_imag * shift_real - errs_real * shift_imag)) * inv_len
        grad_total = grad_total + jnp.stack([grad_real, grad_imag], 0)
    return jnp.stack(outputs, 0), grad_total
```

```python
import jax
import jax.numpy as jnp
import numpy as np
from jax import lax
from jax.experimental import pallas as pl
from jax.experimental.pallas import tpu as pltpu
from jax.sharding import PartitionSpec as P

N1 = 256
N2 = 256
BF16 = jnp.bfloat16
F32 = jnp.float32

two_pi = 6.283185307179586
smart_weight = 2.0


def tables():
    ids = np.arange(N1)
    phase = (ids[:, None] * ids[None, :] % N1) * (two_pi / N1)
    cos_table, sin_table = np.cos(phase), np.sin(phase)
    split_rows = np.concatenate([cos_table, -sin_table], 0)
    forward = np.block([[cos_table, -sin_table], [sin_table, cos_table]])
    inverse = np.block([[cos_table, sin_table], [-sin_table, cos_table]])
    join_rows = np.concatenate([cos_table, -sin_table], 1) / (N1 * N2)
    angle = (ids[:, None] * ids[None, :]) * (two_pi / (N1 * N2))
    twiddle = np.stack([np.cos(angle), np.sin(angle)], 0)
    small = [jnp.asarray(t.astype(jnp.bfloat16)) for t in (split_rows, forward, inverse, join_rows)]
    return (*small, jnp.asarray(twiddle.astype(np.float32)))


def dot(a, b):
    return jnp.dot(a, b, preferred_element_type=F32)


def half_forward(rows, tw_cos, tw_sin):
    part_real, part_imag = rows[:N1], rows[N1:]
    out_real = part_real * tw_cos + part_imag * tw_sin
    out_imag = part_imag * tw_cos - part_real * tw_sin
    return jnp.concatenate([out_real.astype(BF16), out_imag.astype(BF16)], 1)


def conv_kernel(
    gain_ref, ep_ref, filt_ref, split_ref, fwd_ref, inv_ref, join_ref, tw_ref,
    send_ref, gap_ref, spec_ref, grad_ref,
):
    q, d = pl.program_id(0), pl.program_id(1)
    tw_cos, tw_sin = tw_ref[0], tw_ref[1]
    clean = ep_ref[0, :, 0, 0].reshape(N1, N2)
    clean_wide = clean.astype(F32)
    shifted = (clean_wide + ep_ref[0, :, 1, 0].reshape(N1, N2).astype(F32)).astype(BF16)
    shifted_wide = shifted.astype(F32)
    half = [half_forward(dot(split_ref[...], x), tw_cos, tw_sin) for x in (clean, shifted)]
    spec = [dot(h, fwd_ref[...]) for h in half]
    spec_ref[0, 0] = spec[0]
    filter_real = filt_ref[0, :, 0, 0].reshape(N1, N2).astype(F32)
    filter_imag = filt_ref[1, :, 0, 0].reshape(N1, N2).astype(F32)
    gain = gain_ref[q]
    ys = []
    for x_wide, x_spec in zip((clean_wide, shifted_wide), spec):
        real, imag = x_spec[:, :N2], x_spec[:, N2:]
        prod_real = (filter_real * real - filter_imag * imag).astype(BF16)
        prod_imag = (filter_real * imag + filter_imag * real).astype(BF16)
        back = dot(jnp.concatenate([prod_real, prod_imag], 1), inv_ref[...])
        back_real, back_imag = back[:, :N2], back[:, N2:]
        mixed_real = (back_real * tw_cos - back_imag * tw_sin).astype(BF16)
        mixed_imag = (back_imag * tw_cos + back_real * tw_sin).astype(BF16)
        conv = dot(join_ref[...], jnp.concatenate([mixed_real, mixed_imag], 0))
        conv = conv.astype(BF16).astype(F32)
        ys.append(x_wide * conv + gain * x_wide)
    send_ref[0, :, 0, 0] = ys[0].astype(BF16).reshape(send_ref.shape[1], -1, N2)
    gap = smart_weight * (ys[1] - ys[0])
    gap_ref[0, 0] = gap
    err = (shifted_wide * gap).astype(BF16)
    err_spec = dot(half_forward(dot(split_ref[...], err), tw_cos, tw_sin), fwd_ref[...])
    add_grad(grad_ref, d, err_spec, spec[1])


def add_grad(grad_ref, d, err_spec, spec):
    err_real, err_imag = err_spec[:, :N2], err_spec[:, N2:]
    real, imag = spec[:, :N2], spec[:, N2:]
    term_real = err_real * real + err_imag * imag
    term_imag = err_imag * real - err_real * imag

    @pl.when(d == 0)
    def _():
        grad_ref[0, 0] = term_real
        grad_ref[0, 1] = term_imag

    @pl.when(d != 0)
    def _():
        grad_ref[0, 0] += term_real
        grad_ref[0, 1] += term_imag


def grad_kernel(
    ep_ref, cot_ref, gap_ref, spec_ref, part_ref, split_ref, fwd_ref, tw_ref, _, send_ref, sum_ref
):
    d = pl.program_id(1)
    tw_cos, tw_sin = tw_ref[0], tw_ref[1]
    clean = ep_ref[0, :, 0, 0].reshape(N1, N2).astype(F32)
    cot = cot_ref[0, :, 0].reshape(N1, N2).astype(F32)
    err = (clean * (cot - gap_ref[0, 0])).astype(BF16)
    err_spec = dot(half_forward(dot(split_ref[...], err), tw_cos, tw_sin), fwd_ref[...])
    add_grad(sum_ref, d, err_spec, spec_ref[0, 0])

    @pl.when(d == pl.num_programs(1) - 1)
    def _():
        total = ((sum_ref[0] + part_ref[0]) * (1.0 / (N1 * N2))).astype(BF16)
        count = send_ref.shape[0]
        width = N2 // count
        for i in range(count):
            cols = jnp.concatenate([total[0, :, i * width : (i + 1) * width], total[1, :, i * width : (i + 1) * width]], 1)
            send_ref[i, :, 0, 0] = cols.reshape(send_ref.shape[1], -1, 2 * width)


def whole(x):
    return pl.BlockSpec(x.shape, lambda q, d: (0,) * x.ndim)


def conv_call(gain, received, tabs):
    dp, ctx, _, per, rows, _ = received.shape
    split_rows, forward, inverse, join_rows, twiddle = tabs
    return pl.pallas_call(
        conv_kernel,
        grid=(per, dp),
        in_specs=[
            pl.BlockSpec(memory_space=pltpu.SMEM),
            pl.BlockSpec((1, ctx, 2, 1, rows, N2), lambda q, d: (d, 0, 0, q, 0, 0)),
            pl.BlockSpec((dp, ctx, 1, 1, rows, N2), lambda q, d: (0, 0, 2, q, 0, 0)),
            *[whole(t) for t in tabs],
        ],
        out_specs=[
            pl.BlockSpec((1, ctx, 1, 1, rows, N2), lambda q, d: (d, 0, 0, q, 0, 0)),
            pl.BlockSpec((1, 1, N1, N2), lambda q, d: (q, d, 0, 0)),
            pl.BlockSpec((1, 1, N1, 2 * N2), lambda q, d: (q, d, 0, 0)),
            pl.BlockSpec((1, 2, N1, N2), lambda q, d: (q, 0, 0, 0)),
        ],
        out_shape=[
            jax.ShapeDtypeStruct((dp, ctx, 2, per, rows, N2), BF16),
            jax.ShapeDtypeStruct((per, dp, N1, N2), F32),
            jax.ShapeDtypeStruct((per, dp, N1, 2 * N2), F32),
            jax.ShapeDtypeStruct((per, 2, N1, N2), F32),
        ],
        compiler_params=pltpu.CompilerParams(vmem_limit_bytes=40 << 20),
        cost_estimate=pl.CostEstimate(flops=8 * per * dp * N1 * N1 * N1 * 12, bytes_accessed=20 << 20, transcendentals=0),
        name="conv",
    )(gain, received, received, split_rows, forward, inverse, join_rows, twiddle)


def grad_call(received, cot, gap, spec, part, tabs, send):
    dp, ctx, _, per, rows, _ = received.shape
    split_rows, forward, _, _, twiddle = tabs
    return pl.pallas_call(
        grad_kernel,
        grid=(per, dp),
        in_specs=[
            pl.BlockSpec((1, ctx, 1, 1, rows, N2), lambda q, d: (d, 0, 0, q, 0, 0)),
            pl.BlockSpec((1, ctx, 1, rows, N2), lambda q, d: (d, 0, q, 0, 0)),
            pl.BlockSpec((1, 1, N1, N2), lambda q, d: (q, d, 0, 0)),
            pl.BlockSpec((1, 1, N1, 2 * N2), lambda q, d: (q, d, 0, 0)),
            pl.BlockSpec((1, 2, N1, N2), lambda q, d: (q, 0, 0, 0)),
            whole(split_rows),
            whole(forward),
            whole(twiddle),
            pl.BlockSpec(memory_space=pl.ANY),
        ],
        out_specs=pl.BlockSpec((dp, ctx, 1, 1, rows, N2), lambda q, d: (0, 0, 1, q, 0, 0)),
        out_shape=jax.ShapeDtypeStruct(send.shape, BF16),
        scratch_shapes=[pltpu.VMEM((1, 2, N1, N2), F32)],
        input_output_aliases={8: 0},
        compiler_params=pltpu.CompilerParams(vmem_limit_bytes=40 << 20),
        cost_estimate=pl.CostEstimate(flops=2 * per * dp * N1 * N1 * N1 * 6, bytes_accessed=12 << 20, transcendentals=0),
        name="grad",
    )(received, cot, gap, spec, part, split_rows, forward, twiddle, send)


def by_channel_body(embeds, perturb, cotangent, filter_spectrum, skip_gain):
    dp, ctx = lax.axis_size("dp"), lax.axis_size("ctx")
    d, c = lax.axis_index("dp"), lax.axis_index("ctx")
    axes = ("dp", "ctx")
    channels = embeds.shape[2]
    rows = N1 // ctx
    per = channels // (dp * ctx)
    tabs = tables()

    def outward(x):
        return x.reshape(rows * N2, channels).T.reshape(dp * ctx, per, rows, N2)

    filter_part = lax.dynamic_index_in_dim(filter_spectrum, d, 0, keepdims=False).astype(BF16)
    first = jnp.stack([outward(embeds), outward(perturb), outward(filter_part)], 1)
    received = lax.all_to_all(first, axes, 0, 0, tiled=True).reshape(dp, ctx, 3, per, rows, N2)
    cot = lax.all_to_all(outward(cotangent), axes, 0, 0, tiled=True).reshape(dp, ctx, per, rows, N2)
    gain = lax.dynamic_slice(skip_gain, ((d * ctx + c) * per,), (per,))
    send, gap, spec, part = conv_call(gain, received, tabs)
    send = grad_call(received, cot, gap, spec, part, tabs, send)
    last = lax.all_to_all(send.reshape(dp * ctx, 2, per, rows, N2), axes, 0, 0, tiled=True)
    y = last[:, 0].reshape(channels, rows * N2).T.reshape(1, rows * N2, channels)
    grad = last[:, 1].reshape(channels, rows, 2, N2 // dp).transpose(2, 1, 3, 0).astype(F32)
    return y, grad


def trig_table(period):
    row_ids = jnp.arange(period, dtype=jnp.int32)
    exponent = row_ids[:, None] * row_ids[None, :] % period
    phase_angle = exponent.astype(jnp.float32) * (two_pi / period)
    return (jnp.cos(phase_angle).astype(jnp.bfloat16), jnp.sin(phase_angle).astype(jnp.bfloat16))


def twiddle(row_first, row_count, col_first, col_count):
    row_ids = row_first + jnp.arange(row_count, dtype=jnp.int32)
    col_ids = col_first + jnp.arange(col_count, dtype=jnp.int32)
    exponent = row_ids[:, None] * col_ids[None, :] % (N1 * N2)
    phase_angle = exponent.astype(jnp.float32) * (two_pi / (N1 * N2))
    return (jnp.cos(phase_angle)[:, :, None], jnp.sin(phase_angle)[:, :, None])


def first_section(values, col_start):
    cos_table, sin_table = trig_table(N1)
    part_real = jnp.einsum("kn,snmc->skmc", cos_table, values, preferred_element_type=jnp.float32)
    part_imag = -jnp.einsum("kn,snmc->skmc", sin_table, values, preferred_element_type=jnp.float32)
    tw_cos, tw_sin = twiddle(0, N1, col_start, values.shape[2])
    out_real = part_real * tw_cos + part_imag * tw_sin
    out_imag = part_imag * tw_cos - part_real * tw_sin
    return jnp.stack([out_real, out_imag], 1).astype(jnp.bfloat16)


def second_section(section_rows):
    cos_table, sin_table = trig_table(N2)
    with_cos = jnp.einsum(
        "sprnc,kn->sprkc", section_rows, cos_table, preferred_element_type=jnp.float32
    )
    with_sin = jnp.einsum(
        "sprnc,kn->sprkc", section_rows, sin_table, preferred_element_type=jnp.float32
    )
    return jnp.stack([with_cos[:, 0] + with_sin[:, 1], with_cos[:, 1] - with_sin[:, 0]], 1)


def spectral_inverse(product, row_start):
    cos_table, sin_table = trig_table(N2)
    with_cos = jnp.einsum("sprkc,nk->sprnc", product, cos_table, preferred_element_type=jnp.float32)
    with_sin = jnp.einsum("sprkc,nk->sprnc", product, sin_table, preferred_element_type=jnp.float32)
    part_real = with_cos[:, 0] - with_sin[:, 1]
    part_imag = with_cos[:, 1] + with_sin[:, 0]
    tw_cos, tw_sin = twiddle(row_start, product.shape[2], 0, N2)
    out_real = part_real * tw_cos - part_imag * tw_sin
    out_imag = part_imag * tw_cos + part_real * tw_sin
    return jnp.stack([out_real, out_imag], 1).astype(jnp.bfloat16)


def column_inverse(mixed_cols):
    cos_table, sin_table = trig_table(N1)
    with_cos = jnp.einsum(
        "nk,skmc->snmc", cos_table, mixed_cols[:, 0], preferred_element_type=jnp.float32
    )
    with_sin = jnp.einsum(
        "nk,skmc->snmc", sin_table, mixed_cols[:, 1], preferred_element_type=jnp.float32
    )
    return ((with_cos - with_sin) * (1.0 / (N1 * N2))).astype(jnp.bfloat16)


def to_spectrum(section_cols):
    return second_section(
        lax.all_to_all(section_cols, "ctx", split_axis=2, concat_axis=3, tiled=True)
    )


def error_terms(signal, filtered, skip_gain, cotangent_view):
    signal_wide = signal.astype(jnp.float32)
    filtered_wide = lax.optimization_barrier(filtered).astype(jnp.float32)
    outputs = signal_wide * filtered_wide + skip_gain * signal_wide
    clean_y = outputs[0]
    smooth_gap = outputs[1] - clean_y
    err_clean = signal_wide[0] * (cotangent_view.astype(jnp.float32) - smart_weight * smooth_gap)
    err_shift = signal_wide[1] * (smart_weight * smooth_gap)
    return (clean_y, jnp.stack([err_clean, err_shift], 0).astype(jnp.bfloat16))


def body(embeds, perturb, cotangent, filter_spectrum, skip_gain):
    ctx_size = lax.axis_size("ctx")
    ctx_index = lax.axis_index("ctx")
    channels = embeds.shape[2]
    row_count = N1 // ctx_size
    col_count = N2 // ctx_size
    row_start = ctx_index * row_count
    col_start = ctx_index * col_count
    clean_rows = embeds[0].reshape(row_count, N2, channels)
    perturb_rows = perturb[0].reshape(row_count, N2, channels)
    shifted = (clean_rows.astype(jnp.float32) + perturb_rows.astype(jnp.float32)).astype(
        jnp.bfloat16
    )
    inputs = jnp.stack([clean_rows, shifted], 0)
    signal_cols = lax.all_to_all(inputs, "ctx", split_axis=2, concat_axis=1, tiled=True)
    section_cols, signal_cols = (first_section(signal_cols, col_start), signal_cols)
    spectra = to_spectrum(section_cols)
    filter_real = filter_spectrum[0]
    filter_imag = filter_spectrum[1]
    spectrum_real = spectra[:, 0]
    spectrum_imag = spectra[:, 1]
    product = jnp.stack(
        [
            filter_real * spectrum_real - filter_imag * spectrum_imag,
            filter_real * spectrum_imag + filter_imag * spectrum_real,
        ],
        1,
    ).astype(jnp.bfloat16)
    mixed_rows = spectral_inverse(product, row_start)
    filtered = column_inverse(
        lax.all_to_all(mixed_rows, "ctx", split_axis=3, concat_axis=2, tiled=True)
    )
    cotangent_rows = cotangent[0].reshape(row_count, N2, channels)
    filtered_rows = lax.all_to_all(filtered, "ctx", split_axis=1, concat_axis=2, tiled=True)
    clean_y, errors = error_terms(inputs, filtered_rows, skip_gain, cotangent_rows)
    clean_output = clean_y.astype(jnp.bfloat16)
    error_section = first_section(
        lax.all_to_all(errors, "ctx", split_axis=2, concat_axis=1, tiled=True), col_start
    )
    error_spec = to_spectrum(error_section)
    error_real = error_spec[:, 0]
    error_imag = error_spec[:, 1]
    term_real = error_real * spectrum_real + error_imag * spectrum_imag
    term_imag = error_imag * spectrum_real - error_real * spectrum_imag
    local_grad = jnp.stack([term_real[0] + term_real[1], term_imag[0] + term_imag[1]], 0) * (
        1.0 / (N1 * N2)
    )
    grad_shard = lax.psum_scatter(
        local_grad.astype(jnp.bfloat16), "dp", scatter_dimension=2, tiled=True
    ).astype(jnp.float32)
    return (clean_output.reshape(1, row_count * N2, channels), grad_shard)


def solution(mesh):
    dp, ctx = mesh.shape["dp"], mesh.shape["ctx"]

    def run(embeds, *rest):
        apart = dp == 2 and embeds.shape[2] % (dp * ctx) == 0 and N1 // ctx % 16 == 0
        return jax.shard_map(
            by_channel_body if apart else body,
            mesh=mesh,
            in_specs=(
                P("dp", "ctx", None),
                P("dp", "ctx", None),
                P("dp", "ctx", None),
                P(None, "ctx", None, None),
                P(),
            ),
            out_specs=(P("dp", "ctx", None), P(None, "ctx", "dp", None)),
            check_vma=False,
        )(embeds, *rest)

    return run
```

```python
import jax
import jax.numpy as jnp
import numpy as np
from jax import lax
from jax.experimental import pallas as pl
from jax.experimental.pallas import tpu as pltpu
from jax.sharding import PartitionSpec as P

N1 = 256
N2 = 256
BF16 = jnp.bfloat16
F32 = jnp.float32
VMEM = 60 << 20

two_pi = 6.283185307179586
smart_weight = 2.0


def tables():
    ids = np.arange(N1)
    phase = (ids[:, None] * ids[None, :] % N1) * (two_pi / N1)
    cos_table, sin_table = np.cos(phase), np.sin(phase)
    split_rows = np.concatenate([cos_table, -sin_table], 0)
    forward = np.block([[cos_table, -sin_table], [sin_table, cos_table]])
    inverse = np.block([[cos_table, sin_table], [-sin_table, cos_table]])
    join_rows = np.concatenate([cos_table, -sin_table], 1) / (N1 * N2)
    angle = (ids[:, None] * ids[None, :]) * (two_pi / (N1 * N2))
    twiddle = np.stack([np.cos(angle), np.sin(angle)], 0)
    small = [jnp.asarray(t.astype(jnp.bfloat16)) for t in (split_rows, forward, inverse, join_rows)]
    return (*small, jnp.asarray(twiddle.astype(np.float32)))


def dot(a, b):
    return jnp.dot(a, b, preferred_element_type=F32)


def half_forward(rows, tw_cos, tw_sin):
    part_real, part_imag = rows[:N1], rows[N1:]
    out_real = part_real * tw_cos + part_imag * tw_sin
    out_imag = part_imag * tw_cos - part_real * tw_sin
    return jnp.concatenate([out_real.astype(BF16), out_imag.astype(BF16)], 1)


def conv_kernel(
    gain_ref, ep_ref, filt_ref, split_ref, fwd_ref, inv_ref, join_ref, tw_ref,
    send_ref, gap_ref, spec_ref, grad_ref,
):
    q, d = pl.program_id(0), pl.program_id(1)
    tw_cos, tw_sin = tw_ref[0], tw_ref[1]
    clean = ep_ref[0, :, 0, 0].reshape(N1, N2)
    clean_wide = clean.astype(F32)
    shifted = (clean_wide + ep_ref[0, :, 1, 0].reshape(N1, N2).astype(F32)).astype(BF16)
    shifted_wide = shifted.astype(F32)
    half = [half_forward(dot(split_ref[...], x), tw_cos, tw_sin) for x in (clean, shifted)]
    spec = [dot(h, fwd_ref[...]) for h in half]
    spec_ref[0, 0] = spec[0]
    filter_real = filt_ref[0, :, 0, 0].reshape(N1, N2).astype(F32)
    filter_imag = filt_ref[1, :, 0, 0].reshape(N1, N2).astype(F32)
    gain = gain_ref[q]
    ys = []
    for x_wide, x_spec in zip((clean_wide, shifted_wide), spec):
        real, imag = x_spec[:, :N2], x_spec[:, N2:]
        prod_real = (filter_real * real - filter_imag * imag).astype(BF16)
        prod_imag = (filter_real * imag + filter_imag * real).astype(BF16)
        back = dot(jnp.concatenate([prod_real, prod_imag], 1), inv_ref[...])
        back_real, back_imag = back[:, :N2], back[:, N2:]
        mixed_real = (back_real * tw_cos - back_imag * tw_sin).astype(BF16)
        mixed_imag = (back_imag * tw_cos + back_real * tw_sin).astype(BF16)
        conv = dot(join_ref[...], jnp.concatenate([mixed_real, mixed_imag], 0))
        conv = conv.astype(BF16).astype(F32)
        ys.append(x_wide * conv + gain * x_wide)
    send_ref[0, :, 0, 0] = ys[0].astype(BF16).reshape(send_ref.shape[1], -1, N2)
    gap = smart_weight * (ys[1] - ys[0])
    gap_ref[0, 0] = gap
    err = (shifted_wide * gap).astype(BF16)
    err_spec = dot(half_forward(dot(split_ref[...], err), tw_cos, tw_sin), fwd_ref[...])
    add_grad(grad_ref, d, err_spec, spec[1])


def add_grad(grad_ref, d, err_spec, spec):
    err_real, err_imag = err_spec[:, :N2], err_spec[:, N2:]
    real, imag = spec[:, :N2], spec[:, N2:]
    term_real = err_real * real + err_imag * imag
    term_imag = err_imag * real - err_real * imag

    @pl.when(d == 0)
    def _():
        grad_ref[0, 0] = term_real
        grad_ref[0, 1] = term_imag

    @pl.when(d != 0)
    def _():
        grad_ref[0, 0] += term_real
        grad_ref[0, 1] += term_imag


def grad_kernel(
    ep_ref, cot_ref, gap_ref, spec_ref, part_ref, split_ref, fwd_ref, tw_ref, _, send_ref
):
    tw_cos, tw_sin = tw_ref[0], tw_ref[1]
    count = send_ref.shape[0]
    halves = []
    for d in range(count):
        clean = ep_ref[d, :, 0, 0].reshape(N1, N2).astype(F32)
        cot = cot_ref[d, :, 0].reshape(N1, N2).astype(F32)
        err = (clean * (cot - gap_ref[0, d])).astype(BF16)
        halves.append(half_forward(dot(split_ref[...], err), tw_cos, tw_sin))
    total_real, total_imag = part_ref[0, 0], part_ref[0, 1]
    for d in range(count):
        err_spec = dot(halves[d], fwd_ref[...])
        err_real, err_imag = err_spec[:, :N2], err_spec[:, N2:]
        real, imag = spec_ref[0, d, :, :N2], spec_ref[0, d, :, N2:]
        total_real += err_real * real + err_imag * imag
        total_imag += err_imag * real - err_real * imag
    scale = 1.0 / (N1 * N2)
    total_real, total_imag = (total_real * scale).astype(BF16), (total_imag * scale).astype(BF16)
    width = N2 // count
    for i in range(count):
        cols = slice(i * width, (i + 1) * width)
        pair = jnp.concatenate([total_real[:, cols], total_imag[:, cols]], 1)
        send_ref[i, :, 0, 0] = pair.reshape(send_ref.shape[1], -1, 2 * width)


def whole(x):
    return pl.BlockSpec(x.shape, lambda *_: (0,) * x.ndim)


def conv_call(gain, received, tabs):
    dp, ctx, _, per, rows, _ = received.shape
    split_rows, forward, inverse, join_rows, twiddle = tabs
    return pl.pallas_call(
        conv_kernel,
        grid=(per, dp),
        in_specs=[
            pl.BlockSpec(memory_space=pltpu.SMEM),
            pl.BlockSpec((1, ctx, 2, 1, rows, N2), lambda q, d: (d, 0, 0, q, 0, 0)),
            pl.BlockSpec((dp, ctx, 1, 1, rows, N2), lambda q, d: (0, 0, 2, q, 0, 0)),
            *[whole(t) for t in tabs],
        ],
        out_specs=[
            pl.BlockSpec((1, ctx, 1, 1, rows, N2), lambda q, d: (d, 0, 0, q, 0, 0)),
            pl.BlockSpec((1, 1, N1, N2), lambda q, d: (q, d, 0, 0)),
            pl.BlockSpec((1, 1, N1, 2 * N2), lambda q, d: (q, d, 0, 0)),
            pl.BlockSpec((1, 2, N1, N2), lambda q, d: (q, 0, 0, 0)),
        ],
        out_shape=[
            jax.ShapeDtypeStruct((dp, ctx, 2, per, rows, N2), BF16),
            jax.ShapeDtypeStruct((per, dp, N1, N2), F32),
            jax.ShapeDtypeStruct((per, dp, N1, 2 * N2), F32),
            jax.ShapeDtypeStruct((per, 2, N1, N2), F32),
        ],
        compiler_params=pltpu.CompilerParams(vmem_limit_bytes=VMEM),
        cost_estimate=pl.CostEstimate(flops=8 * per * dp * N1 * N1 * N1 * 12, bytes_accessed=20 << 20, transcendentals=0),
        name="conv",
    )(gain, received, received, split_rows, forward, inverse, join_rows, twiddle)


def grad_call(received, cot, gap, spec, part, tabs, send):
    dp, ctx, _, per, rows, _ = received.shape
    split_rows, forward, _, _, twiddle = tabs
    return pl.pallas_call(
        grad_kernel,
        grid=(per,),
        in_specs=[
            pl.BlockSpec((dp, ctx, 1, 1, rows, N2), lambda q: (0, 0, 0, q, 0, 0)),
            pl.BlockSpec((dp, ctx, 1, rows, N2), lambda q: (0, 0, q, 0, 0)),
            pl.BlockSpec((1, dp, N1, N2), lambda q: (q, 0, 0, 0)),
            pl.BlockSpec((1, dp, N1, 2 * N2), lambda q: (q, 0, 0, 0)),
            pl.BlockSpec((1, 2, N1, N2), lambda q: (q, 0, 0, 0)),
            whole(split_rows),
            whole(forward),
            whole(twiddle),
            pl.BlockSpec(memory_space=pl.ANY),
        ],
        out_specs=pl.BlockSpec((dp, ctx, 1, 1, rows, N2), lambda q: (0, 0, 1, q, 0, 0)),
        out_shape=jax.ShapeDtypeStruct(send.shape, BF16),
        input_output_aliases={8: 0},
        compiler_params=pltpu.CompilerParams(vmem_limit_bytes=VMEM),
        cost_estimate=pl.CostEstimate(flops=2 * per * dp * N1 * N1 * N1 * 6, bytes_accessed=12 << 20, transcendentals=0),
        name="grad",
    )(received, cot, gap, spec, part, split_rows, forward, twiddle, send)


def outward_kernel(index_ref, *refs):
    *in_refs, out_ref, rows_ref = refs
    count, _, per, rows, width = out_ref.shape
    channels = count * per
    for t, in_ref in enumerate(in_refs):
        for r in range(rows):
            block = in_ref[0, r].astype(F32).T
            rows_ref[pl.ds(r, channels, stride=rows), :] = block
        out_ref[:, t] = rows_ref[...].astype(BF16).reshape(count, per, rows, width)


def outward(index, arrays, count):
    _, rows, _, channels = arrays[0].shape
    per = channels // count
    width = 128
    picks = [(lambda h, s: (s[0], 0, h, 0)) if a.shape[0] > 1 else (lambda h, s: (0, 0, h, 0)) for a in arrays]
    return pl.pallas_call(
        outward_kernel,
        grid_spec=pltpu.PrefetchScalarGridSpec(
            num_scalar_prefetch=1,
            grid=(N2 // width,),
            in_specs=[pl.BlockSpec((1, rows, width, channels), pick) for pick in picks],
            out_specs=pl.BlockSpec((count, len(arrays), per, rows, width), lambda h, s: (0, 0, 0, 0, h)),
            scratch_shapes=[pltpu.VMEM((channels * rows, width), F32)],
        ),
        out_shape=jax.ShapeDtypeStruct((count, len(arrays), per, rows, N2), BF16),
        compiler_params=pltpu.CompilerParams(vmem_limit_bytes=VMEM),
        cost_estimate=pl.CostEstimate(flops=0, bytes_accessed=(4 * len(arrays)) << 20, transcendentals=0),
        name="outward",
    )(index, *arrays)


def homeward_kernel(last_ref, y_ref, grad_ref, rows_ref):
    count, _, per, rows, width = last_ref.shape
    channels = count * per
    for t in range(2):
        rows_ref[...] = last_ref[:, t].astype(F32).reshape(channels * rows, width)
        for r in range(rows):
            block = rows_ref[pl.ds(r, channels, stride=rows), :].T
            if t == 0:
                y_ref[r] = block.astype(BF16)
            else:
                grad_ref[0, r] = block


def homeward(last):
    count, _, per, rows, _ = last.shape
    channels = count * per
    width = 128
    return pl.pallas_call(
        homeward_kernel,
        grid=(N2 // width,),
        in_specs=[pl.BlockSpec((count, 2, per, rows, width), lambda h: (0, 0, 0, 0, h))],
        out_specs=[
            pl.BlockSpec((rows, width, channels), lambda h: (0, h, 0)),
            pl.BlockSpec((1, rows, width, channels), lambda h: (h, 0, 0, 0)),
        ],
        out_shape=[
            jax.ShapeDtypeStruct((rows, N2, channels), BF16),
            jax.ShapeDtypeStruct((2, rows, width, channels), F32),
        ],
        scratch_shapes=[pltpu.VMEM((channels * rows, width), F32)],
        compiler_params=pltpu.CompilerParams(vmem_limit_bytes=VMEM),
        cost_estimate=pl.CostEstimate(flops=0, bytes_accessed=5 << 20, transcendentals=0),
        name="homeward",
    )(last)


def by_channel_body(embeds, perturb, cotangent, filter_spectrum, skip_gain):
    dp, ctx = lax.axis_size("dp"), lax.axis_size("ctx")
    d, c = lax.axis_index("dp"), lax.axis_index("ctx")
    axes = ("dp", "ctx")
    channels = embeds.shape[2]
    rows = N1 // ctx
    per = channels // (dp * ctx)
    tabs = tables()
    index = d.reshape(1)

    def matrix(x):
        return x.reshape(1, rows, N2, channels)

    first = outward(index, [matrix(embeds), matrix(perturb), filter_spectrum], dp * ctx)
    received = lax.all_to_all(first, axes, 0, 0, tiled=True).reshape(dp, ctx, 3, per, rows, N2)
    second = outward(index, [matrix(cotangent)], dp * ctx)
    cot = lax.all_to_all(second, axes, 0, 0, tiled=True).reshape(dp, ctx, per, rows, N2)
    gain = lax.dynamic_slice(skip_gain, ((d * ctx + c) * per,), (per,))
    send, gap, spec, part = conv_call(gain, received, tabs)
    send = grad_call(received, cot, gap, spec, part, tabs, send)
    last = lax.all_to_all(send.reshape(dp * ctx, 2, per, rows, N2), axes, 0, 0, tiled=True)
    y, grad = homeward(last)
    return y.reshape(1, rows * N2, channels), grad


def trig_table(period):
    row_ids = jnp.arange(period, dtype=jnp.int32)
    exponent = row_ids[:, None] * row_ids[None, :] % period
    phase_angle = exponent.astype(jnp.float32) * (two_pi / period)
    return (jnp.cos(phase_angle).astype(jnp.bfloat16), jnp.sin(phase_angle).astype(jnp.bfloat16))


def twiddle(row_first, row_count, col_first, col_count):
    row_ids = row_first + jnp.arange(row_count, dtype=jnp.int32)
    col_ids = col_first + jnp.arange(col_count, dtype=jnp.int32)
    exponent = row_ids[:, None] * col_ids[None, :] % (N1 * N2)
    phase_angle = exponent.astype(jnp.float32) * (two_pi / (N1 * N2))
    return (jnp.cos(phase_angle)[:, :, None], jnp.sin(phase_angle)[:, :, None])


def first_section(values, col_start):
    cos_table, sin_table = trig_table(N1)
    part_real = jnp.einsum("kn,snmc->skmc", cos_table, values, preferred_element_type=jnp.float32)
    part_imag = -jnp.einsum("kn,snmc->skmc", sin_table, values, preferred_element_type=jnp.float32)
    tw_cos, tw_sin = twiddle(0, N1, col_start, values.shape[2])
    out_real = part_real * tw_cos + part_imag * tw_sin
    out_imag = part_imag * tw_cos - part_real * tw_sin
    return jnp.stack([out_real, out_imag], 1).astype(jnp.bfloat16)


def second_section(section_rows):
    cos_table, sin_table = trig_table(N2)
    with_cos = jnp.einsum(
        "sprnc,kn->sprkc", section_rows, cos_table, preferred_element_type=jnp.float32
    )
    with_sin = jnp.einsum(
        "sprnc,kn->sprkc", section_rows, sin_table, preferred_element_type=jnp.float32
    )
    return jnp.stack([with_cos[:, 0] + with_sin[:, 1], with_cos[:, 1] - with_sin[:, 0]], 1)


def spectral_inverse(product, row_start):
    cos_table, sin_table = trig_table(N2)
    with_cos = jnp.einsum("sprkc,nk->sprnc", product, cos_table, preferred_element_type=jnp.float32)
    with_sin = jnp.einsum("sprkc,nk->sprnc", product, sin_table, preferred_element_type=jnp.float32)
    part_real = with_cos[:, 0] - with_sin[:, 1]
    part_imag = with_cos[:, 1] + with_sin[:, 0]
    tw_cos, tw_sin = twiddle(row_start, product.shape[2], 0, N2)
    out_real = part_real * tw_cos - part_imag * tw_sin
    out_imag = part_imag * tw_cos + part_real * tw_sin
    return jnp.stack([out_real, out_imag], 1).astype(jnp.bfloat16)


def column_inverse(mixed_cols):
    cos_table, sin_table = trig_table(N1)
    with_cos = jnp.einsum(
        "nk,skmc->snmc", cos_table, mixed_cols[:, 0], preferred_element_type=jnp.float32
    )
    with_sin = jnp.einsum(
        "nk,skmc->snmc", sin_table, mixed_cols[:, 1], preferred_element_type=jnp.float32
    )
    return ((with_cos - with_sin) * (1.0 / (N1 * N2))).astype(jnp.bfloat16)


def to_spectrum(section_cols):
    return second_section(
        lax.all_to_all(section_cols, "ctx", split_axis=2, concat_axis=3, tiled=True)
    )


def error_terms(signal, filtered, skip_gain, cotangent_view):
    signal_wide = signal.astype(jnp.float32)
    filtered_wide = lax.optimization_barrier(filtered).astype(jnp.float32)
    outputs = signal_wide * filtered_wide + skip_gain * signal_wide
    clean_y = outputs[0]
    smooth_gap = outputs[1] - clean_y
    err_clean = signal_wide[0] * (cotangent_view.astype(jnp.float32) - smart_weight * smooth_gap)
    err_shift = signal_wide[1] * (smart_weight * smooth_gap)
    return (clean_y, jnp.stack([err_clean, err_shift], 0).astype(jnp.bfloat16))


def body(embeds, perturb, cotangent, filter_spectrum, skip_gain):
    ctx_size = lax.axis_size("ctx")
    ctx_index = lax.axis_index("ctx")
    channels = embeds.shape[2]
    row_count = N1 // ctx_size
    col_count = N2 // ctx_size
    row_start = ctx_index * row_count
    col_start = ctx_index * col_count
    clean_rows = embeds[0].reshape(row_count, N2, channels)
    perturb_rows = perturb[0].reshape(row_count, N2, channels)
    shifted = (clean_rows.astype(jnp.float32) + perturb_rows.astype(jnp.float32)).astype(
        jnp.bfloat16
    )
    inputs = jnp.stack([clean_rows, shifted], 0)
    signal_cols = lax.all_to_all(inputs, "ctx", split_axis=2, concat_axis=1, tiled=True)
    section_cols, signal_cols = (first_section(signal_cols, col_start), signal_cols)
    spectra = to_spectrum(section_cols)
    filter_real = filter_spectrum[0]
    filter_imag = filter_spectrum[1]
    spectrum_real = spectra[:, 0]
    spectrum_imag = spectra[:, 1]
    product = jnp.stack(
        [
            filter_real * spectrum_real - filter_imag * spectrum_imag,
            filter_real * spectrum_imag + filter_imag * spectrum_real,
        ],
        1,
    ).astype(jnp.bfloat16)
    mixed_rows = spectral_inverse(product, row_start)
    filtered = column_inverse(
        lax.all_to_all(mixed_rows, "ctx", split_axis=3, concat_axis=2, tiled=True)
    )
    cotangent_rows = cotangent[0].reshape(row_count, N2, channels)
    filtered_rows = lax.all_to_all(filtered, "ctx", split_axis=1, concat_axis=2, tiled=True)
    clean_y, errors = error_terms(inputs, filtered_rows, skip_gain, cotangent_rows)
    clean_output = clean_y.astype(jnp.bfloat16)
    error_section = first_section(
        lax.all_to_all(errors, "ctx", split_axis=2, concat_axis=1, tiled=True), col_start
    )
    error_spec = to_spectrum(error_section)
    error_real = error_spec[:, 0]
    error_imag = error_spec[:, 1]
    term_real = error_real * spectrum_real + error_imag * spectrum_imag
    term_imag = error_imag * spectrum_real - error_real * spectrum_imag
    local_grad = jnp.stack([term_real[0] + term_real[1], term_imag[0] + term_imag[1]], 0) * (
        1.0 / (N1 * N2)
    )
    grad_shard = lax.psum_scatter(
        local_grad.astype(jnp.bfloat16), "dp", scatter_dimension=2, tiled=True
    ).astype(jnp.float32)
    return (clean_output.reshape(1, row_count * N2, channels), grad_shard)


def solution(mesh):
    dp, ctx = mesh.shape["dp"], mesh.shape["ctx"]

    def run(embeds, *rest):
        apart = dp == 2 and embeds.shape[2] % (dp * ctx) == 0 and N1 // ctx == 16
        return jax.shard_map(
            by_channel_body if apart else body,
            mesh=mesh,
            in_specs=(
                P("dp", "ctx", None),
                P("dp", "ctx", None),
                P("dp", "ctx", None),
                P(None, "ctx", None, None),
                P(),
            ),
            out_specs=(P("dp", "ctx", None), P(None, "ctx", "dp", None)),
            check_vma=False,
        )(embeds, *rest)

    return run
```

```python
import functools

import jax
import jax.numpy as jnp
import numpy as np
from jax import lax
from jax.experimental import pallas as pl
from jax.experimental.pallas import tpu as pltpu
from jax.sharding import PartitionSpec as P

N1 = 256
N2 = 256
BF16 = jnp.bfloat16
F32 = jnp.float32
HALF = 144
VMEM = 26 << 20

two_pi = 6.283185307179586
smart_weight = 2.0


def tables():
    ids = np.arange(N1)
    phase = (ids[:, None] * ids[None, :] % N1) * (two_pi / N1)
    cos_table, sin_table = np.cos(phase), np.sin(phase)
    split_rows = np.concatenate([cos_table[:HALF], -sin_table[:HALF]], 0)
    forward_table = np.block([[cos_table, -sin_table], [sin_table, cos_table]])
    weight = np.where(ids[: N1 // 2] == 0, 1.0, 2.0) / (N1 * N2)
    join_rows = np.concatenate([cos_table[:, : N1 // 2] * weight, -sin_table[:, : N1 // 2] * weight], 1)
    mirror_rows = np.zeros((HALF, N1))
    mirror_rows[ids[:HALF], -ids[:HALF] % N1] = 1
    mirror_cols = np.eye(N2)[::-1]
    lower_rows = np.zeros((N1 // 2, HALF))
    lower_rows[ids[: N1 // 2], N1 // 2 - ids[: N1 // 2]] = 1
    angle = (ids[:HALF, None] * ids[None, :]) * (two_pi / (N1 * N2))
    twiddle = np.stack([np.cos(angle), np.sin(angle)], 0)
    small = (split_rows, forward_table, join_rows, mirror_rows, mirror_cols, lower_rows)
    small = [jnp.asarray(t.astype(jnp.bfloat16)) for t in small]
    return (*small, jnp.asarray(twiddle.astype(np.float32)))


def dot(a, b):
    return jnp.dot(a, b, preferred_element_type=F32)


def near_device(place_ref, j, hop, plane, hops):
    far = (place_ref[0] ^ (j // plane)) * hops + (place_ref[1] ^ hop)
    return far * plane + (place_ref[2] ^ (j % plane))


def forward(signals, split_ref, fwd_ref, tw_cos, tw_sin):
    halves = []
    for x in signals:
        part = dot(split_ref[...], x)
        part_real, part_imag = part[:HALF], part[HALF:]
        out_real = part_real * tw_cos + part_imag * tw_sin
        out_imag = part_imag * tw_cos - part_real * tw_sin
        halves.append(jnp.concatenate([out_real.astype(BF16), out_imag.astype(BF16)], 1))
    spectra = dot(jnp.concatenate(halves, 0), fwd_ref[...])
    return [spectra[i * HALF : (i + 1) * HALF] for i in range(len(signals))]


def hermitian_part(filter_real, filter_imag, mirror_rows, mirror_cols):
    rows = dot(mirror_rows, jnp.concatenate([filter_real, filter_imag], 1)).astype(BF16)
    flipped = dot(jnp.concatenate([rows[:, :N2], rows[:, N2:]], 0), mirror_cols)
    out = []
    for part, other, sign in ((filter_real, flipped[:HALF], 0.5), (filter_imag, flipped[HALF:], -0.5)):
        top = other[:8]
        row = lax.broadcasted_iota(jnp.int32, top.shape, 0)
        top = jnp.where(row == 0, pltpu.roll(top, 1, 1), top)
        other = jnp.concatenate([top, other[8:]], 0)
        out.append(0.5 * part[:HALF].astype(F32) + sign * other)
    return out


def channel_kernel(place_ref, gain_ref, recv_ref, *refs, hops):
    cot_refs, refs = refs[:hops], refs[hops:]
    split_ref, fwd_ref, join_ref, mirror_ref, cols_ref, lower_ref, tw_ref, send_ref, cot_rows = refs
    count, ctx = recv_ref.shape[:2]
    plane = ctx // hops
    q = pl.program_id(0)
    for hop, cot_ref in enumerate(cot_refs):
        for j in range(count * plane):
            cot_rows[near_device(place_ref, j, hop, plane, hops)] = cot_ref[j, q]
    tw_cos, tw_sin = tw_ref[0], tw_ref[1]
    signals = []
    for d in range(count):
        clean = recv_ref[d, :, 0, q].reshape(N1, N2)
        perturb = recv_ref[d, :, 1, q].reshape(N1, N2)
        signals += [clean, (clean.astype(F32) + perturb.astype(F32)).astype(BF16)]
    spectra = forward(signals, split_ref, fwd_ref, tw_cos, tw_sin)
    filter_real, filter_imag = hermitian_part(
        recv_ref[0, :, 2, q].reshape(N1, N2), recv_ref[1, :, 2, q].reshape(N1, N2), mirror_ref[...], cols_ref[...]
    )
    products = []
    for spec in spectra:
        real, imag = spec[:, :N2], spec[:, N2:]
        prod_real = (filter_real * real - filter_imag * imag).astype(BF16)
        minus_imag = (-filter_real * imag - filter_imag * real).astype(BF16)
        products.append(jnp.concatenate([prod_real, minus_imag], 1))
    back = dot(jnp.concatenate(products, 0), fwd_ref[...])
    mixed, middle = [], []
    for i in range(2 * count):
        back_real, minus_imag = back[i * HALF : (i + 1) * HALF, :N2], back[i * HALF : (i + 1) * HALF, N2:]
        mixed_real = (back_real * tw_cos + minus_imag * tw_sin).astype(BF16)
        mixed_imag = (back_real * tw_sin - minus_imag * tw_cos).astype(BF16)
        mixed.append(jnp.concatenate([mixed_real[: N1 // 2], mixed_imag[: N1 // 2]], 0))
        middle.append(mixed_real[N1 // 2 :].astype(F32)[:1])
    conv = dot(join_ref[...], jnp.concatenate(mixed, 1))
    parity = lax.broadcasted_iota(jnp.int32, (N1, N2), 0) % 2
    alternate = (1 - 2 * parity).astype(F32) * (1.0 / (N1 * N2))
    gain = gain_ref[q]
    errors = []
    for d in range(count):
        pair = []
        for i in range(2):
            k = 2 * d + i
            wide = signals[k].astype(F32)
            filtered = conv[:, k * N2 : (k + 1) * N2] + alternate * middle[k]
            pair.append((wide, wide * filtered.astype(BF16).astype(F32) + gain * wide))
        (clean, clean_y), (shifted, shifted_y) = pair
        send_ref[d, :, 0, q] = clean_y.astype(BF16).reshape(ctx, -1, N2)
        gap = smart_weight * (shifted_y - clean_y)
        cot = cot_rows[d * ctx : (d + 1) * ctx].reshape(N1, N2).astype(F32)
        errors += [(clean * (cot - gap)).astype(BF16), (shifted * gap).astype(BF16)]
    total_real = total_imag = 0.0
    for err_spec, spec in zip(forward(errors, split_ref, fwd_ref, tw_cos, tw_sin), spectra):
        err_real, err_imag = err_spec[:, :N2], err_spec[:, N2:]
        real, imag = spec[:, :N2], spec[:, N2:]
        total_real += err_real * real + err_imag * imag
        total_imag += err_imag * real - err_real * imag
    scale = 1.0 / (N1 * N2)
    upper = jnp.concatenate([(total_real * scale).astype(BF16), (total_imag * scale).astype(BF16)], 1)
    lower = dot(lower_ref[...], upper).astype(BF16)
    lower = dot(jnp.concatenate([lower[:, :N2], lower[:, N2:]], 0), cols_ref[...])
    lower_real, lower_imag = lower[: N1 // 2].astype(BF16), (-lower[N1 // 2 :]).astype(BF16)
    width = N2 // count
    for i in range(count):
        first = upper[: N1 // 2, i * width : (i + 1) * width]
        second = upper[: N1 // 2, N2 + i * width : N2 + (i + 1) * width]
        upper_pair = jnp.concatenate([first, second], 1)
        cols = slice(i * width, (i + 1) * width)
        lower_pair = jnp.concatenate([lower_real[:, cols], lower_imag[:, cols]], 1)
        send_ref[i, : ctx // 2, 1, q] = upper_pair.reshape(ctx // 2, -1, 2 * width)
        send_ref[i, ctx // 2 :, 1, q] = lower_pair.reshape(ctx // 2, -1, 2 * width)


def whole(x):
    return pl.BlockSpec(x.shape, lambda *_: (0,) * x.ndim)


def near(x):
    return pltpu.with_memory_space_constraint(x, pltpu.VMEM)


def far(x):
    return pltpu.with_memory_space_constraint(x, pltpu.HBM)


def channel_call(place, gain, received, cots, tabs):
    dp, ctx, _, per, rows, _ = received.shape
    here = pl.BlockSpec(memory_space=pltpu.VMEM)
    return pl.pallas_call(
        functools.partial(channel_kernel, hops=len(cots)),
        grid=(per,),
        in_specs=[
            pl.BlockSpec(memory_space=pltpu.SMEM),
            pl.BlockSpec(memory_space=pltpu.SMEM),
            here,
            *[whole(x) for x in cots],
            *[whole(t) for t in tabs],
        ],
        out_specs=here,
        out_shape=pltpu.VMEM((dp, ctx, 2, per, rows, N2), BF16),
        scratch_shapes=[pltpu.VMEM((dp * ctx, rows, N2), BF16)],
        compiler_params=pltpu.CompilerParams(vmem_limit_bytes=VMEM),
        cost_estimate=pl.CostEstimate(flops=per * dp * 6 * 12 * N1**3, bytes_accessed=8 << 20, transcendentals=0),
        name="channels",
    )(place, gain, near(received), *[far(x) for x in cots], *[far(t) for t in tabs])


def outward_kernel(index_ref, *refs):
    *in_refs, out_ref, rows_ref = refs
    count, _, per, rows, width = out_ref.shape
    channels = count * per
    for t, in_ref in enumerate(in_refs):
        for r in range(rows):
            block = in_ref[0, r].astype(F32).T
            rows_ref[pl.ds(r, channels, stride=rows), :] = block
        out_ref[:, t] = rows_ref[...].astype(BF16).reshape(count, per, rows, width)


def outward(index, arrays, count):
    _, rows, _, channels = arrays[0].shape
    per = channels // count
    width = 128
    picks = [(lambda h, s: (s[0], 0, h, 0)) if a.shape[0] > 1 else (lambda h, s: (0, 0, h, 0)) for a in arrays]
    return pl.pallas_call(
        outward_kernel,
        grid_spec=pltpu.PrefetchScalarGridSpec(
            num_scalar_prefetch=1,
            grid=(N2 // width,),
            in_specs=[pl.BlockSpec((1, rows, width, channels), pick) for pick in picks],
            out_specs=pl.BlockSpec((count, len(arrays), per, rows, width), lambda h, s: (0, 0, 0, 0, h)),
            scratch_shapes=[pltpu.VMEM((channels * rows, width), F32)],
        ),
        out_shape=jax.ShapeDtypeStruct((count, len(arrays), per, rows, N2), BF16),
        compiler_params=pltpu.CompilerParams(vmem_limit_bytes=VMEM),
        cost_estimate=pl.CostEstimate(flops=0, bytes_accessed=(4 * len(arrays)) << 20, transcendentals=0),
        name="outward",
    )(index, *arrays)


def outward_near_kernel(place_ref, in_ref, *refs, hops, plane):
    *out_refs, rows_ref = refs
    _, per, rows, width = out_refs[0].shape
    channels = in_ref.shape[3]
    for r in range(rows):
        rows_ref[pl.ds(r, channels, stride=rows), :] = in_ref[0, r].astype(F32).T
    for j, out_ref in enumerate(out_refs):
        for hop in range(hops):
            block = near_device(place_ref, j, hop, plane, hops) * (per * rows)
            rows_here = rows_ref[pl.ds(pl.multiple_of(block, per * rows), per * rows), :]
            out_ref[hop] = rows_here.astype(BF16).reshape(per, rows, width)


def outward_near(place, x, count, hops, plane):
    _, rows, _, channels = x.shape
    per = channels // count
    width = 128
    return pl.pallas_call(
        functools.partial(outward_near_kernel, hops=hops, plane=plane),
        grid=(N2 // width,),
        in_specs=[
            pl.BlockSpec(memory_space=pltpu.SMEM),
            pl.BlockSpec((1, rows, width, channels), lambda h: (0, 0, h, 0)),
        ],
        out_specs=[pl.BlockSpec((hops, per, rows, width), lambda h: (0, 0, 0, h))] * (count // hops),
        out_shape=[jax.ShapeDtypeStruct((hops, per, rows, N2), BF16)] * (count // hops),
        scratch_shapes=[pltpu.VMEM((channels * rows, width), F32)],
        compiler_params=pltpu.CompilerParams(vmem_limit_bytes=VMEM),
        cost_estimate=pl.CostEstimate(flops=0, bytes_accessed=2 << 20, transcendentals=0),
        name="outward_near",
    )(place, x)


def regroup_kernel(*refs, count):
    for i, in_ref in enumerate(refs[:count]):
        for j, out_ref in enumerate(refs[count:]):
            out_ref[i] = in_ref[j]


def regroup(arrays):
    hops, *block = arrays[0].shape
    return pl.pallas_call(
        functools.partial(regroup_kernel, count=len(arrays)),
        out_shape=[jax.ShapeDtypeStruct((len(arrays), *block), BF16)] * hops,
        compiler_params=pltpu.CompilerParams(vmem_limit_bytes=VMEM),
        cost_estimate=pl.CostEstimate(flops=0, bytes_accessed=2 << 20, transcendentals=0),
        name="regroup",
    )(*arrays)


def homeward_kernel(last_ref, y_ref, grad_ref, rows_ref):
    count, _, per, rows, _ = last_ref.shape
    channels = count * per
    width = rows_ref.shape[1]
    lanes = pl.ds(pl.multiple_of(pl.program_id(0) * width, width), width)
    for t in range(2):
        rows_ref[...] = last_ref[:, t, :, :, lanes].astype(F32).reshape(channels * rows, width)
        for r in range(rows):
            block = rows_ref[pl.ds(r, channels, stride=rows), :].T
            if t == 0:
                y_ref[r] = block.astype(BF16)
            else:
                grad_ref[0, r] = block


def homeward(last):
    count, _, per, rows, _ = last.shape
    channels = count * per
    width = 128
    return pl.pallas_call(
        homeward_kernel,
        grid=(N2 // width,),
        in_specs=[pl.BlockSpec(memory_space=pltpu.VMEM)],
        out_specs=[
            pl.BlockSpec((rows, width, channels), lambda h: (0, h, 0)),
            pl.BlockSpec((1, rows, width, channels), lambda h: (h, 0, 0, 0)),
        ],
        out_shape=[
            jax.ShapeDtypeStruct((rows, N2, channels), BF16),
            jax.ShapeDtypeStruct((2, rows, width, channels), F32),
        ],
        scratch_shapes=[pltpu.VMEM((channels * rows, width), F32)],
        compiler_params=pltpu.CompilerParams(vmem_limit_bytes=VMEM),
        cost_estimate=pl.CostEstimate(flops=0, bytes_accessed=5 << 20, transcendentals=0),
        name="homeward",
    )(near(last))


def by_channel_body(embeds, perturb, cotangent, filter_spectrum, skip_gain):
    dp, ctx = lax.axis_size("dp"), lax.axis_size("ctx")
    d, c = lax.axis_index("dp"), lax.axis_index("ctx")
    axes = ("dp", "ctx")
    count = dp * ctx
    channels = embeds.shape[2]
    rows = N1 // ctx
    per = channels // count
    plane = 4
    hops = ctx // plane
    tabs = tables()
    place = jnp.stack([d, c // plane, c % plane])

    def matrix(x):
        return far(x.reshape(1, rows, N2, channels))

    def exchange(x, mask):
        return lax.ppermute(x, axes, [(i, i ^ mask) for i in range(count)]) if mask else x

    first = outward(place, [matrix(embeds), matrix(perturb), far(filter_spectrum)], count)
    received = lax.all_to_all(first, axes, 0, 0, tiled=True).reshape(dp, ctx, 3, per, rows, N2)
    cots = outward_near(place, matrix(cotangent), count, hops, plane)
    cots = regroup([exchange(x, j // plane * ctx + j % plane) for j, x in enumerate(cots)])
    cots = [exchange(x, hop * plane) for hop, x in enumerate(cots)]
    gain = lax.dynamic_slice(skip_gain, ((d * ctx + c) * per,), (per,))
    send = channel_call(place, gain, received, cots, tabs)
    last = lax.all_to_all(send.reshape(count, 2, per, rows, N2), axes, 0, 0, tiled=True)
    y, grad = homeward(last)
    return y.reshape(1, rows * N2, channels), grad


def trig_table(period):
    row_ids = jnp.arange(period, dtype=jnp.int32)
    exponent = row_ids[:, None] * row_ids[None, :] % period
    phase_angle = exponent.astype(jnp.float32) * (two_pi / period)
    return (jnp.cos(phase_angle).astype(jnp.bfloat16), jnp.sin(phase_angle).astype(jnp.bfloat16))


def twiddle(row_first, row_count, col_first, col_count):
    row_ids = row_first + jnp.arange(row_count, dtype=jnp.int32)
    col_ids = col_first + jnp.arange(col_count, dtype=jnp.int32)
    exponent = row_ids[:, None] * col_ids[None, :] % (N1 * N2)
    phase_angle = exponent.astype(jnp.float32) * (two_pi / (N1 * N2))
    return (jnp.cos(phase_angle)[:, :, None], jnp.sin(phase_angle)[:, :, None])


def first_section(values, col_start):
    cos_table, sin_table = trig_table(N1)
    part_real = jnp.einsum("kn,snmc->skmc", cos_table, values, preferred_element_type=jnp.float32)
    part_imag = -jnp.einsum("kn,snmc->skmc", sin_table, values, preferred_element_type=jnp.float32)
    tw_cos, tw_sin = twiddle(0, N1, col_start, values.shape[2])
    out_real = part_real * tw_cos + part_imag * tw_sin
    out_imag = part_imag * tw_cos - part_real * tw_sin
    return jnp.stack([out_real, out_imag], 1).astype(jnp.bfloat16)


def second_section(section_rows):
    cos_table, sin_table = trig_table(N2)
    with_cos = jnp.einsum(
        "sprnc,kn->sprkc", section_rows, cos_table, preferred_element_type=jnp.float32
    )
    with_sin = jnp.einsum(
        "sprnc,kn->sprkc", section_rows, sin_table, preferred_element_type=jnp.float32
    )
    return jnp.stack([with_cos[:, 0] + with_sin[:, 1], with_cos[:, 1] - with_sin[:, 0]], 1)


def spectral_inverse(product, row_start):
    cos_table, sin_table = trig_table(N2)
    with_cos = jnp.einsum("sprkc,nk->sprnc", product, cos_table, preferred_element_type=jnp.float32)
    with_sin = jnp.einsum("sprkc,nk->sprnc", product, sin_table, preferred_element_type=jnp.float32)
    part_real = with_cos[:, 0] - with_sin[:, 1]
    part_imag = with_cos[:, 1] + with_sin[:, 0]
    tw_cos, tw_sin = twiddle(row_start, product.shape[2], 0, N2)
    out_real = part_real * tw_cos - part_imag * tw_sin
    out_imag = part_imag * tw_cos + part_real * tw_sin
    return jnp.stack([out_real, out_imag], 1).astype(jnp.bfloat16)


def column_inverse(mixed_cols):
    cos_table, sin_table = trig_table(N1)
    with_cos = jnp.einsum(
        "nk,skmc->snmc", cos_table, mixed_cols[:, 0], preferred_element_type=jnp.float32
    )
    with_sin = jnp.einsum(
        "nk,skmc->snmc", sin_table, mixed_cols[:, 1], preferred_element_type=jnp.float32
    )
    return ((with_cos - with_sin) * (1.0 / (N1 * N2))).astype(jnp.bfloat16)


def to_spectrum(section_cols):
    return second_section(
        lax.all_to_all(section_cols, "ctx", split_axis=2, concat_axis=3, tiled=True)
    )


def error_terms(signal, filtered, skip_gain, cotangent_view):
    signal_wide = signal.astype(jnp.float32)
    filtered_wide = lax.optimization_barrier(filtered).astype(jnp.float32)
    outputs = signal_wide * filtered_wide + skip_gain * signal_wide
    clean_y = outputs[0]
    smooth_gap = outputs[1] - clean_y
    err_clean = signal_wide[0] * (cotangent_view.astype(jnp.float32) - smart_weight * smooth_gap)
    err_shift = signal_wide[1] * (smart_weight * smooth_gap)
    return (clean_y, jnp.stack([err_clean, err_shift], 0).astype(jnp.bfloat16))


def body(embeds, perturb, cotangent, filter_spectrum, skip_gain):
    ctx_size = lax.axis_size("ctx")
    ctx_index = lax.axis_index("ctx")
    channels = embeds.shape[2]
    row_count = N1 // ctx_size
    col_count = N2 // ctx_size
    row_start = ctx_index * row_count
    col_start = ctx_index * col_count
    clean_rows = embeds[0].reshape(row_count, N2, channels)
    perturb_rows = perturb[0].reshape(row_count, N2, channels)
    shifted = (clean_rows.astype(jnp.float32) + perturb_rows.astype(jnp.float32)).astype(
        jnp.bfloat16
    )
    inputs = jnp.stack([clean_rows, shifted], 0)
    signal_cols = lax.all_to_all(inputs, "ctx", split_axis=2, concat_axis=1, tiled=True)
    section_cols, signal_cols = (first_section(signal_cols, col_start), signal_cols)
    spectra = to_spectrum(section_cols)
    filter_real = filter_spectrum[0]
    filter_imag = filter_spectrum[1]
    spectrum_real = spectra[:, 0]
    spectrum_imag = spectra[:, 1]
    product = jnp.stack(
        [
            filter_real * spectrum_real - filter_imag * spectrum_imag,
            filter_real * spectrum_imag + filter_imag * spectrum_real,
        ],
        1,
    ).astype(jnp.bfloat16)
    mixed_rows = spectral_inverse(product, row_start)
    filtered = column_inverse(
        lax.all_to_all(mixed_rows, "ctx", split_axis=3, concat_axis=2, tiled=True)
    )
    cotangent_rows = cotangent[0].reshape(row_count, N2, channels)
    filtered_rows = lax.all_to_all(filtered, "ctx", split_axis=1, concat_axis=2, tiled=True)
    clean_y, errors = error_terms(inputs, filtered_rows, skip_gain, cotangent_rows)
    clean_output = clean_y.astype(jnp.bfloat16)
    error_section = first_section(
        lax.all_to_all(errors, "ctx", split_axis=2, concat_axis=1, tiled=True), col_start
    )
    error_spec = to_spectrum(error_section)
    error_real = error_spec[:, 0]
    error_imag = error_spec[:, 1]
    term_real = error_real * spectrum_real + error_imag * spectrum_imag
    term_imag = error_imag * spectrum_real - error_real * spectrum_imag
    local_grad = jnp.stack([term_real[0] + term_real[1], term_imag[0] + term_imag[1]], 0) * (
        1.0 / (N1 * N2)
    )
    grad_shard = lax.psum_scatter(
        local_grad.astype(jnp.bfloat16), "dp", scatter_dimension=2, tiled=True
    ).astype(jnp.float32)
    return (clean_output.reshape(1, row_count * N2, channels), grad_shard)


def solution(mesh):
    dp, ctx = mesh.shape["dp"], mesh.shape["ctx"]

    def run(embeds, *rest):
        apart = dp == 2 and embeds.shape[2] % (dp * ctx) == 0 and N1 // ctx == 16 and embeds.shape[2] // (dp * ctx) > 1
        return jax.shard_map(
            by_channel_body if apart else body,
            mesh=mesh,
            in_specs=(
                P("dp", "ctx", None),
                P("dp", "ctx", None),
                P("dp", "ctx", None),
                P(None, "ctx", None, None),
                P(),
            ),
            out_specs=(P("dp", "ctx", None), P(None, "ctx", "dp", None)),
            check_vma=False,
        )(embeds, *rest)

    return run
```

```python
import functools

import jax
import jax.numpy as jnp
import numpy as np
from jax import lax
from jax.experimental import pallas as pl
from jax.experimental.pallas import tpu as pltpu
from jax.sharding import PartitionSpec as P

N1 = 256
N2 = 256
BF16 = jnp.bfloat16
F32 = jnp.float32
KEPT = jnp.float32
HALF = 144
VMEM = 26 << 20

two_pi = 6.283185307179586
smart_weight = 2.0


def tables():
    ids = np.arange(N1)
    phase = (ids[:, None] * ids[None, :] % N1) * (two_pi / N1)
    cos_table, sin_table = np.cos(phase), np.sin(phase)
    split_rows = np.concatenate([cos_table[:HALF], -sin_table[:HALF]], 0)
    forward_table = np.block([[cos_table, -sin_table], [sin_table, cos_table]])
    weight = np.where(ids[: N1 // 2] == 0, 1.0, 2.0) / (N1 * N2)
    join_rows = np.concatenate([cos_table[:, : N1 // 2] * weight, -sin_table[:, : N1 // 2] * weight], 1)
    mirror_rows = np.zeros((HALF, N1))
    mirror_rows[ids[:HALF], -ids[:HALF] % N1] = 1
    mirror_cols = np.eye(N2)[::-1]
    lower_rows = np.zeros((N1 // 2, HALF))
    lower_rows[ids[: N1 // 2], N1 // 2 - ids[: N1 // 2]] = 1
    angle = (ids[:HALF, None] * ids[None, :]) * (two_pi / (N1 * N2))
    twiddle = np.stack([np.cos(angle), np.sin(angle)], 0)
    small = (split_rows, forward_table, join_rows, mirror_rows, mirror_cols, lower_rows)
    small = [jnp.asarray(t.astype(jnp.bfloat16)) for t in small]
    return (*small, jnp.asarray(twiddle.astype(np.float32)))


def dot(a, b):
    return jnp.dot(a, b, preferred_element_type=F32)


def near_device(place_ref, j, hop, plane, hops):
    far = (place_ref[0] ^ (j // plane)) * hops + (place_ref[1] ^ hop)
    return far * plane + (place_ref[2] ^ (j % plane))


def forward(signals, split_ref, fwd_ref, tw_cos, tw_sin):
    halves = []
    for x in signals:
        part = dot(split_ref[...], x)
        part_real, part_imag = part[:HALF], part[HALF:]
        out_real = part_real * tw_cos + part_imag * tw_sin
        out_imag = part_imag * tw_cos - part_real * tw_sin
        halves.append(jnp.concatenate([out_real.astype(BF16), out_imag.astype(BF16)], 1))
    spectra = dot(jnp.concatenate(halves, 0), fwd_ref[...])
    return [spectra[i * HALF : (i + 1) * HALF] for i in range(len(signals))]


def hermitian_part(filter_real, filter_imag, mirror_rows, mirror_cols):
    rows = dot(mirror_rows, jnp.concatenate([filter_real, filter_imag], 1)).astype(BF16)
    flipped = dot(jnp.concatenate([rows[:, :N2], rows[:, N2:]], 0), mirror_cols)
    out = []
    for part, other, sign in ((filter_real, flipped[:HALF], 0.5), (filter_imag, flipped[HALF:], -0.5)):
        top = other[:8]
        row = lax.broadcasted_iota(jnp.int32, top.shape, 0)
        top = jnp.where(row == 0, pltpu.roll(top, 1, 1), top)
        other = jnp.concatenate([top, other[8:]], 0)
        out.append(0.5 * part[:HALF].astype(F32) + sign * other)
    return out


def gradient(err_spectra, spectra):
    total_real = total_imag = 0.0
    for err_spec, spec in zip(err_spectra, spectra):
        err_real, err_imag = err_spec[:, :N2], err_spec[:, N2:]
        real, imag = spec[:, :N2], spec[:, N2:]
        total_real += err_real * real + err_imag * imag
        total_imag += err_imag * real - err_real * imag
    return total_real, total_imag


def conv_kernel(
    gain_ref, recv_ref, split_ref, fwd_ref, join_ref, mirror_ref, cols_ref, tw_ref,
    send_ref, gap_ref, spec_ref, part_ref,
):
    count, ctx = recv_ref.shape[:2]
    q = pl.program_id(0)
    tw_cos, tw_sin = tw_ref[0], tw_ref[1]
    signals = []
    for d in range(count):
        clean = recv_ref[d, :, 0, q].reshape(N1, N2)
        perturb = recv_ref[d, :, 1, q].reshape(N1, N2)
        signals += [clean, (clean.astype(F32) + perturb.astype(F32)).astype(BF16)]
    spectra = forward(signals, split_ref, fwd_ref, tw_cos, tw_sin)
    filter_real, filter_imag = hermitian_part(
        recv_ref[0, :, 2, q].reshape(N1, N2), recv_ref[1, :, 2, q].reshape(N1, N2), mirror_ref[...], cols_ref[...]
    )
    products = []
    for spec in spectra:
        real, imag = spec[:, :N2], spec[:, N2:]
        prod_real = (filter_real * real - filter_imag * imag).astype(BF16)
        minus_imag = (-filter_real * imag - filter_imag * real).astype(BF16)
        products.append(jnp.concatenate([prod_real, minus_imag], 1))
    back = dot(jnp.concatenate(products, 0), fwd_ref[...])
    mixed, middle = [], []
    for i in range(2 * count):
        back_real, minus_imag = back[i * HALF : (i + 1) * HALF, :N2], back[i * HALF : (i + 1) * HALF, N2:]
        mixed_real = (back_real * tw_cos + minus_imag * tw_sin).astype(BF16)
        mixed_imag = (back_real * tw_sin - minus_imag * tw_cos).astype(BF16)
        mixed.append(jnp.concatenate([mixed_real[: N1 // 2], mixed_imag[: N1 // 2]], 0))
        middle.append(mixed_real[N1 // 2 :].astype(F32)[:1])
    conv = dot(join_ref[...], jnp.concatenate(mixed, 1))
    parity = lax.broadcasted_iota(jnp.int32, (N1, N2), 0) % 2
    alternate = (1 - 2 * parity).astype(F32) * (1.0 / (N1 * N2))
    gain = gain_ref[q]
    errors = []
    for d in range(count):
        pair = []
        for i in range(2):
            k = 2 * d + i
            wide = signals[k].astype(F32)
            filtered = conv[:, k * N2 : (k + 1) * N2] + alternate * middle[k]
            pair.append((wide, wide * filtered.astype(BF16).astype(F32) + gain * wide))
        (clean, clean_y), (shifted, shifted_y) = pair
        send_ref[d, :, 0, q] = clean_y.astype(BF16).reshape(ctx, -1, N2)
        gap = smart_weight * (shifted_y - clean_y)
        gap_ref[q, d] = gap.astype(gap_ref.dtype)
        spec_ref[q, d] = spectra[2 * d].astype(spec_ref.dtype)
        errors.append((shifted * gap).astype(BF16))
    total_real, total_imag = gradient(forward(errors, split_ref, fwd_ref, tw_cos, tw_sin), spectra[1::2])
    part_ref[q, 0] = total_real
    part_ref[q, 1] = total_imag


def grad_kernel(place_ref, recv_ref, gap_ref, spec_ref, part_ref, *refs, hops):
    cot_refs, refs = refs[:hops], refs[hops:]
    split_ref, fwd_ref, cols_ref, lower_ref, tw_ref, _, send_ref, cot_rows = refs
    count, ctx = recv_ref.shape[:2]
    near = cot_refs[0].shape[0]
    plane = near // count
    q = pl.program_id(0)
    for hop, cot_ref in enumerate(cot_refs):
        for j in range(near):
            cot_rows[near_device(place_ref, j, hop, plane, hops)] = cot_ref[j, q]
    errors = []
    for d in range(count):
        clean = recv_ref[d, :, 0, q].reshape(N1, N2).astype(F32)
        cot = cot_rows[d * ctx : (d + 1) * ctx].reshape(N1, N2).astype(F32)
        errors.append((clean * (cot - gap_ref[q, d].astype(F32))).astype(BF16))
    spectra = [spec_ref[q, d].astype(F32) for d in range(count)]
    total_real, total_imag = gradient(forward(errors, split_ref, fwd_ref, tw_ref[0], tw_ref[1]), spectra)
    total_real += part_ref[q, 0]
    total_imag += part_ref[q, 1]
    scale = 1.0 / (N1 * N2)
    upper = jnp.concatenate([(total_real * scale).astype(BF16), (total_imag * scale).astype(BF16)], 1)
    lower = dot(lower_ref[...], upper).astype(BF16)
    lower = dot(jnp.concatenate([lower[:, :N2], lower[:, N2:]], 0), cols_ref[...])
    lower_real, lower_imag = lower[: N1 // 2].astype(BF16), (-lower[N1 // 2 :]).astype(BF16)
    width = N2 // count
    for i in range(count):
        first = upper[: N1 // 2, i * width : (i + 1) * width]
        second = upper[: N1 // 2, N2 + i * width : N2 + (i + 1) * width]
        upper_pair = jnp.concatenate([first, second], 1)
        cols = slice(i * width, (i + 1) * width)
        lower_pair = jnp.concatenate([lower_real[:, cols], lower_imag[:, cols]], 1)
        send_ref[i, : ctx // 2, 1, q] = upper_pair.reshape(ctx // 2, -1, 2 * width)
        send_ref[i, ctx // 2 :, 1, q] = lower_pair.reshape(ctx // 2, -1, 2 * width)


def whole(x):
    return pl.BlockSpec(x.shape, lambda *_: (0,) * x.ndim)


def near(x):
    return pltpu.with_memory_space_constraint(x, pltpu.VMEM)


def far(x):
    return pltpu.with_memory_space_constraint(x, pltpu.HBM)


def conv_call(gain, received, tabs):
    dp, ctx, _, per, rows, _ = received.shape
    split_rows, forward_table, join_rows, mirror_rows, mirror_cols, _, twiddle = tabs
    tabs = (split_rows, forward_table, join_rows, mirror_rows, mirror_cols, twiddle)
    return pl.pallas_call(
        conv_kernel,
        grid=(per,),
        in_specs=[
            pl.BlockSpec(memory_space=pltpu.SMEM),
            pl.BlockSpec(memory_space=pltpu.VMEM),
            *[whole(t) for t in tabs],
        ],
        out_specs=[pl.BlockSpec(memory_space=pltpu.VMEM)] * 4,
        out_shape=[
            pltpu.VMEM((dp, ctx, 2, per, rows, N2), BF16),
            pltpu.VMEM((per, dp, N1, N2), KEPT),
            pltpu.VMEM((per, dp, HALF, 2 * N2), KEPT),
            pltpu.VMEM((per, 2, HALF, N2), F32),
        ],
        compiler_params=pltpu.CompilerParams(vmem_limit_bytes=VMEM),
        cost_estimate=pl.CostEstimate(flops=per * dp * 5 * 6 * N1**3, bytes_accessed=8 << 20, transcendentals=0),
        name="conv",
    )(gain, received, *[far(t) for t in tabs])


def grad_call(place, received, kept, cots, tabs, send):
    dp, ctx, _, per, rows, _ = received.shape
    split_rows, forward_table, _, _, mirror_cols, lower_rows, twiddle = tabs
    tabs = (split_rows, forward_table, mirror_cols, lower_rows, twiddle)
    operands = (place, received, *[near(x) for x in kept], *[near(x) for x in cots], *[far(t) for t in tabs], near(send))
    return pl.pallas_call(
        functools.partial(grad_kernel, hops=len(cots)),
        grid=(per,),
        in_specs=[
            pl.BlockSpec(memory_space=pltpu.SMEM),
            pl.BlockSpec(memory_space=pltpu.VMEM),
            *[pl.BlockSpec(memory_space=pltpu.VMEM)] * 3,
            *[pl.BlockSpec(memory_space=pltpu.VMEM) for _ in cots],
            *[whole(t) for t in tabs],
            pl.BlockSpec(memory_space=pltpu.VMEM),
        ],
        out_specs=pl.BlockSpec(memory_space=pltpu.VMEM),
        out_shape=pltpu.VMEM(send.shape, BF16),
        scratch_shapes=[pltpu.VMEM((dp * ctx, rows, N2), BF16)],
        input_output_aliases={len(operands) - 1: 0},
        compiler_params=pltpu.CompilerParams(vmem_limit_bytes=VMEM),
        cost_estimate=pl.CostEstimate(flops=per * dp * 6 * N1**3, bytes_accessed=8 << 20, transcendentals=0),
        name="grad",
    )(*operands)


def outward_kernel(index_ref, *refs):
    *in_refs, out_ref, rows_ref = refs
    count, _, per, rows, width = out_ref.shape
    channels = count * per
    for t, in_ref in enumerate(in_refs):
        for r in range(rows):
            block = in_ref[0, r].astype(F32).T
            rows_ref[pl.ds(r, channels, stride=rows), :] = block
        out_ref[:, t] = rows_ref[...].astype(BF16).reshape(count, per, rows, width)


def outward(index, arrays, count):
    _, rows, _, channels = arrays[0].shape
    per = channels // count
    width = 128
    picks = [(lambda h, s: (s[0], 0, h, 0)) if a.shape[0] > 1 else (lambda h, s: (0, 0, h, 0)) for a in arrays]
    return pl.pallas_call(
        outward_kernel,
        grid_spec=pltpu.PrefetchScalarGridSpec(
            num_scalar_prefetch=1,
            grid=(N2 // width,),
            in_specs=[pl.BlockSpec((1, rows, width, channels), pick) for pick in picks],
            out_specs=pl.BlockSpec((count, len(arrays), per, rows, width), lambda h, s: (0, 0, 0, 0, h)),
            scratch_shapes=[pltpu.VMEM((channels * rows, width), F32)],
        ),
        out_shape=jax.ShapeDtypeStruct((count, len(arrays), per, rows, N2), BF16),
        compiler_params=pltpu.CompilerParams(vmem_limit_bytes=VMEM),
        cost_estimate=pl.CostEstimate(flops=0, bytes_accessed=(4 * len(arrays)) << 20, transcendentals=0),
        name="outward",
    )(index, *arrays)


def outward_near_kernel(place_ref, in_ref, *refs, hops, plane):
    *out_refs, rows_ref = refs
    _, per, rows, width = out_refs[0].shape
    channels = in_ref.shape[3]
    for r in range(rows):
        rows_ref[pl.ds(r, channels, stride=rows), :] = in_ref[0, r].astype(F32).T
    for j, out_ref in enumerate(out_refs):
        for hop in range(hops):
            block = near_device(place_ref, j, hop, plane, hops) * (per * rows)
            rows_here = rows_ref[pl.ds(pl.multiple_of(block, per * rows), per * rows), :]
            out_ref[hop] = rows_here.astype(BF16).reshape(per, rows, width)


def outward_near(place, x, count, hops, plane):
    _, rows, _, channels = x.shape
    per = channels // count
    width = 128
    return pl.pallas_call(
        functools.partial(outward_near_kernel, hops=hops, plane=plane),
        grid=(N2 // width,),
        in_specs=[
            pl.BlockSpec(memory_space=pltpu.SMEM),
            pl.BlockSpec((1, rows, width, channels), lambda h: (0, 0, h, 0)),
        ],
        out_specs=[pl.BlockSpec((hops, per, rows, width), lambda h: (0, 0, 0, h))] * (count // hops),
        out_shape=[jax.ShapeDtypeStruct((hops, per, rows, N2), BF16)] * (count // hops),
        scratch_shapes=[pltpu.VMEM((channels * rows, width), F32)],
        compiler_params=pltpu.CompilerParams(vmem_limit_bytes=VMEM),
        cost_estimate=pl.CostEstimate(flops=0, bytes_accessed=2 << 20, transcendentals=0),
        name="outward_near",
    )(place, x)


def regroup_kernel(*refs, count):
    for i, in_ref in enumerate(refs[:count]):
        for j, out_ref in enumerate(refs[count:]):
            out_ref[i] = in_ref[j]


def regroup(arrays):
    hops, *block = arrays[0].shape
    return pl.pallas_call(
        functools.partial(regroup_kernel, count=len(arrays)),
        out_shape=[jax.ShapeDtypeStruct((len(arrays), *block), BF16)] * hops,
        compiler_params=pltpu.CompilerParams(vmem_limit_bytes=VMEM),
        cost_estimate=pl.CostEstimate(flops=0, bytes_accessed=2 << 20, transcendentals=0),
        name="regroup",
    )(*arrays)


def homeward_kernel(last_ref, y_ref, grad_ref, rows_ref):
    count, _, per, rows, _ = last_ref.shape
    channels = count * per
    width = rows_ref.shape[1]
    lanes = pl.ds(pl.multiple_of(pl.program_id(0) * width, width), width)
    for t in range(2):
        rows_ref[...] = last_ref[:, t, :, :, lanes].astype(F32).reshape(channels * rows, width)
        for r in range(rows):
            block = rows_ref[pl.ds(r, channels, stride=rows), :].T
            if t == 0:
                y_ref[r] = block.astype(BF16)
            else:
                grad_ref[0, r] = block


def homeward(last):
    count, _, per, rows, _ = last.shape
    channels = count * per
    width = 128
    return pl.pallas_call(
        homeward_kernel,
        grid=(N2 // width,),
        in_specs=[pl.BlockSpec(memory_space=pltpu.VMEM)],
        out_specs=[
            pl.BlockSpec((rows, width, channels), lambda h: (0, h, 0)),
            pl.BlockSpec((1, rows, width, channels), lambda h: (h, 0, 0, 0)),
        ],
        out_shape=[
            jax.ShapeDtypeStruct((rows, N2, channels), BF16),
            jax.ShapeDtypeStruct((2, rows, width, channels), F32),
        ],
        scratch_shapes=[pltpu.VMEM((channels * rows, width), F32)],
        compiler_params=pltpu.CompilerParams(vmem_limit_bytes=VMEM),
        cost_estimate=pl.CostEstimate(flops=0, bytes_accessed=5 << 20, transcendentals=0),
        name="homeward",
    )(near(last))


def by_channel_body(embeds, perturb, cotangent, filter_spectrum, skip_gain):
    dp, ctx = lax.axis_size("dp"), lax.axis_size("ctx")
    d, c = lax.axis_index("dp"), lax.axis_index("ctx")
    axes = ("dp", "ctx")
    count = dp * ctx
    channels = embeds.shape[2]
    rows = N1 // ctx
    per = channels // count
    plane = 4
    hops = ctx // plane
    tabs = tables()
    place = jnp.stack([d, c // plane, c % plane])

    def matrix(x):
        return far(x.reshape(1, rows, N2, channels))

    def exchange(x, mask):
        return lax.ppermute(x, axes, [(i, i ^ mask) for i in range(count)]) if mask else x

    first = outward(place, [matrix(embeds), matrix(perturb), far(filter_spectrum)], count)
    received = lax.all_to_all(first, axes, 0, 0, tiled=True).reshape(dp, ctx, 3, per, rows, N2)
    cots = outward_near(place, matrix(cotangent), count, hops, plane)
    cots = regroup([exchange(x, j // plane * ctx + j % plane) for j, x in enumerate(cots)])
    received = near(received)
    *early, late = cots
    late, received = lax.optimization_barrier((late, received))
    cots = [exchange(x, hop * plane) for hop, x in enumerate([*early, late])]
    gain = lax.dynamic_slice(skip_gain, ((d * ctx + c) * per,), (per,))
    send, *kept = conv_call(gain, received, tabs)
    send = grad_call(place, received, kept, cots, tabs, send)
    last = lax.all_to_all(send.reshape(count, 2, per, rows, N2), axes, 0, 0, tiled=True)
    y, grad = homeward(last)
    return y.reshape(1, rows * N2, channels), grad


def trig_table(period):
    row_ids = jnp.arange(period, dtype=jnp.int32)
    exponent = row_ids[:, None] * row_ids[None, :] % period
    phase_angle = exponent.astype(jnp.float32) * (two_pi / period)
    return (jnp.cos(phase_angle).astype(jnp.bfloat16), jnp.sin(phase_angle).astype(jnp.bfloat16))


def twiddle(row_first, row_count, col_first, col_count):
    row_ids = row_first + jnp.arange(row_count, dtype=jnp.int32)
    col_ids = col_first + jnp.arange(col_count, dtype=jnp.int32)
    exponent = row_ids[:, None] * col_ids[None, :] % (N1 * N2)
    phase_angle = exponent.astype(jnp.float32) * (two_pi / (N1 * N2))
    return (jnp.cos(phase_angle)[:, :, None], jnp.sin(phase_angle)[:, :, None])


def first_section(values, col_start):
    cos_table, sin_table = trig_table(N1)
    part_real = jnp.einsum("kn,snmc->skmc", cos_table, values, preferred_element_type=jnp.float32)
    part_imag = -jnp.einsum("kn,snmc->skmc", sin_table, values, preferred_element_type=jnp.float32)
    tw_cos, tw_sin = twiddle(0, N1, col_start, values.shape[2])
    out_real = part_real * tw_cos + part_imag * tw_sin
    out_imag = part_imag * tw_cos - part_real * tw_sin
    return jnp.stack([out_real, out_imag], 1).astype(jnp.bfloat16)


def second_section(section_rows):
    cos_table, sin_table = trig_table(N2)
    with_cos = jnp.einsum(
        "sprnc,kn->sprkc", section_rows, cos_table, preferred_element_type=jnp.float32
    )
    with_sin = jnp.einsum(
        "sprnc,kn->sprkc", section_rows, sin_table, preferred_element_type=jnp.float32
    )
    return jnp.stack([with_cos[:, 0] + with_sin[:, 1], with_cos[:, 1] - with_sin[:, 0]], 1)


def spectral_inverse(product, row_start):
    cos_table, sin_table = trig_table(N2)
    with_cos = jnp.einsum("sprkc,nk->sprnc", product, cos_table, preferred_element_type=jnp.float32)
    with_sin = jnp.einsum("sprkc,nk->sprnc", product, sin_table, preferred_element_type=jnp.float32)
    part_real = with_cos[:, 0] - with_sin[:, 1]
    part_imag = with_cos[:, 1] + with_sin[:, 0]
    tw_cos, tw_sin = twiddle(row_start, product.shape[2], 0, N2)
    out_real = part_real * tw_cos - part_imag * tw_sin
    out_imag = part_imag * tw_cos + part_real * tw_sin
    return jnp.stack([out_real, out_imag], 1).astype(jnp.bfloat16)


def column_inverse(mixed_cols):
    cos_table, sin_table = trig_table(N1)
    with_cos = jnp.einsum(
        "nk,skmc->snmc", cos_table, mixed_cols[:, 0], preferred_element_type=jnp.float32
    )
    with_sin = jnp.einsum(
        "nk,skmc->snmc", sin_table, mixed_cols[:, 1], preferred_element_type=jnp.float32
    )
    return ((with_cos - with_sin) * (1.0 / (N1 * N2))).astype(jnp.bfloat16)


def to_spectrum(section_cols):
    return second_section(
        lax.all_to_all(section_cols, "ctx", split_axis=2, concat_axis=3, tiled=True)
    )


def error_terms(signal, filtered, skip_gain, cotangent_view):
    signal_wide = signal.astype(jnp.float32)
    filtered_wide = lax.optimization_barrier(filtered).astype(jnp.float32)
    outputs = signal_wide * filtered_wide + skip_gain * signal_wide
    clean_y = outputs[0]
    smooth_gap = outputs[1] - clean_y
    err_clean = signal_wide[0] * (cotangent_view.astype(jnp.float32) - smart_weight * smooth_gap)
    err_shift = signal_wide[1] * (smart_weight * smooth_gap)
    return (clean_y, jnp.stack([err_clean, err_shift], 0).astype(jnp.bfloat16))


def body(embeds, perturb, cotangent, filter_spectrum, skip_gain):
    ctx_size = lax.axis_size("ctx")
    ctx_index = lax.axis_index("ctx")
    channels = embeds.shape[2]
    row_count = N1 // ctx_size
    col_count = N2 // ctx_size
    row_start = ctx_index * row_count
    col_start = ctx_index * col_count
    clean_rows = embeds[0].reshape(row_count, N2, channels)
    perturb_rows = perturb[0].reshape(row_count, N2, channels)
    shifted = (clean_rows.astype(jnp.float32) + perturb_rows.astype(jnp.float32)).astype(
        jnp.bfloat16
    )
    inputs = jnp.stack([clean_rows, shifted], 0)
    signal_cols = lax.all_to_all(inputs, "ctx", split_axis=2, concat_axis=1, tiled=True)
    section_cols, signal_cols = (first_section(signal_cols, col_start), signal_cols)
    spectra = to_spectrum(section_cols)
    filter_real = filter_spectrum[0]
    filter_imag = filter_spectrum[1]
    spectrum_real = spectra[:, 0]
    spectrum_imag = spectra[:, 1]
    product = jnp.stack(
        [
            filter_real * spectrum_real - filter_imag * spectrum_imag,
            filter_real * spectrum_imag + filter_imag * spectrum_real,
        ],
        1,
    ).astype(jnp.bfloat16)
    mixed_rows = spectral_inverse(product, row_start)
    filtered = column_inverse(
        lax.all_to_all(mixed_rows, "ctx", split_axis=3, concat_axis=2, tiled=True)
    )
    cotangent_rows = cotangent[0].reshape(row_count, N2, channels)
    filtered_rows = lax.all_to_all(filtered, "ctx", split_axis=1, concat_axis=2, tiled=True)
    clean_y, errors = error_terms(inputs, filtered_rows, skip_gain, cotangent_rows)
    clean_output = clean_y.astype(jnp.bfloat16)
    error_section = first_section(
        lax.all_to_all(errors, "ctx", split_axis=2, concat_axis=1, tiled=True), col_start
    )
    error_spec = to_spectrum(error_section)
    error_real = error_spec[:, 0]
    error_imag = error_spec[:, 1]
    term_real = error_real * spectrum_real + error_imag * spectrum_imag
    term_imag = error_imag * spectrum_real - error_real * spectrum_imag
    local_grad = jnp.stack([term_real[0] + term_real[1], term_imag[0] + term_imag[1]], 0) * (
        1.0 / (N1 * N2)
    )
    grad_shard = lax.psum_scatter(
        local_grad.astype(jnp.bfloat16), "dp", scatter_dimension=2, tiled=True
    ).astype(jnp.float32)
    return (clean_output.reshape(1, row_count * N2, channels), grad_shard)


def solution(mesh):
    dp, ctx = mesh.shape["dp"], mesh.shape["ctx"]

    def run(embeds, *rest):
        apart = dp == 2 and embeds.shape[2] % (dp * ctx) == 0 and N1 // ctx == 16 and embeds.shape[2] // (dp * ctx) > 1
        return jax.shard_map(
            by_channel_body if apart else body,
            mesh=mesh,
            in_specs=(
                P("dp", "ctx", None),
                P("dp", "ctx", None),
                P("dp", "ctx", None),
                P(None, "ctx", None, None),
                P(),
            ),
            out_specs=(P("dp", "ctx", None), P(None, "ctx", "dp", None)),
            check_vma=False,
        )(embeds, *rest)

    return run
```

```python
import functools

import jax
import jax.numpy as jnp
import numpy as np
from jax import lax
from jax.experimental import pallas as pl
from jax.experimental.pallas import tpu as pltpu
from jax.sharding import PartitionSpec as P

N1 = 256
N2 = 256
BF16 = jnp.bfloat16
F32 = jnp.float32
KEPT = jnp.float32
HALF = 144
VMEM = 26 << 20

two_pi = 6.283185307179586
smart_weight = 2.0


def tables():
    ids = np.arange(N1)
    phase = (ids[:, None] * ids[None, :] % N1) * (two_pi / N1)
    cos_table, sin_table = np.cos(phase), np.sin(phase)
    split_rows = np.concatenate([cos_table[:HALF], -sin_table[:HALF]], 0)
    forward_table = np.block([[cos_table, -sin_table], [sin_table, cos_table]])
    weight = np.where(ids[: N1 // 2] == 0, 1.0, 2.0) / (N1 * N2)
    join_rows = np.concatenate([cos_table[:, : N1 // 2] * weight, -sin_table[:, : N1 // 2] * weight], 1)
    mirror_rows = np.zeros((HALF, N1))
    mirror_rows[ids[:HALF], -ids[:HALF] % N1] = 1
    mirror_cols = np.eye(N2)[::-1]
    angle = (ids[:HALF, None] * ids[None, :]) * (two_pi / (N1 * N2))
    twiddle = np.stack([np.cos(angle), np.sin(angle)], 0)
    small = (split_rows, forward_table, join_rows, mirror_rows, mirror_cols)
    small = [jnp.asarray(t.astype(jnp.bfloat16)) for t in small]
    return (*small, jnp.asarray(twiddle.astype(np.float32)))


def dot(a, b):
    return jnp.dot(a, b, preferred_element_type=F32)


def near_device(place_ref, j, hop, plane, hops):
    far = (place_ref[0] ^ (j // plane)) * hops + (place_ref[1] ^ hop)
    return far * plane + (place_ref[2] ^ (j % plane))


def forward(signals, split_ref, fwd_ref, tw_cos, tw_sin):
    halves = []
    for x in signals:
        part = dot(split_ref[...], x)
        part_real, part_imag = part[:HALF], part[HALF:]
        out_real = part_real * tw_cos + part_imag * tw_sin
        out_imag = part_imag * tw_cos - part_real * tw_sin
        halves.append(jnp.concatenate([out_real.astype(BF16), out_imag.astype(BF16)], 1))
    spectra = dot(jnp.concatenate(halves, 0), fwd_ref[...])
    return [spectra[i * HALF : (i + 1) * HALF] for i in range(len(signals))]


def hermitian_part(filter_real, filter_imag, mirror_rows, mirror_cols):
    rows = dot(mirror_rows, jnp.concatenate([filter_real, filter_imag], 1)).astype(BF16)
    flipped = dot(jnp.concatenate([rows[:, :N2], rows[:, N2:]], 0), mirror_cols)
    out = []
    for part, other, sign in ((filter_real, flipped[:HALF], 0.5), (filter_imag, flipped[HALF:], -0.5)):
        top = other[:8]
        row = lax.broadcasted_iota(jnp.int32, top.shape, 0)
        top = jnp.where(row == 0, pltpu.roll(top, 1, 1), top)
        other = jnp.concatenate([top, other[8:]], 0)
        out.append(0.5 * part[:HALF].astype(F32) + sign * other)
    return out


def gradient(err_spectra, spectra):
    total_real = total_imag = 0.0
    for err_spec, spec in zip(err_spectra, spectra):
        err_real, err_imag = err_spec[:, :N2], err_spec[:, N2:]
        real, imag = spec[:, :N2], spec[:, N2:]
        total_real += err_real * real + err_imag * imag
        total_imag += err_imag * real - err_real * imag
    return total_real, total_imag


def conv_kernel(
    gain_ref, recv_ref, split_ref, fwd_ref, join_ref, mirror_ref, cols_ref, tw_ref,
    send_ref, gap_ref, spec_ref, part_ref, *held_refs,
):
    count, ctx = recv_ref.shape[:2]
    q = pl.program_id(0)

    @pl.when(q == 0)
    def _():
        for held_ref, table_ref in zip(held_refs, (split_ref, fwd_ref, tw_ref)):
            held_ref[...] = table_ref[...]

    tw_cos, tw_sin = tw_ref[0], tw_ref[1]
    signals = []
    for d in range(count):
        clean = recv_ref[d, :, 0, q].reshape(N1, N2)
        perturb = recv_ref[d, :, 1, q].reshape(N1, N2)
        signals += [clean, (clean.astype(F32) + perturb.astype(F32)).astype(BF16)]
    spectra = forward(signals, split_ref, fwd_ref, tw_cos, tw_sin)
    filter_real, filter_imag = hermitian_part(
        recv_ref[0, :, 2, q].reshape(N1, N2), recv_ref[1, :, 2, q].reshape(N1, N2), mirror_ref[...], cols_ref[...]
    )
    products = []
    for spec in spectra:
        real, imag = spec[:, :N2], spec[:, N2:]
        prod_real = (filter_real * real - filter_imag * imag).astype(BF16)
        minus_imag = (-filter_real * imag - filter_imag * real).astype(BF16)
        products.append(jnp.concatenate([prod_real, minus_imag], 1))
    back = dot(jnp.concatenate(products, 0), fwd_ref[...])
    mixed, middle = [], []
    for i in range(2 * count):
        back_real, minus_imag = back[i * HALF : (i + 1) * HALF, :N2], back[i * HALF : (i + 1) * HALF, N2:]
        mixed_real = (back_real * tw_cos + minus_imag * tw_sin).astype(BF16)
        mixed_imag = (back_real * tw_sin - minus_imag * tw_cos).astype(BF16)
        mixed.append(jnp.concatenate([mixed_real[: N1 // 2], mixed_imag[: N1 // 2]], 0))
        middle.append(mixed_real[N1 // 2 :].astype(F32)[:1])
    conv = dot(join_ref[...], jnp.concatenate(mixed, 1))
    parity = lax.broadcasted_iota(jnp.int32, (N1, N2), 0) % 2
    alternate = (1 - 2 * parity).astype(F32) * (1.0 / (N1 * N2))
    gain = gain_ref[q]
    errors = []
    for d in range(count):
        pair = []
        for i in range(2):
            k = 2 * d + i
            wide = signals[k].astype(F32)
            filtered = conv[:, k * N2 : (k + 1) * N2] + alternate * middle[k]
            pair.append((wide, wide * filtered.astype(BF16).astype(F32) + gain * wide))
        (clean, clean_y), (shifted, shifted_y) = pair
        send_ref[d, :, 0, q] = clean_y.astype(BF16).reshape(ctx, -1, N2)
        gap = smart_weight * (shifted_y - clean_y)
        gap_ref[q, d] = gap.astype(gap_ref.dtype)
        spec_ref[q, d] = spectra[2 * d].astype(spec_ref.dtype)
        errors.append((shifted * gap).astype(BF16))
    total_real, total_imag = gradient(forward(errors, split_ref, fwd_ref, tw_cos, tw_sin), spectra[1::2])
    part_ref[q, 0] = total_real
    part_ref[q, 1] = total_imag


def grad_kernel(place_ref, recv_ref, gap_ref, spec_ref, part_ref, *refs, hops):
    cot_refs, refs = refs[:hops], refs[hops:]
    split_ref, fwd_ref, tw_ref, _, send_ref, cot_rows = refs
    count, ctx = recv_ref.shape[:2]
    near = cot_refs[0].shape[0]
    plane = near // count
    per = recv_ref.shape[3]
    for hop, cot_ref in enumerate(cot_refs):
        for j in range(near):
            cot_rows[near_device(place_ref, j, hop, plane, hops)] = cot_ref[j]
    errors = []
    for q in range(per):
        for d in range(count):
            clean = recv_ref[d, :, 0, q].reshape(N1, N2).astype(F32)
            cot = cot_rows[d * ctx : (d + 1) * ctx, q].reshape(N1, N2).astype(F32)
            errors.append((clean * (cot - gap_ref[q, d])).astype(BF16))
    err_spectra = forward(errors, split_ref, fwd_ref, tw_ref[0], tw_ref[1])
    for q in range(per):
        spectra = [spec_ref[q, d] for d in range(count)]
        total = gradient(err_spectra[q * count : (q + 1) * count], spectra)
        send_grad(send_ref, q, *[t + part_ref[q, i] for i, t in enumerate(total)])


def send_grad(send_ref, q, total_real, total_imag):
    count, ctx, _, _, rows, _ = send_ref.shape
    total = jnp.concatenate([total_real, total_imag], 1) * (1.0 / (N1 * N2))
    upper, after = total[: N1 // 2], total[rows : N1 // 2 + rows]
    first = lax.broadcasted_iota(jnp.int32, upper.shape, 0) % rows == 0
    lower = jnp.where(first, after, upper).astype(BF16)
    upper = upper.astype(BF16)
    width = N2 // count
    for i in range(count):
        for half, x, side in ((0, upper, i), (1, lower, count - 1 - i)):
            cols = slice(side * width, (side + 1) * width)
            pair = jnp.concatenate([x[:, :N2][:, cols], x[:, N2:][:, cols]], 1)
            for block in range(ctx // 2):
                target = ctx - 1 - block if half else block
                send_ref[i, target, 1, q] = pair[block * rows : (block + 1) * rows]


def whole(x):
    return pl.BlockSpec(x.shape, lambda *_: (0,) * x.ndim)


def near(x):
    return pltpu.with_memory_space_constraint(x, pltpu.VMEM)


def far(x):
    return pltpu.with_memory_space_constraint(x, pltpu.HBM)


def conv_call(gain, received, tabs):
    dp, ctx, _, per, rows, _ = received.shape
    split_rows, forward_table, *_, twiddle = tabs
    held = [pltpu.VMEM(t.shape, t.dtype) for t in (split_rows, forward_table, twiddle)]
    return pl.pallas_call(
        conv_kernel,
        grid=(per,),
        in_specs=[
            pl.BlockSpec(memory_space=pltpu.SMEM),
            pl.BlockSpec(memory_space=pltpu.VMEM),
            *[whole(t) for t in tabs],
        ],
        out_specs=[pl.BlockSpec(memory_space=pltpu.VMEM)] * 7,
        out_shape=[
            pltpu.VMEM((dp, ctx, 2, per, rows, N2), BF16),
            pltpu.VMEM((per, dp, N1, N2), KEPT),
            pltpu.VMEM((per, dp, HALF, 2 * N2), KEPT),
            pltpu.VMEM((per, 2, HALF, N2), F32),
            *held,
        ],
        compiler_params=pltpu.CompilerParams(vmem_limit_bytes=VMEM),
        cost_estimate=pl.CostEstimate(flops=per * dp * 5 * 6 * N1**3, bytes_accessed=8 << 20, transcendentals=0),
        name="conv",
    )(gain, received, *[far(t) for t in tabs])


def grad_call(place, received, kept, cots, send):
    dp, ctx, _, per, rows, _ = received.shape
    *kept, split_rows, forward_table, twiddle = [near(x) for x in kept]
    operands = (place, received, *kept, *[near(x) for x in cots], split_rows, forward_table, twiddle, near(send))
    return pl.pallas_call(
        functools.partial(grad_kernel, hops=len(cots)),
        grid=(1,),
        in_specs=[
            pl.BlockSpec(memory_space=pltpu.SMEM),
            *[pl.BlockSpec(memory_space=pltpu.VMEM)] * (len(operands) - 1),
        ],
        out_specs=pl.BlockSpec(memory_space=pltpu.VMEM),
        out_shape=pltpu.VMEM(send.shape, BF16),
        scratch_shapes=[pltpu.VMEM((dp * ctx, per, rows, N2), BF16)],
        input_output_aliases={len(operands) - 1: 0},
        compiler_params=pltpu.CompilerParams(vmem_limit_bytes=VMEM),
        cost_estimate=pl.CostEstimate(flops=per * dp * 6 * N1**3, bytes_accessed=8 << 20, transcendentals=0),
        name="grad",
    )(*operands)


def outward_kernel(place_ref, *refs, count):
    in_refs, refs = refs[:count], refs[count:]
    out_ref, refs = refs[0], refs[1:]
    held_refs, (rows_ref, ready_ref, load_sems, store_sems) = refs[:count], refs[count:]
    devices, _, per, rows, _ = out_ref.shape
    pitch = rows_ref.shape[1] // (devices * per)
    width = rows_ref.shape[2]
    loads, stores = [], []
    for t, (in_ref, held_ref) in enumerate(zip(in_refs, held_refs)):
        source = in_ref.at[place_ref[0] if in_ref.shape[0] > 1 else 0]
        loads.append(pltpu.make_async_copy(source, held_ref, load_sems.at[t]))
        loads[t].start()
    for t, held_ref in enumerate(held_refs):
        loads[t].wait()
        for h in range(N2 // width):
            lanes = slice(h * width, (h + 1) * width)
            for r in range(rows):
                block = held_ref[r, lanes].astype(BF16).T.astype(F32)
                rows_ref[h, pl.ds(r, devices * per, stride=pitch), :] = block
            block = rows_ref[h].reshape(devices, per, pitch, width)[:, :, :rows].astype(BF16)
            ready_ref[t, :, :, :, lanes] = block
        stores.append(pltpu.make_async_copy(ready_ref.at[t], out_ref.at[:, t], store_sems.at[t]))
        stores[t].start()
    for store in stores:
        store.wait()


def outward(place, arrays, devices):
    _, rows, _, channels = arrays[0].shape
    count, per, width, pitch = len(arrays), channels // devices, 128, rows + 8
    shape = (devices, count, per, rows, N2)
    return pl.pallas_call(
        functools.partial(outward_kernel, count=count),
        in_specs=[pl.BlockSpec(memory_space=pltpu.SMEM), *[pl.BlockSpec(memory_space=pl.ANY)] * count],
        out_specs=pl.BlockSpec(memory_space=pl.ANY),
        out_shape=jax.ShapeDtypeStruct(shape, BF16),
        scratch_shapes=[
            *[pltpu.VMEM(a.shape[1:], a.dtype) for a in arrays],
            pltpu.VMEM((N2 // width, channels * pitch, width), F32),
            pltpu.VMEM((count, devices, per, rows, N2), BF16),
            pltpu.SemaphoreType.DMA((count,)),
            pltpu.SemaphoreType.DMA((count,)),
        ],
        compiler_params=pltpu.CompilerParams(vmem_limit_bytes=VMEM),
        cost_estimate=pl.CostEstimate(flops=0, bytes_accessed=7 << 20, transcendentals=0),
        name="outward",
    )(place, *arrays)


def outward_near_kernel(place_ref, in_ref, *refs, hops, plane):
    *out_refs, rows_ref = refs
    _, per, rows, width = out_refs[0].shape
    channels = in_ref.shape[3]
    pitch = rows_ref.shape[0] // channels
    for r in range(rows):
        rows_ref[pl.ds(r, channels, stride=pitch), :] = in_ref[0, r].T.astype(F32)
    for j, out_ref in enumerate(out_refs):
        for hop in range(hops):
            block = near_device(place_ref, j, hop, plane, hops) * (per * pitch)
            rows_here = rows_ref[pl.ds(pl.multiple_of(block, per * pitch), per * pitch), :]
            out_ref[hop] = rows_here.reshape(per, pitch, width)[:, :rows].astype(BF16)


def outward_near(place, x, count, hops, plane):
    _, rows, _, channels = x.shape
    per = channels // count
    width = 128
    return pl.pallas_call(
        functools.partial(outward_near_kernel, hops=hops, plane=plane),
        grid=(N2 // width,),
        in_specs=[
            pl.BlockSpec(memory_space=pltpu.SMEM),
            pl.BlockSpec((1, rows, width, channels), lambda h: (0, 0, h, 0)),
        ],
        out_specs=[pl.BlockSpec((hops, per, rows, width), lambda h: (0, 0, 0, h))] * (count // hops),
        out_shape=[jax.ShapeDtypeStruct((hops, per, rows, N2), BF16)] * (count // hops),
        scratch_shapes=[pltpu.VMEM((channels * (rows + 8), width), F32)],
        compiler_params=pltpu.CompilerParams(vmem_limit_bytes=VMEM),
        cost_estimate=pl.CostEstimate(flops=0, bytes_accessed=2 << 20, transcendentals=0),
        name="outward_near",
    )(place, x)


def regroup_kernel(*refs, count):
    for i, in_ref in enumerate(refs[:count]):
        for j, out_ref in enumerate(refs[count:]):
            out_ref[i] = in_ref[j]


def regroup(arrays):
    hops, *block = arrays[0].shape
    return pl.pallas_call(
        functools.partial(regroup_kernel, count=len(arrays)),
        out_shape=[jax.ShapeDtypeStruct((len(arrays), *block), BF16)] * hops,
        compiler_params=pltpu.CompilerParams(vmem_limit_bytes=VMEM),
        cost_estimate=pl.CostEstimate(flops=0, bytes_accessed=2 << 20, transcendentals=0),
        name="regroup",
    )(*arrays)


def homeward_kernel(place_ref, last_ref, y_hbm, grad_hbm, y_ref, grad_ref, rows_ref, sems):
    count, _, per, rows, _ = last_ref.shape
    width = rows_ref.shape[2]
    pitch = rows_ref.shape[1] // (count * per)
    lower = place_ref[1] >= place_ref[3]
    row = lax.broadcasted_iota(jnp.int32, (width, width), 0)
    col = lax.broadcasted_iota(jnp.int32, (width, width), 1)
    turn = (col == jnp.where(lower, width - 1 - row, row)).astype(F32)
    copies = []
    for step, (t, h) in enumerate(((1, 0), (1, 1), (0, 0), (0, 1))):
        lanes = slice(h * width, (h + 1) * width)
        block = last_ref[:, t, :, :, lanes].astype(F32)
        rows_ref.at[step].reshape(count, per, pitch, width)[:, :, :rows] = block
        sign = jnp.where(lower, -1.0, 1.0) if h else 1.0
        pick = (turn * sign).astype(BF16)
        for r in range(rows):
            slot = jnp.where(lower, (rows - r) % rows, r) if t else r
            block = rows_ref[step, pl.ds(slot, count * per, stride=pitch), :].astype(BF16)
            if t:
                grad_ref[h, r] = lax.dot_general(pick, block, (((1,), (1,)), ((), ())), preferred_element_type=F32)
            else:
                y_ref[r, lanes] = block.T
        if t:
            copies.append(pltpu.make_async_copy(grad_ref.at[h], grad_hbm.at[h], sems.at[step]))
        else:
            here = pl.ds(h * width, width)
            copies.append(pltpu.make_async_copy(y_ref.at[:, here], y_hbm.at[:, here], sems.at[step]))
        copies[step].start()
    for copy in copies:
        copy.wait()


def homeward(place, last):
    count, _, per, rows, _ = last.shape
    channels, width, pitch = count * per, 128, rows + 8
    y_shape, grad_shape = (rows, N2, channels), (2, rows, width, channels)
    return pl.pallas_call(
        homeward_kernel,
        in_specs=[pl.BlockSpec(memory_space=pltpu.SMEM), pl.BlockSpec(memory_space=pltpu.VMEM)],
        out_specs=[pl.BlockSpec(memory_space=pl.ANY)] * 2,
        out_shape=[jax.ShapeDtypeStruct(y_shape, BF16), jax.ShapeDtypeStruct(grad_shape, F32)],
        scratch_shapes=[
            pltpu.VMEM(y_shape, BF16),
            pltpu.VMEM(grad_shape, F32),
            pltpu.VMEM((4, channels * pitch, width), F32),
            pltpu.SemaphoreType.DMA((4,)),
        ],
        compiler_params=pltpu.CompilerParams(vmem_limit_bytes=VMEM),
        cost_estimate=pl.CostEstimate(flops=0, bytes_accessed=5 << 20, transcendentals=0),
        name="homeward",
    )(place, near(last))


def by_channel_body(embeds, perturb, cotangent, filter_spectrum, skip_gain):
    dp, ctx = lax.axis_size("dp"), lax.axis_size("ctx")
    d, c = lax.axis_index("dp"), lax.axis_index("ctx")
    axes = ("dp", "ctx")
    count = dp * ctx
    channels = embeds.shape[2]
    rows = N1 // ctx
    per = channels // count
    plane = 4
    hops = ctx // plane
    tabs = tables()
    place = jnp.stack([d, c // plane, c % plane, jnp.int32(hops // 2)])

    def matrix(x):
        return far(x.reshape(1, rows, N2, channels))

    def exchange(x, mask):
        return lax.ppermute(x, axes, [(i, i ^ mask) for i in range(count)]) if mask else x

    first = outward(place, [matrix(embeds), matrix(perturb), far(filter_spectrum)], count)
    received = lax.all_to_all(first, axes, 0, 0, tiled=True).reshape(dp, ctx, 3, per, rows, N2)
    cots = outward_near(place, matrix(cotangent), count, hops, plane)
    cots = regroup([exchange(x, j // plane * ctx + j % plane) for j, x in enumerate(cots)])
    received = near(received)
    *early, late = cots
    late, received = lax.optimization_barrier((late, received))
    cots = [exchange(x, hop * plane) for hop, x in enumerate([*early, late])]
    gain = lax.dynamic_slice(skip_gain, ((d * ctx + c) * per,), (per,))
    send, *kept = conv_call(gain, received, tabs)
    send = grad_call(place, received, kept, cots, send)
    last = lax.all_to_all(send.reshape(count, 2, per, rows, N2), axes, 0, 0, tiled=True)
    y, grad = homeward(place, last)
    return y.reshape(1, rows * N2, channels), grad


def trig_table(period):
    row_ids = jnp.arange(period, dtype=jnp.int32)
    exponent = row_ids[:, None] * row_ids[None, :] % period
    phase_angle = exponent.astype(jnp.float32) * (two_pi / period)
    return (jnp.cos(phase_angle).astype(jnp.bfloat16), jnp.sin(phase_angle).astype(jnp.bfloat16))


def twiddle(row_first, row_count, col_first, col_count):
    row_ids = row_first + jnp.arange(row_count, dtype=jnp.int32)
    col_ids = col_first + jnp.arange(col_count, dtype=jnp.int32)
    exponent = row_ids[:, None] * col_ids[None, :] % (N1 * N2)
    phase_angle = exponent.astype(jnp.float32) * (two_pi / (N1 * N2))
    return (jnp.cos(phase_angle)[:, :, None], jnp.sin(phase_angle)[:, :, None])


def first_section(values, col_start):
    cos_table, sin_table = trig_table(N1)
    part_real = jnp.einsum("kn,snmc->skmc", cos_table, values, preferred_element_type=jnp.float32)
    part_imag = -jnp.einsum("kn,snmc->skmc", sin_table, values, preferred_element_type=jnp.float32)
    tw_cos, tw_sin = twiddle(0, N1, col_start, values.shape[2])
    out_real = part_real * tw_cos + part_imag * tw_sin
    out_imag = part_imag * tw_cos - part_real * tw_sin
    return jnp.stack([out_real, out_imag], 1).astype(jnp.bfloat16)


def second_section(section_rows):
    cos_table, sin_table = trig_table(N2)
    with_cos = jnp.einsum(
        "sprnc,kn->sprkc", section_rows, cos_table, preferred_element_type=jnp.float32
    )
    with_sin = jnp.einsum(
        "sprnc,kn->sprkc", section_rows, sin_table, preferred_element_type=jnp.float32
    )
    return jnp.stack([with_cos[:, 0] + with_sin[:, 1], with_cos[:, 1] - with_sin[:, 0]], 1)


def spectral_inverse(product, row_start):
    cos_table, sin_table = trig_table(N2)
    with_cos = jnp.einsum("sprkc,nk->sprnc", product, cos_table, preferred_element_type=jnp.float32)
    with_sin = jnp.einsum("sprkc,nk->sprnc", product, sin_table, preferred_element_type=jnp.float32)
    part_real = with_cos[:, 0] - with_sin[:, 1]
    part_imag = with_cos[:, 1] + with_sin[:, 0]
    tw_cos, tw_sin = twiddle(row_start, product.shape[2], 0, N2)
    out_real = part_real * tw_cos - part_imag * tw_sin
    out_imag = part_imag * tw_cos + part_real * tw_sin
    return jnp.stack([out_real, out_imag], 1).astype(jnp.bfloat16)


def column_inverse(mixed_cols):
    cos_table, sin_table = trig_table(N1)
    with_cos = jnp.einsum(
        "nk,skmc->snmc", cos_table, mixed_cols[:, 0], preferred_element_type=jnp.float32
    )
    with_sin = jnp.einsum(
        "nk,skmc->snmc", sin_table, mixed_cols[:, 1], preferred_element_type=jnp.float32
    )
    return ((with_cos - with_sin) * (1.0 / (N1 * N2))).astype(jnp.bfloat16)


def to_spectrum(section_cols):
    return second_section(
        lax.all_to_all(section_cols, "ctx", split_axis=2, concat_axis=3, tiled=True)
    )


def error_terms(signal, filtered, skip_gain, cotangent_view):
    signal_wide = signal.astype(jnp.float32)
    filtered_wide = lax.optimization_barrier(filtered).astype(jnp.float32)
    outputs = signal_wide * filtered_wide + skip_gain * signal_wide
    clean_y = outputs[0]
    smooth_gap = outputs[1] - clean_y
    err_clean = signal_wide[0] * (cotangent_view.astype(jnp.float32) - smart_weight * smooth_gap)
    err_shift = signal_wide[1] * (smart_weight * smooth_gap)
    return (clean_y, jnp.stack([err_clean, err_shift], 0).astype(jnp.bfloat16))


def body(embeds, perturb, cotangent, filter_spectrum, skip_gain):
    ctx_size = lax.axis_size("ctx")
    ctx_index = lax.axis_index("ctx")
    channels = embeds.shape[2]
    row_count = N1 // ctx_size
    col_count = N2 // ctx_size
    row_start = ctx_index * row_count
    col_start = ctx_index * col_count
    clean_rows = embeds[0].reshape(row_count, N2, channels)
    perturb_rows = perturb[0].reshape(row_count, N2, channels)
    shifted = (clean_rows.astype(jnp.float32) + perturb_rows.astype(jnp.float32)).astype(
        jnp.bfloat16
    )
    inputs = jnp.stack([clean_rows, shifted], 0)
    signal_cols = lax.all_to_all(inputs, "ctx", split_axis=2, concat_axis=1, tiled=True)
    section_cols, signal_cols = (first_section(signal_cols, col_start), signal_cols)
    spectra = to_spectrum(section_cols)
    filter_real = filter_spectrum[0]
    filter_imag = filter_spectrum[1]
    spectrum_real = spectra[:, 0]
    spectrum_imag = spectra[:, 1]
    product = jnp.stack(
        [
            filter_real * spectrum_real - filter_imag * spectrum_imag,
            filter_real * spectrum_imag + filter_imag * spectrum_real,
        ],
        1,
    ).astype(jnp.bfloat16)
    mixed_rows = spectral_inverse(product, row_start)
    filtered = column_inverse(
        lax.all_to_all(mixed_rows, "ctx", split_axis=3, concat_axis=2, tiled=True)
    )
    cotangent_rows = cotangent[0].reshape(row_count, N2, channels)
    filtered_rows = lax.all_to_all(filtered, "ctx", split_axis=1, concat_axis=2, tiled=True)
    clean_y, errors = error_terms(inputs, filtered_rows, skip_gain, cotangent_rows)
    clean_output = clean_y.astype(jnp.bfloat16)
    error_section = first_section(
        lax.all_to_all(errors, "ctx", split_axis=2, concat_axis=1, tiled=True), col_start
    )
    error_spec = to_spectrum(error_section)
    error_real = error_spec[:, 0]
    error_imag = error_spec[:, 1]
    term_real = error_real * spectrum_real + error_imag * spectrum_imag
    term_imag = error_imag * spectrum_real - error_real * spectrum_imag
    local_grad = jnp.stack([term_real[0] + term_real[1], term_imag[0] + term_imag[1]], 0) * (
        1.0 / (N1 * N2)
    )
    grad_shard = lax.psum_scatter(
        local_grad.astype(jnp.bfloat16), "dp", scatter_dimension=2, tiled=True
    ).astype(jnp.float32)
    return (clean_output.reshape(1, row_count * N2, channels), grad_shard)


def solution(mesh):
    dp, ctx = mesh.shape["dp"], mesh.shape["ctx"]

    def run(embeds, *rest):
        apart = dp == 2 and embeds.shape[2] % (dp * ctx) == 0 and N1 // ctx == 16 and embeds.shape[2] // (dp * ctx) > 1
        return jax.shard_map(
            by_channel_body if apart else body,
            mesh=mesh,
            in_specs=(
                P("dp", "ctx", None),
                P("dp", "ctx", None),
                P("dp", "ctx", None),
                P(None, "ctx", None, None),
                P(),
            ),
            out_specs=(P("dp", "ctx", None), P(None, "ctx", "dp", None)),
            check_vma=False,
        )(embeds, *rest)

    return run
```

```python
import functools

import jax
import jax.numpy as jnp
import numpy as np
from jax import lax
from jax.experimental import pallas as pl
from jax.experimental.pallas import tpu as pltpu
from jax.sharding import PartitionSpec as P

N1 = 256
N2 = 256
BF16 = jnp.bfloat16
F32 = jnp.float32
KEPT = jnp.float32
HALF = 144
VMEM = 26 << 20

two_pi = 6.283185307179586
smart_weight = 2.0


def tables():
    ids = np.arange(N1)
    phase = (ids[:, None] * ids[None, :] % N1) * (two_pi / N1)
    cos_table, sin_table = np.cos(phase), np.sin(phase)
    split_rows = np.concatenate([cos_table[:HALF], -sin_table[:HALF]], 0)
    forward_table = np.block([[cos_table, -sin_table], [sin_table, cos_table]])
    weight = np.where(ids[: N1 // 2] == 0, 1.0, 2.0) / (N1 * N2)
    join_rows = np.concatenate([cos_table[:, : N1 // 2] * weight, -sin_table[:, : N1 // 2] * weight], 1)
    mirror_rows = np.zeros((HALF, N1))
    mirror_rows[ids[:HALF], -ids[:HALF] % N1] = 1
    mirror_cols = np.eye(N2)[::-1]
    angle = (ids[:HALF, None] * ids[None, :]) * (two_pi / (N1 * N2))
    twiddle = np.stack([np.cos(angle), np.sin(angle)], 0)
    small = (split_rows, forward_table, join_rows, mirror_rows, mirror_cols)
    small = [jnp.asarray(t.astype(jnp.bfloat16)) for t in small]
    return (*small, jnp.asarray(twiddle.astype(np.float32)))


def dot(a, b):
    return jnp.dot(a, b, preferred_element_type=F32)


def place(plane):
    c = lax.axis_index("ctx")
    return lax.axis_index("dp"), c // plane, c % plane


def near_device(here, j, hop, plane, hops):
    far = (here[0] ^ (j // plane)) * hops + (here[1] ^ hop)
    return far * plane + (here[2] ^ (j % plane))


def forward(signals, split_ref, fwd_ref, tw_cos, tw_sin):
    halves = []
    for x in signals:
        part = dot(split_ref[...], x)
        part_real, part_imag = part[:HALF], part[HALF:]
        out_real = part_real * tw_cos + part_imag * tw_sin
        out_imag = part_imag * tw_cos - part_real * tw_sin
        halves.append(jnp.concatenate([out_real.astype(BF16), out_imag.astype(BF16)], 1))
    spectra = dot(jnp.concatenate(halves, 0), fwd_ref[...])
    return [spectra[i * HALF : (i + 1) * HALF] for i in range(len(signals))]


def hermitian_part(filter_real, filter_imag, mirror_rows, mirror_cols):
    rows = dot(mirror_rows, jnp.concatenate([filter_real, filter_imag], 1)).astype(BF16)
    flipped = dot(jnp.concatenate([rows[:, :N2], rows[:, N2:]], 0), mirror_cols)
    out = []
    for part, other, sign in ((filter_real, flipped[:HALF], 0.5), (filter_imag, flipped[HALF:], -0.5)):
        top = other[:8]
        row = lax.broadcasted_iota(jnp.int32, top.shape, 0)
        top = jnp.where(row == 0, pltpu.roll(top, 1, 1), top)
        other = jnp.concatenate([top, other[8:]], 0)
        out.append(0.5 * part[:HALF].astype(F32) + sign * other)
    return out


def gradient(err_spectra, spectra):
    total_real = total_imag = 0.0
    for err_spec, spec in zip(err_spectra, spectra):
        err_real, err_imag = err_spec[:, :N2], err_spec[:, N2:]
        real, imag = spec[:, :N2], spec[:, N2:]
        total_real += err_real * real + err_imag * imag
        total_imag += err_imag * real - err_real * imag
    return total_real, total_imag


def conv_kernel(
    gain_ref, recv_ref, split_ref, fwd_ref, join_ref, mirror_ref, cols_ref, tw_ref,
    send_ref, gap_ref, spec_ref, part_ref, *held_refs,
):
    count, ctx = recv_ref.shape[:2]
    q = pl.program_id(0)

    @pl.when(q == 0)
    def _():
        for held_ref, table_ref in zip(held_refs, (split_ref, fwd_ref, tw_ref)):
            held_ref[...] = table_ref[...]

    tw_cos, tw_sin = tw_ref[0], tw_ref[1]
    signals = []
    for d in range(count):
        clean = recv_ref[d, :, 0, q].reshape(N1, N2)
        perturb = recv_ref[d, :, 1, q].reshape(N1, N2)
        signals += [clean, (clean.astype(F32) + perturb.astype(F32)).astype(BF16)]
    spectra = forward(signals, split_ref, fwd_ref, tw_cos, tw_sin)
    filter_real, filter_imag = hermitian_part(
        recv_ref[0, :, 2, q].reshape(N1, N2), recv_ref[1, :, 2, q].reshape(N1, N2), mirror_ref[...], cols_ref[...]
    )
    products = []
    for spec in spectra:
        real, imag = spec[:, :N2], spec[:, N2:]
        prod_real = (filter_real * real - filter_imag * imag).astype(BF16)
        minus_imag = (-filter_real * imag - filter_imag * real).astype(BF16)
        products.append(jnp.concatenate([prod_real, minus_imag], 1))
    back = dot(jnp.concatenate(products, 0), fwd_ref[...])
    mixed, middle = [], []
    for i in range(2 * count):
        back_real, minus_imag = back[i * HALF : (i + 1) * HALF, :N2], back[i * HALF : (i + 1) * HALF, N2:]
        mixed_real = (back_real * tw_cos + minus_imag * tw_sin).astype(BF16)
        mixed_imag = (back_real * tw_sin - minus_imag * tw_cos).astype(BF16)
        mixed.append(jnp.concatenate([mixed_real[: N1 // 2], mixed_imag[: N1 // 2]], 0))
        middle.append(mixed_real[N1 // 2 :].astype(F32)[:1])
    conv = dot(join_ref[...], jnp.concatenate(mixed, 1))
    parity = lax.broadcasted_iota(jnp.int32, (N1, N2), 0) % 2
    alternate = (1 - 2 * parity).astype(F32) * (1.0 / (N1 * N2))
    gain = gain_ref[q]
    errors = []
    for d in range(count):
        pair = []
        for i in range(2):
            k = 2 * d + i
            wide = signals[k].astype(F32)
            filtered = conv[:, k * N2 : (k + 1) * N2] + alternate * middle[k]
            pair.append((wide, wide * filtered.astype(BF16).astype(F32) + gain * wide))
        (clean, clean_y), (shifted, shifted_y) = pair
        send_ref[d, :, 0, q] = clean_y.astype(BF16).reshape(ctx, -1, N2)
        gap = smart_weight * (shifted_y - clean_y)
        gap_ref[q, d] = gap.astype(gap_ref.dtype)
        spec_ref[q, d] = spectra[2 * d].astype(spec_ref.dtype)
        errors.append((shifted * gap).astype(BF16))
    total_real, total_imag = gradient(forward(errors, split_ref, fwd_ref, tw_cos, tw_sin), spectra[1::2])
    part_ref[q, 0] = total_real
    part_ref[q, 1] = total_imag


def grad_kernel(recv_ref, gap_ref, spec_ref, part_ref, *refs, hops):
    cot_refs, refs = refs[:hops], refs[hops:]
    split_ref, fwd_ref, tw_ref, _, send_ref, cot_rows = refs
    count, ctx = recv_ref.shape[:2]
    near = cot_refs[0].shape[0]
    plane = near // count
    here = place(plane)
    per = recv_ref.shape[3]
    for hop, cot_ref in enumerate(cot_refs):
        for j in range(near):
            cot_rows[near_device(here, j, hop, plane, hops)] = cot_ref[j]
    errors = []
    for q in range(per):
        for d in range(count):
            clean = recv_ref[d, :, 0, q].reshape(N1, N2).astype(F32)
            cot = cot_rows[d * ctx : (d + 1) * ctx, q].reshape(N1, N2).astype(F32)
            errors.append((clean * (cot - gap_ref[q, d])).astype(BF16))
    err_spectra = forward(errors, split_ref, fwd_ref, tw_ref[0], tw_ref[1])
    for q in range(per):
        spectra = [spec_ref[q, d] for d in range(count)]
        total = gradient(err_spectra[q * count : (q + 1) * count], spectra)
        send_grad(send_ref, q, *[t + part_ref[q, i] for i, t in enumerate(total)])


def send_grad(send_ref, q, total_real, total_imag):
    count, ctx, _, _, rows, _ = send_ref.shape
    total = jnp.concatenate([total_real, total_imag], 1) * (1.0 / (N1 * N2))
    upper, after = total[: N1 // 2], total[rows : N1 // 2 + rows]
    first = lax.broadcasted_iota(jnp.int32, upper.shape, 0) % rows == 0
    lower = jnp.where(first, after, upper).astype(BF16)
    upper = upper.astype(BF16)
    width = N2 // count
    for i in range(count):
        for half, x, side in ((0, upper, i), (1, lower, count - 1 - i)):
            cols = slice(side * width, (side + 1) * width)
            pair = jnp.concatenate([x[:, :N2][:, cols], x[:, N2:][:, cols]], 1)
            for block in range(ctx // 2):
                target = ctx - 1 - block if half else block
                send_ref[i, target, 1, q] = pair[block * rows : (block + 1) * rows]


def whole(x):
    return pl.BlockSpec(x.shape, lambda *_: (0,) * x.ndim)


def near(x):
    return pltpu.with_memory_space_constraint(x, pltpu.VMEM)


def far(x):
    return pltpu.with_memory_space_constraint(x, pltpu.HBM)


def conv_call(gain, received, tabs):
    dp, ctx, _, per, rows, _ = received.shape
    split_rows, forward_table, *_, twiddle = tabs
    held = [pltpu.VMEM(t.shape, t.dtype) for t in (split_rows, forward_table, twiddle)]
    return pl.pallas_call(
        conv_kernel,
        grid=(per,),
        in_specs=[
            pl.BlockSpec(memory_space=pltpu.SMEM),
            pl.BlockSpec(memory_space=pltpu.VMEM),
            *[whole(t) for t in tabs],
        ],
        out_specs=[pl.BlockSpec(memory_space=pltpu.VMEM)] * 7,
        out_shape=[
            pltpu.VMEM((dp, ctx, 2, per, rows, N2), BF16),
            pltpu.VMEM((per, dp, N1, N2), KEPT),
            pltpu.VMEM((per, dp, HALF, 2 * N2), KEPT),
            pltpu.VMEM((per, 2, HALF, N2), F32),
            *held,
        ],
        compiler_params=pltpu.CompilerParams(vmem_limit_bytes=VMEM),
        cost_estimate=pl.CostEstimate(flops=per * dp * 5 * 6 * N1**3, bytes_accessed=8 << 20, transcendentals=0),
        name="conv",
    )(gain, received, *[far(t) for t in tabs])


def grad_call(received, kept, cots, send):
    dp, ctx, _, per, rows, _ = received.shape
    *kept, split_rows, forward_table, twiddle = [near(x) for x in kept]
    operands = (received, *kept, *[near(x) for x in cots], split_rows, forward_table, twiddle, near(send))
    return pl.pallas_call(
        functools.partial(grad_kernel, hops=len(cots)),
        grid=(1,),
        in_specs=[pl.BlockSpec(memory_space=pltpu.VMEM)] * len(operands),
        out_specs=pl.BlockSpec(memory_space=pltpu.VMEM),
        out_shape=pltpu.VMEM(send.shape, BF16),
        scratch_shapes=[pltpu.VMEM((dp * ctx, per, rows, N2), BF16)],
        input_output_aliases={len(operands) - 1: 0},
        compiler_params=pltpu.CompilerParams(vmem_limit_bytes=VMEM),
        cost_estimate=pl.CostEstimate(flops=per * dp * 6 * N1**3, bytes_accessed=8 << 20, transcendentals=0),
        name="grad",
    )(*operands)


def outward_kernel(*refs, count):
    in_refs, refs = refs[:count], refs[count:]
    out_ref, refs = refs[0], refs[1:]
    held_refs, (rows_ref, ready_ref, load_sems, store_sems) = refs[:count], refs[count:]
    devices, _, per, rows, _ = out_ref.shape
    pitch = rows_ref.shape[1] // (devices * per)
    width = rows_ref.shape[2]
    loads, stores = [], []
    for t, (in_ref, held_ref) in enumerate(zip(in_refs, held_refs)):
        source = in_ref.at[lax.axis_index("dp") if in_ref.shape[0] > 1 else 0]
        loads.append(pltpu.make_async_copy(source, held_ref, load_sems.at[t]))
        loads[t].start()
    for t, held_ref in enumerate(held_refs):
        loads[t].wait()
        for h in range(N2 // width):
            lanes = slice(h * width, (h + 1) * width)
            for r in range(rows):
                block = held_ref[r, lanes].astype(BF16).T.astype(F32)
                rows_ref[h, pl.ds(r, devices * per, stride=pitch), :] = block
            block = rows_ref[h].reshape(devices, per, pitch, width)[:, :, :rows].astype(BF16)
            ready_ref[t, :, :, :, lanes] = block
        stores.append(pltpu.make_async_copy(ready_ref.at[t], out_ref.at[:, t], store_sems.at[t]))
        stores[t].start()
    for store in stores:
        store.wait()


def outward(arrays, devices):
    _, rows, _, channels = arrays[0].shape
    count, per, width, pitch = len(arrays), channels // devices, 128, rows + 8
    shape = (devices, count, per, rows, N2)
    return pl.pallas_call(
        functools.partial(outward_kernel, count=count),
        in_specs=[pl.BlockSpec(memory_space=pl.ANY)] * count,
        out_specs=pl.BlockSpec(memory_space=pl.ANY),
        out_shape=pltpu.HBM(shape, BF16),
        scratch_shapes=[
            *[pltpu.VMEM(a.shape[1:], a.dtype) for a in arrays],
            pltpu.VMEM((N2 // width, channels * pitch, width), F32),
            pltpu.VMEM((count, devices, per, rows, N2), BF16),
            pltpu.SemaphoreType.DMA((count,)),
            pltpu.SemaphoreType.DMA((count,)),
        ],
        compiler_params=pltpu.CompilerParams(vmem_limit_bytes=VMEM),
        cost_estimate=pl.CostEstimate(flops=0, bytes_accessed=7 << 20, transcendentals=0),
        name="outward",
    )(*arrays)


def outward_near_kernel(in_ref, *refs, hops, plane):
    here = place(plane)
    *out_refs, rows_ref = refs
    _, per, rows, width = out_refs[0].shape
    channels = in_ref.shape[3]
    pitch = rows_ref.shape[0] // channels
    for r in range(rows):
        rows_ref[pl.ds(r, channels, stride=pitch), :] = in_ref[0, r].T.astype(F32)
    for j, out_ref in enumerate(out_refs):
        for hop in range(hops):
            block = near_device(here, j, hop, plane, hops) * (per * pitch)
            rows_here = rows_ref[pl.ds(pl.multiple_of(block, per * pitch), per * pitch), :]
            out_ref[hop] = rows_here.reshape(per, pitch, width)[:, :rows].astype(BF16)


def outward_near(x, count, hops, plane):
    _, rows, _, channels = x.shape
    per = channels // count
    width = 128
    return pl.pallas_call(
        functools.partial(outward_near_kernel, hops=hops, plane=plane),
        grid=(N2 // width,),
        in_specs=[pl.BlockSpec((1, rows, width, channels), lambda h: (0, 0, h, 0))],
        out_specs=[pl.BlockSpec((hops, per, rows, width), lambda h: (0, 0, 0, h))] * (count // hops),
        out_shape=[jax.ShapeDtypeStruct((hops, per, rows, N2), BF16)] * (count // hops),
        scratch_shapes=[pltpu.VMEM((channels * (rows + 8), width), F32)],
        compiler_params=pltpu.CompilerParams(vmem_limit_bytes=VMEM),
        cost_estimate=pl.CostEstimate(flops=0, bytes_accessed=2 << 20, transcendentals=0),
        name="outward_near",
    )(x)


def regroup_kernel(*refs, count):
    for i, in_ref in enumerate(refs[:count]):
        for j, out_ref in enumerate(refs[count:]):
            out_ref[i] = in_ref[j]


def regroup(arrays):
    hops, *block = arrays[0].shape
    return pl.pallas_call(
        functools.partial(regroup_kernel, count=len(arrays)),
        out_shape=[jax.ShapeDtypeStruct((len(arrays), *block), BF16)] * hops,
        compiler_params=pltpu.CompilerParams(vmem_limit_bytes=VMEM),
        cost_estimate=pl.CostEstimate(flops=0, bytes_accessed=2 << 20, transcendentals=0),
        name="regroup",
    )(*arrays)


def homeward_kernel(last_ref, y_ref, grad_ref, rows_ref):
    count, _, per, rows, _ = last_ref.shape
    width = rows_ref.shape[2]
    pitch = rows_ref.shape[1] // (count * per)
    h = pl.program_id(0)
    lanes = pl.ds(pl.multiple_of(h * width, width), width)
    lower = lax.axis_index("ctx") >= lax.axis_size("ctx") // 2
    row = lax.broadcasted_iota(jnp.int32, (width, width), 0)
    col = lax.broadcasted_iota(jnp.int32, (width, width), 1)
    turn = (col == jnp.where(lower, width - 1 - row, row)).astype(F32)
    turn = (turn * jnp.where(lower, (1 - 2 * h).astype(F32), 1.0)).astype(BF16)
    for t in range(2):
        block = last_ref[:, t, :, :, lanes]
        if t:
            block = dot(block.reshape(count * per * rows, width), turn).reshape(block.shape)
        rows_ref.at[t].reshape(count, per, pitch, width)[:, :, :rows] = block.astype(F32)
    for r in range(rows):
        y_ref[r] = rows_ref[0, pl.ds(r, count * per, stride=pitch), :].astype(BF16).T
    for r in range(rows):
        target = jnp.where(lower, (rows - r) % rows, r)
        grad_ref[0, target] = rows_ref[1, pl.ds(r, count * per, stride=pitch), :].T


def homeward(last):
    count, _, per, rows, _ = last.shape
    channels, width, pitch = count * per, 128, rows + 8
    return pl.pallas_call(
        homeward_kernel,
        grid=(N2 // width,),
        in_specs=[pl.BlockSpec(memory_space=pltpu.VMEM)],
        out_specs=[
            pl.BlockSpec((rows, width, channels), lambda h: (0, h, 0)),
            pl.BlockSpec((1, rows, width, channels), lambda h: (h, 0, 0, 0)),
        ],
        out_shape=[
            jax.ShapeDtypeStruct((rows, N2, channels), BF16),
            jax.ShapeDtypeStruct((2, rows, width, channels), F32),
        ],
        scratch_shapes=[pltpu.VMEM((2, channels * pitch, width), F32)],
        compiler_params=pltpu.CompilerParams(vmem_limit_bytes=VMEM),
        cost_estimate=pl.CostEstimate(flops=0, bytes_accessed=5 << 20, transcendentals=0),
        name="homeward",
    )(near(last))


def by_channel_body(embeds, perturb, cotangent, filter_spectrum, skip_gain):
    dp, ctx = lax.axis_size("dp"), lax.axis_size("ctx")
    d, c = lax.axis_index("dp"), lax.axis_index("ctx")
    axes = ("dp", "ctx")
    count = dp * ctx
    channels = embeds.shape[2]
    rows = N1 // ctx
    per = channels // count
    plane = 4
    hops = ctx // plane
    tabs = tables()

    def matrix(x):
        return far(x.reshape(1, rows, N2, channels))

    def exchange(x, mask):
        return lax.ppermute(x, axes, [(i, i ^ mask) for i in range(count)]) if mask else x

    first = outward([matrix(embeds), matrix(perturb), far(filter_spectrum)], count)
    received = lax.all_to_all(first, axes, 0, 0, tiled=True).reshape(dp, ctx, 3, per, rows, N2)
    cots = outward_near(matrix(cotangent), count, hops, plane)
    cots = regroup([exchange(x, j // plane * ctx + j % plane) for j, x in enumerate(cots)])
    received = near(received)
    *early, late = cots
    late, received = lax.optimization_barrier((late, received))
    cots = [exchange(x, hop * plane) for hop, x in enumerate([*early, late])]
    gain = lax.dynamic_slice(skip_gain, ((d * ctx + c) * per,), (per,))
    send, *kept = conv_call(gain, received, tabs)
    send = grad_call(received, kept, cots, send)
    last = lax.all_to_all(send.reshape(count, 2, per, rows, N2), axes, 0, 0, tiled=True)
    y, grad = homeward(last)
    return y.reshape(1, rows * N2, channels), grad


def trig_table(period):
    row_ids = jnp.arange(period, dtype=jnp.int32)
    exponent = row_ids[:, None] * row_ids[None, :] % period
    phase_angle = exponent.astype(jnp.float32) * (two_pi / period)
    return (jnp.cos(phase_angle).astype(jnp.bfloat16), jnp.sin(phase_angle).astype(jnp.bfloat16))


def twiddle(row_first, row_count, col_first, col_count):
    row_ids = row_first + jnp.arange(row_count, dtype=jnp.int32)
    col_ids = col_first + jnp.arange(col_count, dtype=jnp.int32)
    exponent = row_ids[:, None] * col_ids[None, :] % (N1 * N2)
    phase_angle = exponent.astype(jnp.float32) * (two_pi / (N1 * N2))
    return (jnp.cos(phase_angle)[:, :, None], jnp.sin(phase_angle)[:, :, None])


def first_section(values, col_start):
    cos_table, sin_table = trig_table(N1)
    part_real = jnp.einsum("kn,snmc->skmc", cos_table, values, preferred_element_type=jnp.float32)
    part_imag = -jnp.einsum("kn,snmc->skmc", sin_table, values, preferred_element_type=jnp.float32)
    tw_cos, tw_sin = twiddle(0, N1, col_start, values.shape[2])
    out_real = part_real * tw_cos + part_imag * tw_sin
    out_imag = part_imag * tw_cos - part_real * tw_sin
    return jnp.stack([out_real, out_imag], 1).astype(jnp.bfloat16)


def second_section(section_rows):
    cos_table, sin_table = trig_table(N2)
    with_cos = jnp.einsum(
        "sprnc,kn->sprkc", section_rows, cos_table, preferred_element_type=jnp.float32
    )
    with_sin = jnp.einsum(
        "sprnc,kn->sprkc", section_rows, sin_table, preferred_element_type=jnp.float32
    )
    return jnp.stack([with_cos[:, 0] + with_sin[:, 1], with_cos[:, 1] - with_sin[:, 0]], 1)


def spectral_inverse(product, row_start):
    cos_table, sin_table = trig_table(N2)
    with_cos = jnp.einsum("sprkc,nk->sprnc", product, cos_table, preferred_element_type=jnp.float32)
    with_sin = jnp.einsum("sprkc,nk->sprnc", product, sin_table, preferred_element_type=jnp.float32)
    part_real = with_cos[:, 0] - with_sin[:, 1]
    part_imag = with_cos[:, 1] + with_sin[:, 0]
    tw_cos, tw_sin = twiddle(row_start, product.shape[2], 0, N2)
    out_real = part_real * tw_cos - part_imag * tw_sin
    out_imag = part_imag * tw_cos + part_real * tw_sin
    return jnp.stack([out_real, out_imag], 1).astype(jnp.bfloat16)


def column_inverse(mixed_cols):
    cos_table, sin_table = trig_table(N1)
    with_cos = jnp.einsum(
        "nk,skmc->snmc", cos_table, mixed_cols[:, 0], preferred_element_type=jnp.float32
    )
    with_sin = jnp.einsum(
        "nk,skmc->snmc", sin_table, mixed_cols[:, 1], preferred_element_type=jnp.float32
    )
    return ((with_cos - with_sin) * (1.0 / (N1 * N2))).astype(jnp.bfloat16)


def to_spectrum(section_cols):
    return second_section(
        lax.all_to_all(section_cols, "ctx", split_axis=2, concat_axis=3, tiled=True)
    )


def error_terms(signal, filtered, skip_gain, cotangent_view):
    signal_wide = signal.astype(jnp.float32)
    filtered_wide = lax.optimization_barrier(filtered).astype(jnp.float32)
    outputs = signal_wide * filtered_wide + skip_gain * signal_wide
    clean_y = outputs[0]
    smooth_gap = outputs[1] - clean_y
    err_clean = signal_wide[0] * (cotangent_view.astype(jnp.float32) - smart_weight * smooth_gap)
    err_shift = signal_wide[1] * (smart_weight * smooth_gap)
    return (clean_y, jnp.stack([err_clean, err_shift], 0).astype(jnp.bfloat16))


def body(embeds, perturb, cotangent, filter_spectrum, skip_gain):
    ctx_size = lax.axis_size("ctx")
    ctx_index = lax.axis_index("ctx")
    channels = embeds.shape[2]
    row_count = N1 // ctx_size
    col_count = N2 // ctx_size
    row_start = ctx_index * row_count
    col_start = ctx_index * col_count
    clean_rows = embeds[0].reshape(row_count, N2, channels)
    perturb_rows = perturb[0].reshape(row_count, N2, channels)
    shifted = (clean_rows.astype(jnp.float32) + perturb_rows.astype(jnp.float32)).astype(
        jnp.bfloat16
    )
    inputs = jnp.stack([clean_rows, shifted], 0)
    signal_cols = lax.all_to_all(inputs, "ctx", split_axis=2, concat_axis=1, tiled=True)
    section_cols, signal_cols = (first_section(signal_cols, col_start), signal_cols)
    spectra = to_spectrum(section_cols)
    filter_real = filter_spectrum[0]
    filter_imag = filter_spectrum[1]
    spectrum_real = spectra[:, 0]
    spectrum_imag = spectra[:, 1]
    product = jnp.stack(
        [
            filter_real * spectrum_real - filter_imag * spectrum_imag,
            filter_real * spectrum_imag + filter_imag * spectrum_real,
        ],
        1,
    ).astype(jnp.bfloat16)
    mixed_rows = spectral_inverse(product, row_start)
    filtered = column_inverse(
        lax.all_to_all(mixed_rows, "ctx", split_axis=3, concat_axis=2, tiled=True)
    )
    cotangent_rows = cotangent[0].reshape(row_count, N2, channels)
    filtered_rows = lax.all_to_all(filtered, "ctx", split_axis=1, concat_axis=2, tiled=True)
    clean_y, errors = error_terms(inputs, filtered_rows, skip_gain, cotangent_rows)
    clean_output = clean_y.astype(jnp.bfloat16)
    error_section = first_section(
        lax.all_to_all(errors, "ctx", split_axis=2, concat_axis=1, tiled=True), col_start
    )
    error_spec = to_spectrum(error_section)
    error_real = error_spec[:, 0]
    error_imag = error_spec[:, 1]
    term_real = error_real * spectrum_real + error_imag * spectrum_imag
    term_imag = error_imag * spectrum_real - error_real * spectrum_imag
    local_grad = jnp.stack([term_real[0] + term_real[1], term_imag[0] + term_imag[1]], 0) * (
        1.0 / (N1 * N2)
    )
    grad_shard = lax.psum_scatter(
        local_grad.astype(jnp.bfloat16), "dp", scatter_dimension=2, tiled=True
    ).astype(jnp.float32)
    return (clean_output.reshape(1, row_count * N2, channels), grad_shard)


def solution(mesh):
    dp, ctx = mesh.shape["dp"], mesh.shape["ctx"]

    def run(embeds, *rest):
        apart = dp == 2 and embeds.shape[2] % (dp * ctx) == 0 and N1 // ctx == 16 and embeds.shape[2] // (dp * ctx) > 1
        return jax.shard_map(
            by_channel_body if apart else body,
            mesh=mesh,
            in_specs=(
                P("dp", "ctx", None),
                P("dp", "ctx", None),
                P("dp", "ctx", None),
                P(None, "ctx", None, None),
                P(),
            ),
            out_specs=(P("dp", "ctx", None), P(None, "ctx", "dp", None)),
            check_vma=False,
        )(embeds, *rest)

    return run
```

```python
import functools

import jax
import jax.numpy as jnp
import numpy as np
from jax import lax
from jax.experimental import pallas as pl
from jax.experimental.pallas import tpu as pltpu
from jax.sharding import PartitionSpec as P

N1 = 256
N2 = 256
BF16 = jnp.bfloat16
F32 = jnp.float32
EARLY = 2
KEPT = jnp.float32
HALF = 144
VMEM = 26 << 20

two_pi = 6.283185307179586
smart_weight = 2.0


def tables():
    ids = np.arange(N1)
    phase = (ids[:, None] * ids[None, :] % N1) * (two_pi / N1)
    cos_table, sin_table = np.cos(phase), np.sin(phase)
    split_rows = np.concatenate([cos_table[:HALF], -sin_table[:HALF]], 0)
    forward_table = np.block([[cos_table, -sin_table], [sin_table, cos_table]])
    weight = np.where(ids[: N1 // 2] == 0, 1.0, 2.0) / (N1 * N2)
    join_rows = np.concatenate([cos_table[:, : N1 // 2] * weight, -sin_table[:, : N1 // 2] * weight], 1)
    mirror_rows = np.zeros((HALF, N1))
    mirror_rows[ids[:HALF], -ids[:HALF] % N1] = 1
    mirror_cols = np.eye(N2)[::-1]
    angle = (ids[:HALF, None] * ids[None, :]) * (two_pi / (N1 * N2))
    twiddle = np.stack([np.cos(angle), np.sin(angle)], 0)
    small = (split_rows, forward_table, join_rows, mirror_rows, mirror_cols)
    small = [jnp.asarray(t.astype(jnp.bfloat16)) for t in small]
    return (*small, jnp.asarray(twiddle.astype(np.float32)))


def dot(a, b):
    return jnp.dot(a, b, preferred_element_type=F32)


def place(plane):
    c = lax.axis_index("ctx")
    return lax.axis_index("dp"), c // plane, c % plane


def near_device(here, j, hop, plane, hops):
    far = (here[0] ^ (j // plane)) * hops + (here[1] ^ hop)
    return far * plane + (here[2] ^ (j % plane))


def forward(signals, split_ref, fwd_ref, tw_cos, tw_sin):
    halves = []
    for x in signals:
        part = dot(split_ref[...], x)
        part_real, part_imag = part[:HALF], part[HALF:]
        out_real = part_real * tw_cos + part_imag * tw_sin
        out_imag = part_imag * tw_cos - part_real * tw_sin
        halves.append(jnp.concatenate([out_real.astype(BF16), out_imag.astype(BF16)], 1))
    spectra = dot(jnp.concatenate(halves, 0), fwd_ref[...])
    return [spectra[i * HALF : (i + 1) * HALF] for i in range(len(signals))]


def hermitian_part(filter_real, filter_imag, mirror_rows, mirror_cols):
    rows = dot(mirror_rows, jnp.concatenate([filter_real, filter_imag], 1)).astype(BF16)
    flipped = dot(jnp.concatenate([rows[:, :N2], rows[:, N2:]], 0), mirror_cols)
    out = []
    for part, other, sign in ((filter_real, flipped[:HALF], 0.5), (filter_imag, flipped[HALF:], -0.5)):
        top = other[:8]
        row = lax.broadcasted_iota(jnp.int32, top.shape, 0)
        top = jnp.where(row == 0, pltpu.roll(top, 1, 1), top)
        other = jnp.concatenate([top, other[8:]], 0)
        out.append(0.5 * part[:HALF].astype(F32) + sign * other)
    return out


def gradient(err_spectra, spectra):
    total_real = total_imag = 0.0
    for err_spec, spec in zip(err_spectra, spectra):
        err_real, err_imag = err_spec[:, :N2], err_spec[:, N2:]
        real, imag = spec[:, :N2], spec[:, N2:]
        total_real += err_real * real + err_imag * imag
        total_imag += err_imag * real - err_real * imag
    return total_real, total_imag


def conv_kernel(
    gain_ref, recv_ref, split_ref, fwd_ref, join_ref, mirror_ref, cols_ref, tw_ref,
    send_ref, gap_ref, spec_ref, part_ref, *refs,
):
    *refs, y_rows = refs
    held_refs, early_refs = refs[:3], refs[3:]
    count, ctx = recv_ref.shape[:2]
    hops, near_count = len(early_refs), early_refs[0].shape[0]
    here = place(near_count // count)
    q = pl.program_id(0)

    @pl.when(q == 0)
    def _():
        for held_ref, table_ref in zip(held_refs, (split_ref, fwd_ref, tw_ref)):
            held_ref[...] = table_ref[...]

    tw_cos, tw_sin = tw_ref[0], tw_ref[1]
    signals = []
    for d in range(count):
        clean = recv_ref[d, :, 0, q].reshape(N1, N2)
        perturb = recv_ref[d, :, 1, q].reshape(N1, N2)
        signals += [clean, (clean.astype(F32) + perturb.astype(F32)).astype(BF16)]
    spectra = forward(signals, split_ref, fwd_ref, tw_cos, tw_sin)
    filter_real, filter_imag = hermitian_part(
        recv_ref[0, :, 2, q].reshape(N1, N2), recv_ref[1, :, 2, q].reshape(N1, N2), mirror_ref[...], cols_ref[...]
    )
    products = []
    for spec in spectra:
        real, imag = spec[:, :N2], spec[:, N2:]
        prod_real = (filter_real * real - filter_imag * imag).astype(BF16)
        minus_imag = (-filter_real * imag - filter_imag * real).astype(BF16)
        products.append(jnp.concatenate([prod_real, minus_imag], 1))
    back = dot(jnp.concatenate(products, 0), fwd_ref[...])
    mixed, middle = [], []
    for i in range(2 * count):
        back_real, minus_imag = back[i * HALF : (i + 1) * HALF, :N2], back[i * HALF : (i + 1) * HALF, N2:]
        mixed_real = (back_real * tw_cos + minus_imag * tw_sin).astype(BF16)
        mixed_imag = (back_real * tw_sin - minus_imag * tw_cos).astype(BF16)
        mixed.append(jnp.concatenate([mixed_real[: N1 // 2], mixed_imag[: N1 // 2]], 0))
        middle.append(mixed_real[N1 // 2 :].astype(F32)[:1])
    conv = dot(join_ref[...], jnp.concatenate(mixed, 1))
    parity = lax.broadcasted_iota(jnp.int32, (N1, N2), 0) % 2
    alternate = (1 - 2 * parity).astype(F32) * (1.0 / (N1 * N2))
    gain = gain_ref[q]
    errors = []
    for d in range(count):
        pair = []
        for i in range(2):
            k = 2 * d + i
            wide = signals[k].astype(F32)
            filtered = conv[:, k * N2 : (k + 1) * N2] + alternate * middle[k]
            pair.append((wide, wide * filtered.astype(BF16).astype(F32) + gain * wide))
        (clean, clean_y), (shifted, shifted_y) = pair
        y_rows[d * ctx : (d + 1) * ctx] = clean_y.astype(BF16).reshape(ctx, -1, N2)
        gap = smart_weight * (shifted_y - clean_y)
        gap_ref[q, d] = gap.astype(gap_ref.dtype)
        spec_ref[q, d] = spectra[2 * d].astype(spec_ref.dtype)
        errors.append((shifted * gap).astype(BF16))
    total_real, total_imag = gradient(forward(errors, split_ref, fwd_ref, tw_cos, tw_sin), spectra[1::2])
    part_ref[q, 0] = total_real
    part_ref[q, 1] = total_imag

    @pl.when(q < EARLY)
    def _():
        for hop, early_ref in enumerate(early_refs):
            for j in range(near_count):
                early_ref[j, q] = y_rows[near_device(here, j, hop, near_count // count, hops)]

    @pl.when(q >= EARLY)
    def _():
        for d in range(count):
            send_ref[d, :, q - EARLY] = y_rows[d * ctx : (d + 1) * ctx]


def grad_kernel(recv_ref, gap_ref, spec_ref, part_ref, *refs, hops):
    cot_refs, refs = refs[:hops], refs[hops:]
    split_ref, fwd_ref, tw_ref, y_ref, send_ref, cot_rows, ready_ref, sems = refs
    copies = [pltpu.make_async_copy(y_ref, send_ref.at[:, :, pl.ds(0, y_ref.shape[2])], sems.at[0])]
    copies[0].start()
    count, ctx = recv_ref.shape[:2]
    near = cot_refs[0].shape[0]
    plane = near // count
    here = place(plane)
    per = recv_ref.shape[3]
    for hop, cot_ref in enumerate(cot_refs):
        for j in range(near):
            cot_rows[near_device(here, j, hop, plane, hops)] = cot_ref[j]
    errors = []
    for q in range(per):
        for d in range(count):
            clean = recv_ref[d, :, 0, q].reshape(N1, N2).astype(F32)
            cot = cot_rows[d * ctx : (d + 1) * ctx, q].reshape(N1, N2).astype(F32)
            errors.append((clean * (cot - gap_ref[q, d])).astype(BF16))
    err_spectra = forward(errors, split_ref, fwd_ref, tw_ref[0], tw_ref[1])
    for q in range(per):
        spectra = [spec_ref[q, d] for d in range(count)]
        total = gradient(err_spectra[q * count : (q + 1) * count], spectra)
        fill_grad(ready_ref, q, *[t + part_ref[q, i] for i, t in enumerate(total)])
        copies.append(pltpu.make_async_copy(ready_ref.at[q], send_ref.at[:, :, per - EARLY + q], sems.at[1 + q]))
        copies[1 + q].start()
    for copy in copies:
        copy.wait()


def fill_grad(ready_ref, q, total_real, total_imag):
    _, count, ctx, rows, _ = ready_ref.shape
    total = jnp.concatenate([total_real, total_imag], 1) * (1.0 / (N1 * N2))
    upper, after = total[: N1 // 2], total[rows : N1 // 2 + rows]
    first = lax.broadcasted_iota(jnp.int32, upper.shape, 0) % rows == 0
    lower = jnp.where(first, after, upper).astype(BF16)
    upper = upper.astype(BF16)
    width = N2 // count
    for i in range(count):
        for half, x, side in ((0, upper, i), (1, lower, count - 1 - i)):
            cols = slice(side * width, (side + 1) * width)
            pair = jnp.concatenate([x[:, :N2][:, cols], x[:, N2:][:, cols]], 1)
            for block in range(ctx // 2):
                target = ctx - 1 - block if half else block
                ready_ref[q, i, target] = pair[block * rows : (block + 1) * rows]


def whole(x):
    return pl.BlockSpec(x.shape, lambda *_: (0,) * x.ndim)


def near(x):
    return pltpu.with_memory_space_constraint(x, pltpu.VMEM)


def far(x):
    return pltpu.with_memory_space_constraint(x, pltpu.HBM)


def conv_call(gain, received, tabs, plane):
    dp, ctx, _, per, rows, _ = received.shape
    split_rows, forward_table, *_, twiddle = tabs
    early = (dp * plane, EARLY, rows, N2)
    held = [pltpu.VMEM(t.shape, t.dtype) for t in (split_rows, forward_table, twiddle)]
    return pl.pallas_call(
        conv_kernel,
        grid=(per,),
        in_specs=[
            pl.BlockSpec(memory_space=pltpu.SMEM),
            pl.BlockSpec(memory_space=pltpu.VMEM),
            *[whole(t) for t in tabs],
        ],
        out_specs=[
            *[pl.BlockSpec(memory_space=pltpu.VMEM)] * (7 + ctx // plane),
        ],
        out_shape=[
            pltpu.VMEM((dp, ctx, per - EARLY, rows, N2), BF16),
            pltpu.VMEM((per, dp, N1, N2), KEPT),
            pltpu.VMEM((per, dp, HALF, 2 * N2), KEPT),
            pltpu.VMEM((per, 2, HALF, N2), F32),
            *held,
            *[pltpu.VMEM(early, BF16)] * (ctx // plane),
        ],
        scratch_shapes=[pltpu.VMEM((dp * ctx, rows, N2), BF16)],
        compiler_params=pltpu.CompilerParams(vmem_limit_bytes=VMEM),
        cost_estimate=pl.CostEstimate(flops=per * dp * 5 * 6 * N1**3, bytes_accessed=8 << 20, transcendentals=0),
        name="conv",
    )(gain, received, *[far(t) for t in tabs])


def grad_call(received, kept, cots, send):
    dp, ctx, _, per, rows, _ = received.shape
    *kept, split_rows, forward_table, twiddle = [near(x) for x in kept]
    operands = (received, *kept, *[near(x) for x in cots], split_rows, forward_table, twiddle, near(send))
    return pl.pallas_call(
        functools.partial(grad_kernel, hops=len(cots)),
        grid=(1,),
        in_specs=[pl.BlockSpec(memory_space=pltpu.VMEM)] * len(operands),
        out_specs=pl.BlockSpec(memory_space=pl.ANY),
        out_shape=pltpu.HBM((dp, ctx, 2 * per - EARLY, rows, N2), BF16),
        scratch_shapes=[
            pltpu.VMEM((dp * ctx, per, rows, N2), BF16),
            pltpu.VMEM((per, dp, ctx, rows, N2), BF16),
            pltpu.SemaphoreType.DMA((1 + per,)),
        ],
        compiler_params=pltpu.CompilerParams(vmem_limit_bytes=VMEM),
        cost_estimate=pl.CostEstimate(flops=per * dp * 6 * N1**3, bytes_accessed=8 << 20, transcendentals=0),
        name="grad",
    )(*operands)


def outward_kernel(*refs, count):
    in_refs, refs = refs[:count], refs[count:]
    out_ref, refs = refs[0], refs[1:]
    held_refs, (rows_ref, ready_ref, load_sems, store_sems) = refs[:count], refs[count:]
    devices, _, per, rows, _ = out_ref.shape
    pitch = rows_ref.shape[1] // (devices * per)
    width = rows_ref.shape[2]
    loads, stores = [], []
    for t, (in_ref, held_ref) in enumerate(zip(in_refs, held_refs)):
        source = in_ref.at[lax.axis_index("dp") if in_ref.shape[0] > 1 else 0]
        loads.append(pltpu.make_async_copy(source, held_ref, load_sems.at[t]))
        loads[t].start()
    for t, held_ref in enumerate(held_refs):
        loads[t].wait()
        for h in range(N2 // width):
            lanes = slice(h * width, (h + 1) * width)
            for r in range(rows):
                block = held_ref[r, lanes].astype(BF16).T.astype(F32)
                rows_ref[h, pl.ds(r, devices * per, stride=pitch), :] = block
            block = rows_ref[h].reshape(devices, per, pitch, width)[:, :, :rows].astype(BF16)
            ready_ref[t, :, :, :, lanes] = block
        stores.append(pltpu.make_async_copy(ready_ref.at[t], out_ref.at[:, t], store_sems.at[t]))
        stores[t].start()
    for store in stores:
        store.wait()


def outward(arrays, devices):
    _, rows, _, channels = arrays[0].shape
    count, per, width, pitch = len(arrays), channels // devices, 128, rows + 8
    shape = (devices, count, per, rows, N2)
    return pl.pallas_call(
        functools.partial(outward_kernel, count=count),
        in_specs=[pl.BlockSpec(memory_space=pl.ANY)] * count,
        out_specs=pl.BlockSpec(memory_space=pl.ANY),
        out_shape=pltpu.HBM(shape, BF16),
        scratch_shapes=[
            *[pltpu.VMEM(a.shape[1:], a.dtype) for a in arrays],
            pltpu.VMEM((N2 // width, channels * pitch, width), F32),
            pltpu.VMEM((count, devices, per, rows, N2), BF16),
            pltpu.SemaphoreType.DMA((count,)),
            pltpu.SemaphoreType.DMA((count,)),
        ],
        compiler_params=pltpu.CompilerParams(vmem_limit_bytes=VMEM),
        cost_estimate=pl.CostEstimate(flops=0, bytes_accessed=7 << 20, transcendentals=0),
        name="outward",
    )(*arrays)


def outward_near_kernel(in_ref, *refs, hops, plane):
    here = place(plane)
    *out_refs, rows_ref = refs
    _, per, rows, width = out_refs[0].shape
    channels = in_ref.shape[3]
    pitch = rows_ref.shape[0] // channels
    for r in range(rows):
        rows_ref[pl.ds(r, channels, stride=pitch), :] = in_ref[0, r].T.astype(F32)
    for j, out_ref in enumerate(out_refs):
        for hop in range(hops):
            block = near_device(here, j, hop, plane, hops) * (per * pitch)
            rows_here = rows_ref[pl.ds(pl.multiple_of(block, per * pitch), per * pitch), :]
            out_ref[hop] = rows_here.reshape(per, pitch, width)[:, :rows].astype(BF16)


def outward_near(x, count, hops, plane):
    _, rows, _, channels = x.shape
    per = channels // count
    width = 128
    return pl.pallas_call(
        functools.partial(outward_near_kernel, hops=hops, plane=plane),
        grid=(N2 // width,),
        in_specs=[pl.BlockSpec((1, rows, width, channels), lambda h: (0, 0, h, 0))],
        out_specs=[pl.BlockSpec((hops, per, rows, width), lambda h: (0, 0, 0, h))] * (count // hops),
        out_shape=[jax.ShapeDtypeStruct((hops, per, rows, N2), BF16)] * (count // hops),
        scratch_shapes=[pltpu.VMEM((channels * (rows + 8), width), F32)],
        compiler_params=pltpu.CompilerParams(vmem_limit_bytes=VMEM),
        cost_estimate=pl.CostEstimate(flops=0, bytes_accessed=2 << 20, transcendentals=0),
        name="outward_near",
    )(x)


def regroup_kernel(*refs, count):
    for i, in_ref in enumerate(refs[:count]):
        for j, out_ref in enumerate(refs[count:]):
            out_ref[i] = in_ref[j]


def regroup(arrays):
    hops, *block = arrays[0].shape
    return pl.pallas_call(
        functools.partial(regroup_kernel, count=len(arrays)),
        out_shape=[jax.ShapeDtypeStruct((len(arrays), *block), BF16)] * hops,
        compiler_params=pltpu.CompilerParams(vmem_limit_bytes=VMEM),
        cost_estimate=pl.CostEstimate(flops=0, bytes_accessed=2 << 20, transcendentals=0),
        name="regroup",
    )(*arrays)


def homeward_kernel(last_ref, *refs, per):
    *early_refs, y_ref, grad_ref, rows_ref = refs
    count, _, rows, _ = last_ref.shape
    hops = early_refs[0].shape[0]
    plane = count // hops // 2
    here = place(plane)
    width = rows_ref.shape[2]
    pitch = rows_ref.shape[1] // (count * per)
    h = pl.program_id(0)
    lanes = pl.ds(pl.multiple_of(h * width, width), width)
    lower = lax.axis_index("ctx") >= lax.axis_size("ctx") // 2
    row = lax.broadcasted_iota(jnp.int32, (width, width), 0)
    col = lax.broadcasted_iota(jnp.int32, (width, width), 1)
    turn = (col == jnp.where(lower, width - 1 - row, row)).astype(F32)
    turn = (turn * jnp.where(lower, (1 - 2 * h).astype(F32), 1.0)).astype(BF16)
    y_rows = rows_ref.at[0].reshape(count, per, pitch, width)
    grad_rows = rows_ref.at[1].reshape(count, per, pitch, width)
    for j, early_ref in enumerate(early_refs):
        for hop in range(hops):
            y_rows[near_device(here, j, hop, plane, hops), :EARLY, :rows] = early_ref[hop, :, :, lanes].astype(F32)
    y_rows[:, EARLY:, :rows] = last_ref[:, : per - EARLY, :, lanes].astype(F32)
    block = last_ref[:, per - EARLY :, :, lanes]
    grad_rows[:, :, :rows] = dot(block.reshape(count * per * rows, width), turn).reshape(block.shape)
    for r in range(rows):
        y_ref[r] = rows_ref[0, pl.ds(r, count * per, stride=pitch), :].astype(BF16).T
    for r in range(rows):
        target = jnp.where(lower, (rows - r) % rows, r)
        grad_ref[0, target] = rows_ref[1, pl.ds(r, count * per, stride=pitch), :].T


def homeward(last, early):
    count, slots, rows, _ = last.shape
    per = (slots + EARLY) // 2
    channels, width, pitch = count * per, 128, rows + 8
    return pl.pallas_call(
        functools.partial(homeward_kernel, per=per),
        grid=(N2 // width,),
        in_specs=[pl.BlockSpec(memory_space=pltpu.VMEM)] * (1 + len(early)),
        out_specs=[
            pl.BlockSpec((rows, width, channels), lambda h: (0, h, 0)),
            pl.BlockSpec((1, rows, width, channels), lambda h: (h, 0, 0, 0)),
        ],
        out_shape=[
            jax.ShapeDtypeStruct((rows, N2, channels), BF16),
            jax.ShapeDtypeStruct((2, rows, width, channels), F32),
        ],
        scratch_shapes=[pltpu.VMEM((2, channels * pitch, width), F32)],
        compiler_params=pltpu.CompilerParams(vmem_limit_bytes=VMEM),
        cost_estimate=pl.CostEstimate(flops=0, bytes_accessed=5 << 20, transcendentals=0),
        name="homeward",
    )(near(last), *[near(x) for x in early])


def by_channel_body(embeds, perturb, cotangent, filter_spectrum, skip_gain):
    dp, ctx = lax.axis_size("dp"), lax.axis_size("ctx")
    d, c = lax.axis_index("dp"), lax.axis_index("ctx")
    axes = ("dp", "ctx")
    count = dp * ctx
    channels = embeds.shape[2]
    rows = N1 // ctx
    per = channels // count
    plane = 4
    hops = ctx // plane
    tabs = tables()

    def matrix(x):
        return far(x.reshape(1, rows, N2, channels))

    def exchange(x, mask):
        return lax.ppermute(x, axes, [(i, i ^ mask) for i in range(count)]) if mask else x

    first = outward([matrix(embeds), matrix(perturb), far(filter_spectrum)], count)
    received = lax.all_to_all(first, axes, 0, 0, tiled=True).reshape(dp, ctx, 3, per, rows, N2)
    cots = outward_near(matrix(cotangent), count, hops, plane)
    cots = regroup([exchange(x, j // plane * ctx + j % plane) for j, x in enumerate(cots)])
    received = near(received)
    *early, late = cots
    late, received = lax.optimization_barrier((late, received))
    cots = [exchange(x, hop * plane) for hop, x in enumerate([*early, late])]
    gain = lax.dynamic_slice(skip_gain, ((d * ctx + c) * per,), (per,))
    outs = conv_call(gain, received, tabs, plane)
    (send, *kept), early = outs[:-hops], outs[-hops:]
    early = [exchange(x, hop * plane) for hop, x in enumerate(early)]
    send = grad_call(received, kept, cots, send)
    send, *early = lax.optimization_barrier((send, *early))
    last = lax.all_to_all(send.reshape(count, *send.shape[2:]), axes, 0, 0, tiled=True)
    early = [exchange(x, j // plane * ctx + j % plane) for j, x in enumerate(regroup(early))]
    y, grad = homeward(last, early)
    return y.reshape(1, rows * N2, channels), grad


def trig_table(period):
    row_ids = jnp.arange(period, dtype=jnp.int32)
    exponent = row_ids[:, None] * row_ids[None, :] % period
    phase_angle = exponent.astype(jnp.float32) * (two_pi / period)
    return (jnp.cos(phase_angle).astype(jnp.bfloat16), jnp.sin(phase_angle).astype(jnp.bfloat16))


def twiddle(row_first, row_count, col_first, col_count):
    row_ids = row_first + jnp.arange(row_count, dtype=jnp.int32)
    col_ids = col_first + jnp.arange(col_count, dtype=jnp.int32)
    exponent = row_ids[:, None] * col_ids[None, :] % (N1 * N2)
    phase_angle = exponent.astype(jnp.float32) * (two_pi / (N1 * N2))
    return (jnp.cos(phase_angle)[:, :, None], jnp.sin(phase_angle)[:, :, None])


def first_section(values, col_start):
    cos_table, sin_table = trig_table(N1)
    part_real = jnp.einsum("kn,snmc->skmc", cos_table, values, preferred_element_type=jnp.float32)
    part_imag = -jnp.einsum("kn,snmc->skmc", sin_table, values, preferred_element_type=jnp.float32)
    tw_cos, tw_sin = twiddle(0, N1, col_start, values.shape[2])
    out_real = part_real * tw_cos + part_imag * tw_sin
    out_imag = part_imag * tw_cos - part_real * tw_sin
    return jnp.stack([out_real, out_imag], 1).astype(jnp.bfloat16)


def second_section(section_rows):
    cos_table, sin_table = trig_table(N2)
    with_cos = jnp.einsum(
        "sprnc,kn->sprkc", section_rows, cos_table, preferred_element_type=jnp.float32
    )
    with_sin = jnp.einsum(
        "sprnc,kn->sprkc", section_rows, sin_table, preferred_element_type=jnp.float32
    )
    return jnp.stack([with_cos[:, 0] + with_sin[:, 1], with_cos[:, 1] - with_sin[:, 0]], 1)


def spectral_inverse(product, row_start):
    cos_table, sin_table = trig_table(N2)
    with_cos = jnp.einsum("sprkc,nk->sprnc", product, cos_table, preferred_element_type=jnp.float32)
    with_sin = jnp.einsum("sprkc,nk->sprnc", product, sin_table, preferred_element_type=jnp.float32)
    part_real = with_cos[:, 0] - with_sin[:, 1]
    part_imag = with_cos[:, 1] + with_sin[:, 0]
    tw_cos, tw_sin = twiddle(row_start, product.shape[2], 0, N2)
    out_real = part_real * tw_cos - part_imag * tw_sin
    out_imag = part_imag * tw_cos + part_real * tw_sin
    return jnp.stack([out_real, out_imag], 1).astype(jnp.bfloat16)


def column_inverse(mixed_cols):
    cos_table, sin_table = trig_table(N1)
    with_cos = jnp.einsum(
        "nk,skmc->snmc", cos_table, mixed_cols[:, 0], preferred_element_type=jnp.float32
    )
    with_sin = jnp.einsum(
        "nk,skmc->snmc", sin_table, mixed_cols[:, 1], preferred_element_type=jnp.float32
    )
    return ((with_cos - with_sin) * (1.0 / (N1 * N2))).astype(jnp.bfloat16)


def to_spectrum(section_cols):
    return second_section(
        lax.all_to_all(section_cols, "ctx", split_axis=2, concat_axis=3, tiled=True)
    )


def error_terms(signal, filtered, skip_gain, cotangent_view):
    signal_wide = signal.astype(jnp.float32)
    filtered_wide = lax.optimization_barrier(filtered).astype(jnp.float32)
    outputs = signal_wide * filtered_wide + skip_gain * signal_wide
    clean_y = outputs[0]
    smooth_gap = outputs[1] - clean_y
    err_clean = signal_wide[0] * (cotangent_view.astype(jnp.float32) - smart_weight * smooth_gap)
    err_shift = signal_wide[1] * (smart_weight * smooth_gap)
    return (clean_y, jnp.stack([err_clean, err_shift], 0).astype(jnp.bfloat16))


def body(embeds, perturb, cotangent, filter_spectrum, skip_gain):
    ctx_size = lax.axis_size("ctx")
    ctx_index = lax.axis_index("ctx")
    channels = embeds.shape[2]
    row_count = N1 // ctx_size
    col_count = N2 // ctx_size
    row_start = ctx_index * row_count
    col_start = ctx_index * col_count
    clean_rows = embeds[0].reshape(row_count, N2, channels)
    perturb_rows = perturb[0].reshape(row_count, N2, channels)
    shifted = (clean_rows.astype(jnp.float32) + perturb_rows.astype(jnp.float32)).astype(
        jnp.bfloat16
    )
    inputs = jnp.stack([clean_rows, shifted], 0)
    signal_cols = lax.all_to_all(inputs, "ctx", split_axis=2, concat_axis=1, tiled=True)
    section_cols, signal_cols = (first_section(signal_cols, col_start), signal_cols)
    spectra = to_spectrum(section_cols)
    filter_real = filter_spectrum[0]
    filter_imag = filter_spectrum[1]
    spectrum_real = spectra[:, 0]
    spectrum_imag = spectra[:, 1]
    product = jnp.stack(
        [
            filter_real * spectrum_real - filter_imag * spectrum_imag,
            filter_real * spectrum_imag + filter_imag * spectrum_real,
        ],
        1,
    ).astype(jnp.bfloat16)
    mixed_rows = spectral_inverse(product, row_start)
    filtered = column_inverse(
        lax.all_to_all(mixed_rows, "ctx", split_axis=3, concat_axis=2, tiled=True)
    )
    cotangent_rows = cotangent[0].reshape(row_count, N2, channels)
    filtered_rows = lax.all_to_all(filtered, "ctx", split_axis=1, concat_axis=2, tiled=True)
    clean_y, errors = error_terms(inputs, filtered_rows, skip_gain, cotangent_rows)
    clean_output = clean_y.astype(jnp.bfloat16)
    error_section = first_section(
        lax.all_to_all(errors, "ctx", split_axis=2, concat_axis=1, tiled=True), col_start
    )
    error_spec = to_spectrum(error_section)
    error_real = error_spec[:, 0]
    error_imag = error_spec[:, 1]
    term_real = error_real * spectrum_real + error_imag * spectrum_imag
    term_imag = error_imag * spectrum_real - error_real * spectrum_imag
    local_grad = jnp.stack([term_real[0] + term_real[1], term_imag[0] + term_imag[1]], 0) * (
        1.0 / (N1 * N2)
    )
    grad_shard = lax.psum_scatter(
        local_grad.astype(jnp.bfloat16), "dp", scatter_dimension=2, tiled=True
    ).astype(jnp.float32)
    return (clean_output.reshape(1, row_count * N2, channels), grad_shard)


def solution(mesh):
    dp, ctx = mesh.shape["dp"], mesh.shape["ctx"]

    def run(embeds, *rest):
        apart = dp == 2 and embeds.shape[2] % (dp * ctx) == 0 and N1 // ctx == 16 and embeds.shape[2] // (dp * ctx) > 1
        return jax.shard_map(
            by_channel_body if apart else body,
            mesh=mesh,
            in_specs=(
                P("dp", "ctx", None),
                P("dp", "ctx", None),
                P("dp", "ctx", None),
                P(None, "ctx", None, None),
                P(),
            ),
            out_specs=(P("dp", "ctx", None), P(None, "ctx", "dp", None)),
            check_vma=False,
        )(embeds, *rest)

    return run
```

```python
import functools

import jax
import jax.numpy as jnp
import numpy as np
from jax import lax
from jax.experimental import pallas as pl
from jax.experimental.pallas import tpu as pltpu
from jax.sharding import PartitionSpec as P

N1 = 256
N2 = 256
BF16 = jnp.bfloat16
F32 = jnp.float32
EARLY = 2
KEPT = jnp.float32
HALF = 144
VMEM = 26 << 20

two_pi = 6.283185307179586
smart_weight = 2.0


def tables():
    ids = np.arange(N1)
    phase = (ids[:, None] * ids[None, :] % N1) * (two_pi / N1)
    cos_table, sin_table = np.cos(phase), np.sin(phase)
    split_rows = np.concatenate([cos_table[:HALF], -sin_table[:HALF]], 0)
    forward_table = np.block([[cos_table, -sin_table], [sin_table, cos_table]])
    weight = np.where(ids[: N1 // 2] == 0, 1.0, 2.0) / (N1 * N2)
    join_rows = np.concatenate([cos_table[:, : N1 // 2] * weight, -sin_table[:, : N1 // 2] * weight], 1)
    mirror_rows = np.zeros((HALF, N1))
    mirror_rows[ids[:HALF], -ids[:HALF] % N1] = 1
    mirror_cols = np.eye(N2)[::-1]
    angle = (ids[:HALF, None] * ids[None, :]) * (two_pi / (N1 * N2))
    twiddle = np.stack([np.cos(angle), np.sin(angle)], 0)
    small = (split_rows, forward_table, join_rows, mirror_rows, mirror_cols)
    small = [jnp.asarray(t.astype(jnp.bfloat16)) for t in small]
    return (*small, jnp.asarray(twiddle.astype(np.float32)))


def dot(a, b):
    return jnp.dot(a, b, preferred_element_type=F32)


def place(plane):
    c = lax.axis_index("ctx")
    return lax.axis_index("dp"), c // plane, c % plane


def peer(here, j, hop, plane):
    return here[0] ^ (j // plane), (here[1] ^ hop) * plane + (here[2] ^ (j % plane))


def owner(here, j, hop, plane):
    d, c = peer(here, j, hop, plane)
    return c * lax.axis_size("dp") + d


def forward(signals, split_ref, fwd_ref, tw_cos, tw_sin):
    halves = []
    for x in signals:
        part = dot(split_ref[...], x)
        part_real, part_imag = part[:HALF], part[HALF:]
        out_real = part_real * tw_cos + part_imag * tw_sin
        out_imag = part_imag * tw_cos - part_real * tw_sin
        halves.append(jnp.concatenate([out_real.astype(BF16), out_imag.astype(BF16)], 1))
    spectra = dot(jnp.concatenate(halves, 0), fwd_ref[...])
    return [spectra[i * HALF : (i + 1) * HALF] for i in range(len(signals))]


def hermitian_part(filter_real, filter_imag, mirror_rows, mirror_cols):
    rows = dot(mirror_rows, jnp.concatenate([filter_real, filter_imag], 1)).astype(BF16)
    flipped = dot(jnp.concatenate([rows[:, :N2], rows[:, N2:]], 0), mirror_cols)
    out = []
    for part, other, sign in ((filter_real, flipped[:HALF], 0.5), (filter_imag, flipped[HALF:], -0.5)):
        top = other[:8]
        row = lax.broadcasted_iota(jnp.int32, top.shape, 0)
        top = jnp.where(row == 0, pltpu.roll(top, 1, 1), top)
        other = jnp.concatenate([top, other[8:]], 0)
        out.append(0.5 * part[:HALF].astype(F32) + sign * other)
    return out


def gradient(err_spectra, spectra):
    total_real = total_imag = 0.0
    for err_spec, spec in zip(err_spectra, spectra):
        err_real, err_imag = err_spec[:, :N2], err_spec[:, N2:]
        real, imag = spec[:, :N2], spec[:, N2:]
        total_real += err_real * real + err_imag * imag
        total_imag += err_imag * real - err_real * imag
    return total_real, total_imag


def conv_kernel(
    gain_ref, recv_ref, split_ref, fwd_ref, join_ref, mirror_ref, cols_ref, tw_ref,
    send_ref, gap_ref, spec_ref, part_ref, *refs,
):
    *refs, y_rows = refs
    held_refs, early_refs = refs[:3], refs[3:]
    ctx, count = recv_ref.shape[:2]
    hops, near_count = len(early_refs), early_refs[0].shape[0]
    here = place(near_count // count)
    q = pl.program_id(0)

    @pl.when(q == 0)
    def _():
        for held_ref, table_ref in zip(held_refs, (split_ref, fwd_ref, tw_ref)):
            held_ref[...] = table_ref[...]

    tw_cos, tw_sin = tw_ref[0], tw_ref[1]
    signals = []
    for d in range(count):
        clean = recv_ref[:, d, 0, q].reshape(N1, N2)
        perturb = recv_ref[:, d, 1, q].reshape(N1, N2)
        signals += [clean, (clean.astype(F32) + perturb.astype(F32)).astype(BF16)]
    spectra = forward(signals, split_ref, fwd_ref, tw_cos, tw_sin)
    filter_real, filter_imag = hermitian_part(
        recv_ref[:, 0, 2, q].reshape(N1, N2), recv_ref[:, 1, 2, q].reshape(N1, N2), mirror_ref[...], cols_ref[...]
    )
    products = []
    for spec in spectra:
        real, imag = spec[:, :N2], spec[:, N2:]
        prod_real = (filter_real * real - filter_imag * imag).astype(BF16)
        minus_imag = (-filter_real * imag - filter_imag * real).astype(BF16)
        products.append(jnp.concatenate([prod_real, minus_imag], 1))
    back = dot(jnp.concatenate(products, 0), fwd_ref[...])
    mixed, middle = [], []
    for i in range(2 * count):
        back_real, minus_imag = back[i * HALF : (i + 1) * HALF, :N2], back[i * HALF : (i + 1) * HALF, N2:]
        mixed_real = (back_real * tw_cos + minus_imag * tw_sin).astype(BF16)
        mixed_imag = (back_real * tw_sin - minus_imag * tw_cos).astype(BF16)
        mixed.append(jnp.concatenate([mixed_real[: N1 // 2], mixed_imag[: N1 // 2]], 0))
        middle.append(mixed_real[N1 // 2 :].astype(F32)[:1])
    conv = dot(join_ref[...], jnp.concatenate(mixed, 1))
    parity = lax.broadcasted_iota(jnp.int32, (N1, N2), 0) % 2
    alternate = (1 - 2 * parity).astype(F32) * (1.0 / (N1 * N2))
    gain = gain_ref[q]
    errors = []
    for d in range(count):
        pair = []
        for i in range(2):
            k = 2 * d + i
            wide = signals[k].astype(F32)
            filtered = conv[:, k * N2 : (k + 1) * N2] + alternate * middle[k]
            pair.append((wide, wide * filtered.astype(BF16).astype(F32) + gain * wide))
        (clean, clean_y), (shifted, shifted_y) = pair
        y_rows[d * ctx : (d + 1) * ctx] = clean_y.astype(BF16).reshape(ctx, -1, N2)
        gap = smart_weight * (shifted_y - clean_y)
        gap_ref[q, d] = gap.astype(gap_ref.dtype)
        spec_ref[q, d] = spectra[2 * d].astype(spec_ref.dtype)
        errors.append((shifted * gap).astype(BF16))
    total_real, total_imag = gradient(forward(errors, split_ref, fwd_ref, tw_cos, tw_sin), spectra[1::2])
    part_ref[q, 0] = total_real
    part_ref[q, 1] = total_imag

    @pl.when(q < EARLY)
    def _():
        for hop, early_ref in enumerate(early_refs):
            for j in range(near_count):
                side, block = peer(here, j, hop, near_count // count)
                early_ref[j, q] = y_rows[side * ctx + block]

    @pl.when(q >= EARLY)
    def _():
        for d in range(count):
            send_ref[:, d, q - EARLY] = y_rows[d * ctx : (d + 1) * ctx]


def grad_kernel(recv_ref, gap_ref, spec_ref, part_ref, *refs, hops):
    cot_refs, refs = refs[:hops], refs[hops:]
    split_ref, fwd_ref, tw_ref, y_ref, send_ref, cot_rows, ready_ref, sems = refs
    copies = [pltpu.make_async_copy(y_ref, send_ref.at[:, :, pl.ds(0, y_ref.shape[2])], sems.at[0])]
    copies[0].start()
    ctx, count = recv_ref.shape[:2]
    near = cot_refs[0].shape[0]
    plane = near // count
    here = place(plane)
    per = recv_ref.shape[3]
    for hop, cot_ref in enumerate(cot_refs):
        for j in range(near):
            side, block = peer(here, j, hop, plane)
            cot_rows[side * ctx + block] = cot_ref[j]
    errors = []
    for q in range(per):
        for d in range(count):
            clean = recv_ref[:, d, 0, q].reshape(N1, N2).astype(F32)
            cot = cot_rows[d * ctx : (d + 1) * ctx, q].reshape(N1, N2).astype(F32)
            errors.append((clean * (cot - gap_ref[q, d])).astype(BF16))
    err_spectra = forward(errors, split_ref, fwd_ref, tw_ref[0], tw_ref[1])
    for q in range(per):
        spectra = [spec_ref[q, d] for d in range(count)]
        total = gradient(err_spectra[q * count : (q + 1) * count], spectra)
        fill_grad(ready_ref, q, *[t + part_ref[q, i] for i, t in enumerate(total)])
        copies.append(pltpu.make_async_copy(ready_ref.at[q], send_ref.at[:, :, per - EARLY + q], sems.at[1 + q]))
        copies[1 + q].start()
    for copy in copies:
        copy.wait()


def fill_grad(ready_ref, q, total_real, total_imag):
    _, ctx, count, rows, _ = ready_ref.shape
    total = jnp.concatenate([total_real, total_imag], 1) * (1.0 / (N1 * N2))
    upper, after = total[: N1 // 2], total[rows : N1 // 2 + rows]
    first = lax.broadcasted_iota(jnp.int32, upper.shape, 0) % rows == 0
    lower = jnp.where(first, after, upper).astype(BF16)
    upper = upper.astype(BF16)
    width = N2 // count
    for i in range(count):
        for half, x, side in ((0, upper, i), (1, lower, count - 1 - i)):
            cols = slice(side * width, (side + 1) * width)
            pair = jnp.concatenate([x[:, :N2][:, cols], x[:, N2:][:, cols]], 1)
            for block in range(ctx // 2):
                target = ctx - 1 - block if half else block
                ready_ref[q, target, i] = pair[block * rows : (block + 1) * rows]


def whole(x):
    return pl.BlockSpec(x.shape, lambda *_: (0,) * x.ndim)


def near(x):
    return pltpu.with_memory_space_constraint(x, pltpu.VMEM)


def far(x):
    return pltpu.with_memory_space_constraint(x, pltpu.HBM)


def conv_call(gain, received, tabs, plane):
    ctx, dp, _, per, rows, _ = received.shape
    split_rows, forward_table, *_, twiddle = tabs
    early = (dp * plane, EARLY, rows, N2)
    held = [pltpu.VMEM(t.shape, t.dtype) for t in (split_rows, forward_table, twiddle)]
    return pl.pallas_call(
        conv_kernel,
        grid=(per,),
        in_specs=[
            pl.BlockSpec(memory_space=pltpu.SMEM),
            pl.BlockSpec(memory_space=pltpu.VMEM),
            *[whole(t) for t in tabs],
        ],
        out_specs=[
            *[pl.BlockSpec(memory_space=pltpu.VMEM)] * (7 + ctx // plane),
        ],
        out_shape=[
            pltpu.VMEM((ctx, dp, per - EARLY, rows, N2), BF16),
            pltpu.VMEM((per, dp, N1, N2), KEPT),
            pltpu.VMEM((per, dp, HALF, 2 * N2), KEPT),
            pltpu.VMEM((per, 2, HALF, N2), F32),
            *held,
            *[pltpu.VMEM(early, BF16)] * (ctx // plane),
        ],
        scratch_shapes=[pltpu.VMEM((dp * ctx, rows, N2), BF16)],
        compiler_params=pltpu.CompilerParams(vmem_limit_bytes=VMEM),
        cost_estimate=pl.CostEstimate(flops=per * dp * 5 * 6 * N1**3, bytes_accessed=8 << 20, transcendentals=0),
        name="conv",
    )(gain, received, *[far(t) for t in tabs])


def grad_call(received, kept, cots, send):
    ctx, dp, _, per, rows, _ = received.shape
    *kept, split_rows, forward_table, twiddle = [near(x) for x in kept]
    operands = (received, *kept, *[near(x) for x in cots], split_rows, forward_table, twiddle, near(send))
    return pl.pallas_call(
        functools.partial(grad_kernel, hops=len(cots)),
        grid=(1,),
        in_specs=[pl.BlockSpec(memory_space=pltpu.VMEM)] * len(operands),
        out_specs=pl.BlockSpec(memory_space=pl.ANY),
        out_shape=pltpu.HBM((ctx, dp, 2 * per - EARLY, rows, N2), BF16),
        scratch_shapes=[
            pltpu.VMEM((dp * ctx, per, rows, N2), BF16),
            pltpu.VMEM((per, ctx, dp, rows, N2), BF16),
            pltpu.SemaphoreType.DMA((1 + per,)),
        ],
        compiler_params=pltpu.CompilerParams(vmem_limit_bytes=VMEM),
        cost_estimate=pl.CostEstimate(flops=per * dp * 6 * N1**3, bytes_accessed=8 << 20, transcendentals=0),
        name="grad",
    )(*operands)


def outward_kernel(*refs, count):
    in_refs, refs = refs[:count], refs[count:]
    out_ref, refs = refs[0], refs[1:]
    held_refs, (rows_ref, ready_ref, load_sems, store_sems) = refs[:count], refs[count:]
    devices, _, per, rows, _ = out_ref.shape
    pitch = rows_ref.shape[1] // (devices * per)
    width = rows_ref.shape[2]
    loads, stores = [], []
    for t, (in_ref, held_ref) in enumerate(zip(in_refs, held_refs)):
        source = in_ref.at[lax.axis_index("dp") if in_ref.shape[0] > 1 else 0]
        loads.append(pltpu.make_async_copy(source, held_ref, load_sems.at[t]))
        loads[t].start()
    for t, held_ref in enumerate(held_refs):
        loads[t].wait()
        for h in range(N2 // width):
            lanes = slice(h * width, (h + 1) * width)
            for r in range(rows):
                block = held_ref[r, lanes].astype(BF16).T.astype(F32)
                rows_ref[h, pl.ds(r, devices * per, stride=pitch), :] = block
            block = rows_ref[h].reshape(devices, per, pitch, width)[:, :, :rows].astype(BF16)
            ready_ref[t, :, :, :, lanes] = block
        stores.append(pltpu.make_async_copy(ready_ref.at[t], out_ref.at[:, t], store_sems.at[t]))
        stores[t].start()
    for store in stores:
        store.wait()


def outward(arrays, devices):
    _, rows, _, channels = arrays[0].shape
    count, per, width, pitch = len(arrays), channels // devices, 128, rows + 8
    shape = (devices, count, per, rows, N2)
    return pl.pallas_call(
        functools.partial(outward_kernel, count=count),
        in_specs=[pl.BlockSpec(memory_space=pl.ANY)] * count,
        out_specs=pl.BlockSpec(memory_space=pl.ANY),
        out_shape=pltpu.HBM(shape, BF16),
        scratch_shapes=[
            *[pltpu.VMEM(a.shape[1:], a.dtype) for a in arrays],
            pltpu.VMEM((N2 // width, channels * pitch, width), F32),
            pltpu.VMEM((count, devices, per, rows, N2), BF16),
            pltpu.SemaphoreType.DMA((count,)),
            pltpu.SemaphoreType.DMA((count,)),
        ],
        compiler_params=pltpu.CompilerParams(vmem_limit_bytes=VMEM),
        cost_estimate=pl.CostEstimate(flops=0, bytes_accessed=7 << 20, transcendentals=0),
        name="outward",
    )(*arrays)


def outward_near_kernel(in_ref, *refs, hops, plane):
    here = place(plane)
    *out_refs, rows_ref = refs
    _, per, rows, width = out_refs[0].shape
    channels = in_ref.shape[3]
    pitch = rows_ref.shape[0] // channels
    for r in range(rows):
        rows_ref[pl.ds(r, channels, stride=pitch), :] = in_ref[0, r].T.astype(F32)
    for j, out_ref in enumerate(out_refs):
        for hop in range(hops):
            block = owner(here, j, hop, plane) * (per * pitch)
            rows_here = rows_ref[pl.ds(pl.multiple_of(block, per * pitch), per * pitch), :]
            out_ref[hop] = rows_here.reshape(per, pitch, width)[:, :rows].astype(BF16)


def outward_near(x, count, hops, plane):
    _, rows, _, channels = x.shape
    per = channels // count
    width = 128
    return pl.pallas_call(
        functools.partial(outward_near_kernel, hops=hops, plane=plane),
        grid=(N2 // width,),
        in_specs=[pl.BlockSpec((1, rows, width, channels), lambda h: (0, 0, h, 0))],
        out_specs=[pl.BlockSpec((hops, per, rows, width), lambda h: (0, 0, 0, h))] * (count // hops),
        out_shape=[jax.ShapeDtypeStruct((hops, per, rows, N2), BF16)] * (count // hops),
        scratch_shapes=[pltpu.VMEM((channels * (rows + 8), width), F32)],
        compiler_params=pltpu.CompilerParams(vmem_limit_bytes=VMEM),
        cost_estimate=pl.CostEstimate(flops=0, bytes_accessed=2 << 20, transcendentals=0),
        name="outward_near",
    )(x)


def regroup_kernel(*refs, count):
    for i, in_ref in enumerate(refs[:count]):
        for j, out_ref in enumerate(refs[count:]):
            out_ref[i] = in_ref[j]


def regroup(arrays):
    hops, *block = arrays[0].shape
    return pl.pallas_call(
        functools.partial(regroup_kernel, count=len(arrays)),
        out_shape=[jax.ShapeDtypeStruct((len(arrays), *block), BF16)] * hops,
        compiler_params=pltpu.CompilerParams(vmem_limit_bytes=VMEM),
        cost_estimate=pl.CostEstimate(flops=0, bytes_accessed=2 << 20, transcendentals=0),
        name="regroup",
    )(*arrays)


def homeward_kernel(last_ref, *refs, per):
    *early_refs, y_ref, grad_ref, rows_ref = refs
    count, _, rows, _ = last_ref.shape
    hops = early_refs[0].shape[0]
    plane = count // hops // 2
    here = place(plane)
    width = rows_ref.shape[2]
    pitch = rows_ref.shape[1] // (count * per)
    h = pl.program_id(0)
    lanes = pl.ds(pl.multiple_of(h * width, width), width)
    lower = lax.axis_index("ctx") >= lax.axis_size("ctx") // 2
    row = lax.broadcasted_iota(jnp.int32, (width, width), 0)
    col = lax.broadcasted_iota(jnp.int32, (width, width), 1)
    turn = (col == jnp.where(lower, width - 1 - row, row)).astype(F32)
    turn = (turn * jnp.where(lower, (1 - 2 * h).astype(F32), 1.0)).astype(BF16)
    y_rows = rows_ref.at[0].reshape(count, per, pitch, width)
    grad_rows = rows_ref.at[1].reshape(count, per, pitch, width)
    for j, early_ref in enumerate(early_refs):
        for hop in range(hops):
            y_rows[owner(here, j, hop, plane), :EARLY, :rows] = early_ref[hop, :, :, lanes].astype(F32)
    y_rows[:, EARLY:, :rows] = last_ref[:, : per - EARLY, :, lanes].astype(F32)
    block = last_ref[:, per - EARLY :, :, lanes]
    grad_rows[:, :, :rows] = dot(block.reshape(count * per * rows, width), turn).reshape(block.shape)
    for r in range(rows):
        y_ref[r] = rows_ref[0, pl.ds(r, count * per, stride=pitch), :].astype(BF16).T
    for r in range(rows):
        target = jnp.where(lower, (rows - r) % rows, r)
        grad_ref[0, target] = rows_ref[1, pl.ds(r, count * per, stride=pitch), :].T


def homeward(last, early):
    count, slots, rows, _ = last.shape
    per = (slots + EARLY) // 2
    channels, width, pitch = count * per, 128, rows + 8
    return pl.pallas_call(
        functools.partial(homeward_kernel, per=per),
        grid=(N2 // width,),
        in_specs=[pl.BlockSpec(memory_space=pltpu.VMEM)] * (1 + len(early)),
        out_specs=[
            pl.BlockSpec((rows, width, channels), lambda h: (0, h, 0)),
            pl.BlockSpec((1, rows, width, channels), lambda h: (h, 0, 0, 0)),
        ],
        out_shape=[
            jax.ShapeDtypeStruct((rows, N2, channels), BF16),
            jax.ShapeDtypeStruct((2, rows, width, channels), F32),
        ],
        scratch_shapes=[pltpu.VMEM((2, channels * pitch, width), F32)],
        compiler_params=pltpu.CompilerParams(vmem_limit_bytes=VMEM),
        cost_estimate=pl.CostEstimate(flops=0, bytes_accessed=5 << 20, transcendentals=0),
        name="homeward",
    )(near(last), *[near(x) for x in early])


def by_channel_body(embeds, perturb, cotangent, filter_spectrum, skip_gain):
    dp, ctx = lax.axis_size("dp"), lax.axis_size("ctx")
    d, c = lax.axis_index("dp"), lax.axis_index("ctx")
    axes, order = ("dp", "ctx"), ("ctx", "dp")
    count = dp * ctx
    channels = embeds.shape[2]
    rows = N1 // ctx
    per = channels // count
    plane = 4
    hops = ctx // plane
    tabs = tables()

    def matrix(x):
        return far(x.reshape(1, rows, N2, channels))

    def exchange(x, mask):
        return lax.ppermute(x, axes, [(i, i ^ mask) for i in range(count)]) if mask else x

    first = outward([matrix(embeds), matrix(perturb), far(filter_spectrum)], count)
    received = lax.all_to_all(first, order, 0, 0, tiled=True).reshape(ctx, dp, 3, per, rows, N2)
    cots = outward_near(matrix(cotangent), count, hops, plane)
    cots = regroup([exchange(x, j // plane * ctx + j % plane) for j, x in enumerate(cots)])
    received = near(received)
    *early, late = cots
    late, received = lax.optimization_barrier((late, received))
    cots = [exchange(x, hop * plane) for hop, x in enumerate([*early, late])]
    gain = lax.dynamic_slice(skip_gain, ((c * dp + d) * per,), (per,))
    outs = conv_call(gain, received, tabs, plane)
    (send, *kept), early = outs[:-hops], outs[-hops:]
    early = [exchange(x, hop * plane) for hop, x in enumerate(early)]
    send = grad_call(received, kept, cots, send)
    send, *early = lax.optimization_barrier((send, *early))
    last = lax.all_to_all(send.reshape(count, *send.shape[2:]), order, 0, 0, tiled=True)
    early = [exchange(x, j // plane * ctx + j % plane) for j, x in enumerate(regroup(early))]
    y, grad = homeward(last, early)
    return y.reshape(1, rows * N2, channels), grad


def trig_table(period):
    row_ids = jnp.arange(period, dtype=jnp.int32)
    exponent = row_ids[:, None] * row_ids[None, :] % period
    phase_angle = exponent.astype(jnp.float32) * (two_pi / period)
    return (jnp.cos(phase_angle).astype(jnp.bfloat16), jnp.sin(phase_angle).astype(jnp.bfloat16))


def twiddle(row_first, row_count, col_first, col_count):
    row_ids = row_first + jnp.arange(row_count, dtype=jnp.int32)
    col_ids = col_first + jnp.arange(col_count, dtype=jnp.int32)
    exponent = row_ids[:, None] * col_ids[None, :] % (N1 * N2)
    phase_angle = exponent.astype(jnp.float32) * (two_pi / (N1 * N2))
    return (jnp.cos(phase_angle)[:, :, None], jnp.sin(phase_angle)[:, :, None])


def first_section(values, col_start):
    cos_table, sin_table = trig_table(N1)
    part_real = jnp.einsum("kn,snmc->skmc", cos_table, values, preferred_element_type=jnp.float32)
    part_imag = -jnp.einsum("kn,snmc->skmc", sin_table, values, preferred_element_type=jnp.float32)
    tw_cos, tw_sin = twiddle(0, N1, col_start, values.shape[2])
    out_real = part_real * tw_cos + part_imag * tw_sin
    out_imag = part_imag * tw_cos - part_real * tw_sin
    return jnp.stack([out_real, out_imag], 1).astype(jnp.bfloat16)


def second_section(section_rows):
    cos_table, sin_table = trig_table(N2)
    with_cos = jnp.einsum(
        "sprnc,kn->sprkc", section_rows, cos_table, preferred_element_type=jnp.float32
    )
    with_sin = jnp.einsum(
        "sprnc,kn->sprkc", section_rows, sin_table, preferred_element_type=jnp.float32
    )
    return jnp.stack([with_cos[:, 0] + with_sin[:, 1], with_cos[:, 1] - with_sin[:, 0]], 1)


def spectral_inverse(product, row_start):
    cos_table, sin_table = trig_table(N2)
    with_cos = jnp.einsum("sprkc,nk->sprnc", product, cos_table, preferred_element_type=jnp.float32)
    with_sin = jnp.einsum("sprkc,nk->sprnc", product, sin_table, preferred_element_type=jnp.float32)
    part_real = with_cos[:, 0] - with_sin[:, 1]
    part_imag = with_cos[:, 1] + with_sin[:, 0]
    tw_cos, tw_sin = twiddle(row_start, product.shape[2], 0, N2)
    out_real = part_real * tw_cos - part_imag * tw_sin
    out_imag = part_imag * tw_cos + part_real * tw_sin
    return jnp.stack([out_real, out_imag], 1).astype(jnp.bfloat16)


def column_inverse(mixed_cols):
    cos_table, sin_table = trig_table(N1)
    with_cos = jnp.einsum(
        "nk,skmc->snmc", cos_table, mixed_cols[:, 0], preferred_element_type=jnp.float32
    )
    with_sin = jnp.einsum(
        "nk,skmc->snmc", sin_table, mixed_cols[:, 1], preferred_element_type=jnp.float32
    )
    return ((with_cos - with_sin) * (1.0 / (N1 * N2))).astype(jnp.bfloat16)


def to_spectrum(section_cols):
    return second_section(
        lax.all_to_all(section_cols, "ctx", split_axis=2, concat_axis=3, tiled=True)
    )


def error_terms(signal, filtered, skip_gain, cotangent_view):
    signal_wide = signal.astype(jnp.float32)
    filtered_wide = lax.optimization_barrier(filtered).astype(jnp.float32)
    outputs = signal_wide * filtered_wide + skip_gain * signal_wide
    clean_y = outputs[0]
    smooth_gap = outputs[1] - clean_y
    err_clean = signal_wide[0] * (cotangent_view.astype(jnp.float32) - smart_weight * smooth_gap)
    err_shift = signal_wide[1] * (smart_weight * smooth_gap)
    return (clean_y, jnp.stack([err_clean, err_shift], 0).astype(jnp.bfloat16))


def body(embeds, perturb, cotangent, filter_spectrum, skip_gain):
    ctx_size = lax.axis_size("ctx")
    ctx_index = lax.axis_index("ctx")
    channels = embeds.shape[2]
    row_count = N1 // ctx_size
    col_count = N2 // ctx_size
    row_start = ctx_index * row_count
    col_start = ctx_index * col_count
    clean_rows = embeds[0].reshape(row_count, N2, channels)
    perturb_rows = perturb[0].reshape(row_count, N2, channels)
    shifted = (clean_rows.astype(jnp.float32) + perturb_rows.astype(jnp.float32)).astype(
        jnp.bfloat16
    )
    inputs = jnp.stack([clean_rows, shifted], 0)
    signal_cols = lax.all_to_all(inputs, "ctx", split_axis=2, concat_axis=1, tiled=True)
    section_cols, signal_cols = (first_section(signal_cols, col_start), signal_cols)
    spectra = to_spectrum(section_cols)
    filter_real = filter_spectrum[0]
    filter_imag = filter_spectrum[1]
    spectrum_real = spectra[:, 0]
    spectrum_imag = spectra[:, 1]
    product = jnp.stack(
        [
            filter_real * spectrum_real - filter_imag * spectrum_imag,
            filter_real * spectrum_imag + filter_imag * spectrum_real,
        ],
        1,
    ).astype(jnp.bfloat16)
    mixed_rows = spectral_inverse(product, row_start)
    filtered = column_inverse(
        lax.all_to_all(mixed_rows, "ctx", split_axis=3, concat_axis=2, tiled=True)
    )
    cotangent_rows = cotangent[0].reshape(row_count, N2, channels)
    filtered_rows = lax.all_to_all(filtered, "ctx", split_axis=1, concat_axis=2, tiled=True)
    clean_y, errors = error_terms(inputs, filtered_rows, skip_gain, cotangent_rows)
    clean_output = clean_y.astype(jnp.bfloat16)
    error_section = first_section(
        lax.all_to_all(errors, "ctx", split_axis=2, concat_axis=1, tiled=True), col_start
    )
    error_spec = to_spectrum(error_section)
    error_real = error_spec[:, 0]
    error_imag = error_spec[:, 1]
    term_real = error_real * spectrum_real + error_imag * spectrum_imag
    term_imag = error_imag * spectrum_real - error_real * spectrum_imag
    local_grad = jnp.stack([term_real[0] + term_real[1], term_imag[0] + term_imag[1]], 0) * (
        1.0 / (N1 * N2)
    )
    grad_shard = lax.psum_scatter(
        local_grad.astype(jnp.bfloat16), "dp", scatter_dimension=2, tiled=True
    ).astype(jnp.float32)
    return (clean_output.reshape(1, row_count * N2, channels), grad_shard)


def solution(mesh):
    dp, ctx = mesh.shape["dp"], mesh.shape["ctx"]

    def run(embeds, *rest):
        apart = dp == 2 and embeds.shape[2] % (dp * ctx) == 0 and N1 // ctx == 16 and embeds.shape[2] // (dp * ctx) > 1
        return jax.shard_map(
            by_channel_body if apart else body,
            mesh=mesh,
            in_specs=(
                P("dp", "ctx", None),
                P("dp", "ctx", None),
                P("dp", "ctx", None),
                P(None, "ctx", None, None),
                P(),
            ),
            out_specs=(P("dp", "ctx", None), P(None, "ctx", "dp", None)),
            check_vma=False,
        )(embeds, *rest)

    return run
```

```python
import functools

import jax
import jax.numpy as jnp
import numpy as np
from jax import lax
from jax.experimental import pallas as pl
from jax.experimental.pallas import tpu as pltpu
from jax.sharding import PartitionSpec as P

N1 = 256
N2 = 256
BF16 = jnp.bfloat16
F32 = jnp.float32
EARLY = 2
KEPT = jnp.float32
HALF = 144
VMEM = 26 << 20

two_pi = 6.283185307179586
smart_weight = 2.0


def tables():
    ids = np.arange(N1)
    phase = (ids[:, None] * ids[None, :] % N1) * (two_pi / N1)
    cos_table, sin_table = np.cos(phase), np.sin(phase)
    split_rows = np.concatenate([cos_table[:HALF], -sin_table[:HALF]], 0)
    forward_table = np.block([[cos_table, -sin_table], [sin_table, cos_table]])
    weight = np.where(ids[: N1 // 2] == 0, 1.0, 2.0) / (N1 * N2)
    join_rows = np.concatenate([cos_table[:, : N1 // 2] * weight, -sin_table[:, : N1 // 2] * weight], 1)
    mirror_rows = np.zeros((HALF, N1))
    mirror_rows[ids[:HALF], -ids[:HALF] % N1] = 1
    mirror_cols = np.eye(N2)[::-1]
    angle = (ids[:HALF, None] * ids[None, :]) * (two_pi / (N1 * N2))
    twiddle = np.stack([np.cos(angle), np.sin(angle)], 0)
    small = (split_rows, forward_table, join_rows, mirror_rows, mirror_cols)
    small = [jnp.asarray(t.astype(jnp.bfloat16)) for t in small]
    return (*small, jnp.asarray(twiddle.astype(np.float32)))


def dot(a, b):
    return jnp.dot(a, b, preferred_element_type=F32)


def place(plane):
    c = lax.axis_index("ctx")
    return lax.axis_index("dp"), c // plane, c % plane


def peer(here, j, hop, plane):
    return here[0] ^ (j // plane), (here[1] ^ hop) * plane + (here[2] ^ (j % plane))


def owner(here, j, hop, plane):
    d, c = peer(here, j, hop, plane)
    return c * lax.axis_size("dp") + d


def forward(signals, split_ref, fwd_ref, tw_cos, tw_sin):
    halves = []
    for x in signals:
        part = dot(split_ref[...], x)
        part_real, part_imag = part[:HALF], part[HALF:]
        out_real = part_real * tw_cos + part_imag * tw_sin
        out_imag = part_imag * tw_cos - part_real * tw_sin
        halves.append(jnp.concatenate([out_real.astype(BF16), out_imag.astype(BF16)], 1))
    spectra = dot(jnp.concatenate(halves, 0), fwd_ref[...])
    return [spectra[i * HALF : (i + 1) * HALF] for i in range(len(signals))]


def hermitian_part(filter_real, filter_imag, mirror_rows, mirror_cols):
    rows = dot(mirror_rows, jnp.concatenate([filter_real, filter_imag], 1)).astype(BF16)
    flipped = dot(jnp.concatenate([rows[:, :N2], rows[:, N2:]], 0), mirror_cols)
    out = []
    for part, other, sign in ((filter_real, flipped[:HALF], 0.5), (filter_imag, flipped[HALF:], -0.5)):
        top = other[:8]
        row = lax.broadcasted_iota(jnp.int32, top.shape, 0)
        top = jnp.where(row == 0, pltpu.roll(top, 1, 1), top)
        other = jnp.concatenate([top, other[8:]], 0)
        out.append(0.5 * part[:HALF].astype(F32) + sign * other)
    return out


def gradient(err_spectra, spectra):
    total_real = total_imag = 0.0
    for err_spec, spec in zip(err_spectra, spectra):
        err_real, err_imag = err_spec[:, :N2], err_spec[:, N2:]
        real, imag = spec[:, :N2], spec[:, N2:]
        total_real += err_real * real + err_imag * imag
        total_imag += err_imag * real - err_real * imag
    return total_real, total_imag


def conv_kernel(
    gain_ref, recv_ref, split_ref, fwd_ref, join_ref, mirror_ref, cols_ref, tw_ref,
    send_ref, gap_ref, spec_ref, part_ref, *refs,
):
    *refs, y_rows = refs
    held_refs, early_refs = refs[:3], refs[3:]
    ctx, count = recv_ref.shape[:2]
    hops, near_count = len(early_refs), early_refs[0].shape[0]
    here = place(near_count // count)
    q = pl.program_id(0)

    @pl.when(q == 0)
    def _():
        for held_ref, table_ref in zip(held_refs, (split_ref, fwd_ref, tw_ref)):
            held_ref[...] = table_ref[...]

    tw_cos, tw_sin = tw_ref[0], tw_ref[1]
    signals = []
    for d in range(count):
        clean = recv_ref[:, d, 0, q].reshape(N1, N2)
        perturb = recv_ref[:, d, 1, q].reshape(N1, N2)
        signals += [clean, (clean.astype(F32) + perturb.astype(F32)).astype(BF16)]
    spectra = forward(signals, split_ref, fwd_ref, tw_cos, tw_sin)
    filter_real, filter_imag = hermitian_part(
        recv_ref[:, 0, 2, q].reshape(N1, N2), recv_ref[:, 1, 2, q].reshape(N1, N2), mirror_ref[...], cols_ref[...]
    )
    products = []
    for spec in spectra:
        real, imag = spec[:, :N2], spec[:, N2:]
        prod_real = (filter_real * real - filter_imag * imag).astype(BF16)
        minus_imag = (-filter_real * imag - filter_imag * real).astype(BF16)
        products.append(jnp.concatenate([prod_real, minus_imag], 1))
    back = dot(jnp.concatenate(products, 0), fwd_ref[...])
    mixed, middle = [], []
    for i in range(2 * count):
        back_real, minus_imag = back[i * HALF : (i + 1) * HALF, :N2], back[i * HALF : (i + 1) * HALF, N2:]
        mixed_real = (back_real * tw_cos + minus_imag * tw_sin).astype(BF16)
        mixed_imag = (back_real * tw_sin - minus_imag * tw_cos).astype(BF16)
        mixed.append(jnp.concatenate([mixed_real[: N1 // 2], mixed_imag[: N1 // 2]], 0))
        middle.append(mixed_real[N1 // 2 :].astype(F32)[:1])
    conv = dot(join_ref[...], jnp.concatenate(mixed, 1))
    parity = lax.broadcasted_iota(jnp.int32, (N1, N2), 0) % 2
    alternate = (1 - 2 * parity).astype(F32) * (1.0 / (N1 * N2))
    gain = gain_ref[q]
    errors = []
    for d in range(count):
        pair = []
        for i in range(2):
            k = 2 * d + i
            wide = signals[k].astype(F32)
            filtered = conv[:, k * N2 : (k + 1) * N2] + alternate * middle[k]
            pair.append((wide, wide * filtered.astype(BF16).astype(F32) + gain * wide))
        (clean, clean_y), (shifted, shifted_y) = pair
        y_rows[d * ctx : (d + 1) * ctx] = clean_y.astype(BF16).reshape(ctx, -1, N2)
        gap = smart_weight * (shifted_y - clean_y)
        gap_ref[q, d] = gap.astype(gap_ref.dtype)
        spec_ref[q, d] = spectra[2 * d].astype(spec_ref.dtype)
        errors.append((shifted * gap).astype(BF16))
    total_real, total_imag = gradient(forward(errors, split_ref, fwd_ref, tw_cos, tw_sin), spectra[1::2])
    part_ref[q, 0] = total_real
    part_ref[q, 1] = total_imag

    @pl.when(q < EARLY)
    def _():
        for hop, early_ref in enumerate(early_refs):
            for j in range(near_count):
                side, block = peer(here, j, hop, near_count // count)
                early_ref[j, q] = y_rows[side * ctx + block]

    @pl.when(q >= EARLY)
    def _():
        for d in range(count):
            send_ref[:, d, q - EARLY] = y_rows[d * ctx : (d + 1) * ctx]


def grad_kernel(recv_ref, gap_ref, spec_ref, part_ref, *refs, hops):
    cot_refs, refs = refs[:hops], refs[hops:]
    split_ref, fwd_ref, tw_ref, y_ref, send_ref, cot_rows, ready_ref, sems = refs
    copies = [pltpu.make_async_copy(y_ref, send_ref.at[:, :, pl.ds(0, y_ref.shape[2])], sems.at[0])]
    copies[0].start()
    ctx, count = recv_ref.shape[:2]
    near = cot_refs[0].shape[0]
    plane = near // count
    here = place(plane)
    per = recv_ref.shape[3]
    for hop, cot_ref in enumerate(cot_refs):
        for j in range(near):
            side, block = peer(here, j, hop, plane)
            cot_rows[side * ctx + block] = cot_ref[j]
    errors = []
    for q in range(per):
        for d in range(count):
            clean = recv_ref[:, d, 0, q].reshape(N1, N2).astype(F32)
            cot = cot_rows[d * ctx : (d + 1) * ctx, q].reshape(N1, N2).astype(F32)
            errors.append((clean * (cot - gap_ref[q, d])).astype(BF16))
    err_spectra = forward(errors, split_ref, fwd_ref, tw_ref[0], tw_ref[1])
    for q in range(per):
        spectra = [spec_ref[q, d] for d in range(count)]
        total = gradient(err_spectra[q * count : (q + 1) * count], spectra)
        fill_grad(ready_ref, q, *[t + part_ref[q, i] for i, t in enumerate(total)])
        copies.append(pltpu.make_async_copy(ready_ref.at[q], send_ref.at[:, :, per - EARLY + q], sems.at[1 + q]))
        copies[1 + q].start()
    for copy in copies:
        copy.wait()


def fill_grad(ready_ref, q, total_real, total_imag):
    _, ctx, count, rows, _ = ready_ref.shape
    total = jnp.concatenate([total_real, total_imag], 1) * (1.0 / (N1 * N2))
    upper, after = total[: N1 // 2], total[rows : N1 // 2 + rows]
    first = lax.broadcasted_iota(jnp.int32, upper.shape, 0) % rows == 0
    lower = jnp.where(first, after, upper).astype(BF16)
    upper = upper.astype(BF16)
    width = N2 // count
    for i in range(count):
        for half, x, side in ((0, upper, i), (1, lower, count - 1 - i)):
            cols = slice(side * width, (side + 1) * width)
            pair = jnp.concatenate([x[:, :N2][:, cols], x[:, N2:][:, cols]], 1)
            for block in range(ctx // 2):
                target = ctx - 1 - block if half else block
                ready_ref[q, target, i] = pair[block * rows : (block + 1) * rows]


def whole(x):
    return pl.BlockSpec(x.shape, lambda *_: (0,) * x.ndim)


def near(x):
    return pltpu.with_memory_space_constraint(x, pltpu.VMEM)


def far(x):
    return pltpu.with_memory_space_constraint(x, pltpu.HBM)


def conv_call(gain, received, tabs, plane):
    ctx, dp, _, per, rows, _ = received.shape
    split_rows, forward_table, *_, twiddle = tabs
    early = (dp * plane, EARLY, rows, N2)
    held = [pltpu.VMEM(t.shape, t.dtype) for t in (split_rows, forward_table, twiddle)]
    return pl.pallas_call(
        conv_kernel,
        grid=(per,),
        in_specs=[
            pl.BlockSpec(memory_space=pltpu.SMEM),
            pl.BlockSpec(memory_space=pltpu.VMEM),
            *[whole(t) for t in tabs],
        ],
        out_specs=[
            *[pl.BlockSpec(memory_space=pltpu.VMEM)] * (7 + ctx // plane),
        ],
        out_shape=[
            pltpu.VMEM((ctx, dp, per - EARLY, rows, N2), BF16),
            pltpu.VMEM((per, dp, N1, N2), KEPT),
            pltpu.VMEM((per, dp, HALF, 2 * N2), KEPT),
            pltpu.VMEM((per, 2, HALF, N2), F32),
            *held,
            *[pltpu.VMEM(early, BF16)] * (ctx // plane),
        ],
        scratch_shapes=[pltpu.VMEM((dp * ctx, rows, N2), BF16)],
        compiler_params=pltpu.CompilerParams(vmem_limit_bytes=VMEM),
        cost_estimate=pl.CostEstimate(flops=per * dp * 5 * 6 * N1**3, bytes_accessed=8 << 20, transcendentals=0),
        name="conv",
    )(gain, received, *[far(t) for t in tabs])


def grad_call(received, kept, cots, send):
    ctx, dp, _, per, rows, _ = received.shape
    *kept, split_rows, forward_table, twiddle = [near(x) for x in kept]
    operands = (received, *kept, *[near(x) for x in cots], split_rows, forward_table, twiddle, near(send))
    return pl.pallas_call(
        functools.partial(grad_kernel, hops=len(cots)),
        grid=(1,),
        in_specs=[pl.BlockSpec(memory_space=pltpu.VMEM)] * len(operands),
        out_specs=pl.BlockSpec(memory_space=pl.ANY),
        out_shape=pltpu.HBM((ctx, dp, 2 * per - EARLY, rows, N2), BF16),
        scratch_shapes=[
            pltpu.VMEM((dp * ctx, per, rows, N2), BF16),
            pltpu.VMEM((per, ctx, dp, rows, N2), BF16),
            pltpu.SemaphoreType.DMA((1 + per,)),
        ],
        compiler_params=pltpu.CompilerParams(vmem_limit_bytes=VMEM),
        cost_estimate=pl.CostEstimate(flops=per * dp * 6 * N1**3, bytes_accessed=8 << 20, transcendentals=0),
        name="grad",
    )(*operands)


def outward_kernel(*refs, count):
    in_refs, refs = refs[:count], refs[count:]
    out_ref, refs = refs[0], refs[1:]
    held_refs, (rows_ref, ready_ref, load_sems, store_sems) = refs[:count], refs[count:]
    devices, _, per, rows, _ = out_ref.shape
    pitch = rows_ref.shape[1] // (devices * per)
    width = rows_ref.shape[2]
    loads, stores = [], []
    for t, (in_ref, held_ref) in enumerate(zip(in_refs, held_refs)):
        source = in_ref.at[lax.axis_index("dp") if in_ref.shape[0] > 1 else 0]
        loads.append(pltpu.make_async_copy(source, held_ref, load_sems.at[t]))
        loads[t].start()
    for t, held_ref in enumerate(held_refs):
        loads[t].wait()
        for h in range(N2 // width):
            lanes = slice(h * width, (h + 1) * width)
            for r in range(rows):
                block = held_ref[r, lanes].astype(BF16).T.astype(F32)
                rows_ref[h, pl.ds(r, devices * per, stride=pitch), :] = block
            block = rows_ref[h].reshape(devices, per, pitch, width)[:, :, :rows].astype(BF16)
            ready_ref[t, :, :, :, lanes] = block
        stores.append(pltpu.make_async_copy(ready_ref.at[t], out_ref.at[:, t], store_sems.at[t]))
        stores[t].start()
    for store in stores:
        store.wait()


def outward(arrays, devices):
    _, rows, _, channels = arrays[0].shape
    count, per, width, pitch = len(arrays), channels // devices, 128, rows + 8
    shape = (devices, count, per, rows, N2)
    return pl.pallas_call(
        functools.partial(outward_kernel, count=count),
        in_specs=[pl.BlockSpec(memory_space=pl.ANY)] * count,
        out_specs=pl.BlockSpec(memory_space=pl.ANY),
        out_shape=pltpu.HBM(shape, BF16),
        scratch_shapes=[
            *[pltpu.VMEM(a.shape[1:], a.dtype) for a in arrays],
            pltpu.VMEM((N2 // width, channels * pitch, width), F32),
            pltpu.VMEM((count, devices, per, rows, N2), BF16),
            pltpu.SemaphoreType.DMA((count,)),
            pltpu.SemaphoreType.DMA((count,)),
        ],
        compiler_params=pltpu.CompilerParams(vmem_limit_bytes=VMEM),
        cost_estimate=pl.CostEstimate(flops=0, bytes_accessed=7 << 20, transcendentals=0),
        name="outward",
    )(*arrays)


def outward_near_kernel(in_ref, *refs, hops, plane):
    here = place(plane)
    *out_refs, rows_ref = refs
    _, per, rows, width = out_refs[0].shape
    channels = in_ref.shape[3]
    pitch = rows_ref.shape[0] // channels
    for r in range(rows):
        rows_ref[pl.ds(r, channels, stride=pitch), :] = in_ref[0, r].T.astype(F32)
    for j, out_ref in enumerate(out_refs):
        for hop in range(hops):
            block = owner(here, j, hop, plane) * (per * pitch)
            rows_here = rows_ref[pl.ds(pl.multiple_of(block, per * pitch), per * pitch), :]
            out_ref[hop] = rows_here.reshape(per, pitch, width)[:, :rows].astype(BF16)


def outward_near(x, count, hops, plane):
    _, rows, _, channels = x.shape
    per = channels // count
    width = 128
    return pl.pallas_call(
        functools.partial(outward_near_kernel, hops=hops, plane=plane),
        grid=(N2 // width,),
        in_specs=[pl.BlockSpec((1, rows, width, channels), lambda h: (0, 0, h, 0))],
        out_specs=[pl.BlockSpec((hops, per, rows, width), lambda h: (0, 0, 0, h))] * (count // hops),
        out_shape=[jax.ShapeDtypeStruct((hops, per, rows, N2), BF16)] * (count // hops),
        scratch_shapes=[pltpu.VMEM((channels * (rows + 8), width), F32)],
        compiler_params=pltpu.CompilerParams(vmem_limit_bytes=VMEM),
        cost_estimate=pl.CostEstimate(flops=0, bytes_accessed=2 << 20, transcendentals=0),
        name="outward_near",
    )(x)


def regroup_kernel(*refs, count):
    for i, in_ref in enumerate(refs[:count]):
        for j, out_ref in enumerate(refs[count:]):
            out_ref[i] = in_ref[j]


def regroup(arrays):
    hops, *block = arrays[0].shape
    return pl.pallas_call(
        functools.partial(regroup_kernel, count=len(arrays)),
        out_shape=[jax.ShapeDtypeStruct((len(arrays), *block), BF16)] * hops,
        compiler_params=pltpu.CompilerParams(vmem_limit_bytes=VMEM),
        cost_estimate=pl.CostEstimate(flops=0, bytes_accessed=2 << 20, transcendentals=0),
        name="regroup",
    )(*arrays)


def homeward_kernel(last_ref, *refs, per):
    *early_refs, y_ref, grad_ref, rows_ref = refs
    count, _, rows, _ = last_ref.shape
    hops = early_refs[0].shape[0]
    plane = count // hops // 2
    here = place(plane)
    width = rows_ref.shape[2]
    pitch = rows_ref.shape[1] // (count * per)
    h = pl.program_id(0)
    lanes = pl.ds(pl.multiple_of(h * width, width), width)
    lower = lax.axis_index("ctx") >= lax.axis_size("ctx") // 2
    row = lax.broadcasted_iota(jnp.int32, (width, width), 0)
    col = lax.broadcasted_iota(jnp.int32, (width, width), 1)
    turn = (col == jnp.where(lower, width - 1 - row, row)).astype(F32)
    turn = (turn * jnp.where(lower, (1 - 2 * h).astype(F32), 1.0)).astype(BF16)
    y_rows = rows_ref.at[0].reshape(count, per, pitch, width)
    grad_rows = rows_ref.at[1].reshape(count, per, pitch, width)
    for j, early_ref in enumerate(early_refs):
        for hop in range(hops):
            y_rows[owner(here, j, hop, plane), :EARLY, :rows] = early_ref[hop, :, :, lanes].astype(F32)
    y_rows[:, EARLY:, :rows] = last_ref[:, : per - EARLY, :, lanes].astype(F32)
    block = last_ref[:, per - EARLY :, :, lanes]
    grad_rows[:, :, :rows] = dot(block.reshape(count * per * rows, width), turn).reshape(block.shape)
    for r in range(rows):
        y_ref[r] = rows_ref[0, pl.ds(r, count * per, stride=pitch), :].astype(BF16).T
    for r in range(rows):
        target = jnp.where(lower, (rows - r) % rows, r)
        grad_ref[0, target] = rows_ref[1, pl.ds(r, count * per, stride=pitch), :].T


def homeward(last, early):
    count, slots, rows, _ = last.shape
    per = (slots + EARLY) // 2
    channels, width, pitch = count * per, 128, rows + 8
    return pl.pallas_call(
        functools.partial(homeward_kernel, per=per),
        grid=(N2 // width,),
        in_specs=[pl.BlockSpec(memory_space=pltpu.VMEM)] * (1 + len(early)),
        out_specs=[
            pl.BlockSpec((rows, width, channels), lambda h: (0, h, 0)),
            pl.BlockSpec((1, rows, width, channels), lambda h: (h, 0, 0, 0)),
        ],
        out_shape=[
            jax.ShapeDtypeStruct((rows, N2, channels), BF16),
            jax.ShapeDtypeStruct((2, rows, width, channels), F32),
        ],
        scratch_shapes=[pltpu.VMEM((2, channels * pitch, width), F32)],
        compiler_params=pltpu.CompilerParams(vmem_limit_bytes=VMEM),
        cost_estimate=pl.CostEstimate(flops=0, bytes_accessed=5 << 20, transcendentals=0),
        name="homeward",
    )(near(last), *[near(x) for x in early])


def by_channel_body(embeds, perturb, cotangent, filter_spectrum, skip_gain):
    dp, ctx = lax.axis_size("dp"), lax.axis_size("ctx")
    d, c = lax.axis_index("dp"), lax.axis_index("ctx")
    axes, order = ("dp", "ctx"), ("ctx", "dp")
    count = dp * ctx
    channels = embeds.shape[2]
    rows = N1 // ctx
    per = channels // count
    plane = 4
    hops = ctx // plane
    tabs = tables()

    def matrix(x):
        return far(x.reshape(1, rows, N2, channels))

    def exchange(x, mask):
        return lax.ppermute(x, axes, [(i, i ^ mask) for i in range(count)]) if mask else x

    first = outward([matrix(embeds), matrix(perturb), far(filter_spectrum)], count)
    received = lax.all_to_all(first, order, 0, 0, tiled=True).reshape(ctx, dp, 3, per, rows, N2)
    cots = outward_near(matrix(cotangent), count, hops, plane)
    cots = regroup([exchange(x, j // plane * ctx + j % plane) for j, x in enumerate(cots)])
    received = near(received)
    *early, late = cots
    late, received = lax.optimization_barrier((late, received))
    cots = [exchange(x, hop * plane) for hop, x in enumerate([*early, late])]
    gain = lax.dynamic_slice(skip_gain, ((c * dp + d) * per,), (per,))
    outs = conv_call(gain, received, tabs, plane)
    (send, *kept), early = outs[:-hops], outs[-hops:]
    early = [exchange(x, hop * plane) for hop, x in enumerate(early)]
    send = grad_call(received, kept, cots, send)
    send, *early = lax.optimization_barrier((send, *early))
    send, *early = lax.optimization_barrier((send, *regroup(early)))
    last = lax.all_to_all(send.reshape(count, *send.shape[2:]), order, 0, 0, tiled=True)
    early = [exchange(x, j // plane * ctx + j % plane) for j, x in enumerate(early)]
    y, grad = homeward(last, early)
    return y.reshape(1, rows * N2, channels), grad


def trig_table(period):
    row_ids = jnp.arange(period, dtype=jnp.int32)
    exponent = row_ids[:, None] * row_ids[None, :] % period
    phase_angle = exponent.astype(jnp.float32) * (two_pi / period)
    return (jnp.cos(phase_angle).astype(jnp.bfloat16), jnp.sin(phase_angle).astype(jnp.bfloat16))


def twiddle(row_first, row_count, col_first, col_count):
    row_ids = row_first + jnp.arange(row_count, dtype=jnp.int32)
    col_ids = col_first + jnp.arange(col_count, dtype=jnp.int32)
    exponent = row_ids[:, None] * col_ids[None, :] % (N1 * N2)
    phase_angle = exponent.astype(jnp.float32) * (two_pi / (N1 * N2))
    return (jnp.cos(phase_angle)[:, :, None], jnp.sin(phase_angle)[:, :, None])


def first_section(values, col_start):
    cos_table, sin_table = trig_table(N1)
    part_real = jnp.einsum("kn,snmc->skmc", cos_table, values, preferred_element_type=jnp.float32)
    part_imag = -jnp.einsum("kn,snmc->skmc", sin_table, values, preferred_element_type=jnp.float32)
    tw_cos, tw_sin = twiddle(0, N1, col_start, values.shape[2])
    out_real = part_real * tw_cos + part_imag * tw_sin
    out_imag = part_imag * tw_cos - part_real * tw_sin
    return jnp.stack([out_real, out_imag], 1).astype(jnp.bfloat16)


def second_section(section_rows):
    cos_table, sin_table = trig_table(N2)
    with_cos = jnp.einsum(
        "sprnc,kn->sprkc", section_rows, cos_table, preferred_element_type=jnp.float32
    )
    with_sin = jnp.einsum(
        "sprnc,kn->sprkc", section_rows, sin_table, preferred_element_type=jnp.float32
    )
    return jnp.stack([with_cos[:, 0] + with_sin[:, 1], with_cos[:, 1] - with_sin[:, 0]], 1)


def spectral_inverse(product, row_start):
    cos_table, sin_table = trig_table(N2)
    with_cos = jnp.einsum("sprkc,nk->sprnc", product, cos_table, preferred_element_type=jnp.float32)
    with_sin = jnp.einsum("sprkc,nk->sprnc", product, sin_table, preferred_element_type=jnp.float32)
    part_real = with_cos[:, 0] - with_sin[:, 1]
    part_imag = with_cos[:, 1] + with_sin[:, 0]
    tw_cos, tw_sin = twiddle(row_start, product.shape[2], 0, N2)
    out_real = part_real * tw_cos - part_imag * tw_sin
    out_imag = part_imag * tw_cos + part_real * tw_sin
    return jnp.stack([out_real, out_imag], 1).astype(jnp.bfloat16)


def column_inverse(mixed_cols):
    cos_table, sin_table = trig_table(N1)
    with_cos = jnp.einsum(
        "nk,skmc->snmc", cos_table, mixed_cols[:, 0], preferred_element_type=jnp.float32
    )
    with_sin = jnp.einsum(
        "nk,skmc->snmc", sin_table, mixed_cols[:, 1], preferred_element_type=jnp.float32
    )
    return ((with_cos - with_sin) * (1.0 / (N1 * N2))).astype(jnp.bfloat16)


def to_spectrum(section_cols):
    return second_section(
        lax.all_to_all(section_cols, "ctx", split_axis=2, concat_axis=3, tiled=True)
    )


def error_terms(signal, filtered, skip_gain, cotangent_view):
    signal_wide = signal.astype(jnp.float32)
    filtered_wide = lax.optimization_barrier(filtered).astype(jnp.float32)
    outputs = signal_wide * filtered_wide + skip_gain * signal_wide
    clean_y = outputs[0]
    smooth_gap = outputs[1] - clean_y
    err_clean = signal_wide[0] * (cotangent_view.astype(jnp.float32) - smart_weight * smooth_gap)
    err_shift = signal_wide[1] * (smart_weight * smooth_gap)
    return (clean_y, jnp.stack([err_clean, err_shift], 0).astype(jnp.bfloat16))


def body(embeds, perturb, cotangent, filter_spectrum, skip_gain):
    ctx_size = lax.axis_size("ctx")
    ctx_index = lax.axis_index("ctx")
    channels = embeds.shape[2]
    row_count = N1 // ctx_size
    col_count = N2 // ctx_size
    row_start = ctx_index * row_count
    col_start = ctx_index * col_count
    clean_rows = embeds[0].reshape(row_count, N2, channels)
    perturb_rows = perturb[0].reshape(row_count, N2, channels)
    shifted = (clean_rows.astype(jnp.float32) + perturb_rows.astype(jnp.float32)).astype(
        jnp.bfloat16
    )
    inputs = jnp.stack([clean_rows, shifted], 0)
    signal_cols = lax.all_to_all(inputs, "ctx", split_axis=2, concat_axis=1, tiled=True)
    section_cols, signal_cols = (first_section(signal_cols, col_start), signal_cols)
    spectra = to_spectrum(section_cols)
    filter_real = filter_spectrum[0]
    filter_imag = filter_spectrum[1]
    spectrum_real = spectra[:, 0]
    spectrum_imag = spectra[:, 1]
    product = jnp.stack(
        [
            filter_real * spectrum_real - filter_imag * spectrum_imag,
            filter_real * spectrum_imag + filter_imag * spectrum_real,
        ],
        1,
    ).astype(jnp.bfloat16)
    mixed_rows = spectral_inverse(product, row_start)
    filtered = column_inverse(
        lax.all_to_all(mixed_rows, "ctx", split_axis=3, concat_axis=2, tiled=True)
    )
    cotangent_rows = cotangent[0].reshape(row_count, N2, channels)
    filtered_rows = lax.all_to_all(filtered, "ctx", split_axis=1, concat_axis=2, tiled=True)
    clean_y, errors = error_terms(inputs, filtered_rows, skip_gain, cotangent_rows)
    clean_output = clean_y.astype(jnp.bfloat16)
    error_section = first_section(
        lax.all_to_all(errors, "ctx", split_axis=2, concat_axis=1, tiled=True), col_start
    )
    error_spec = to_spectrum(error_section)
    error_real = error_spec[:, 0]
    error_imag = error_spec[:, 1]
    term_real = error_real * spectrum_real + error_imag * spectrum_imag
    term_imag = error_imag * spectrum_real - error_real * spectrum_imag
    local_grad = jnp.stack([term_real[0] + term_real[1], term_imag[0] + term_imag[1]], 0) * (
        1.0 / (N1 * N2)
    )
    grad_shard = lax.psum_scatter(
        local_grad.astype(jnp.bfloat16), "dp", scatter_dimension=2, tiled=True
    ).astype(jnp.float32)
    return (clean_output.reshape(1, row_count * N2, channels), grad_shard)


def solution(mesh):
    dp, ctx = mesh.shape["dp"], mesh.shape["ctx"]

    def run(embeds, *rest):
        apart = dp == 2 and embeds.shape[2] % (dp * ctx) == 0 and N1 // ctx == 16 and embeds.shape[2] // (dp * ctx) > 1
        return jax.shard_map(
            by_channel_body if apart else body,
            mesh=mesh,
            in_specs=(
                P("dp", "ctx", None),
                P("dp", "ctx", None),
                P("dp", "ctx", None),
                P(None, "ctx", None, None),
                P(),
            ),
            out_specs=(P("dp", "ctx", None), P(None, "ctx", "dp", None)),
            check_vma=False,
        )(embeds, *rest)

    return run
```

```python
import functools

import jax
import jax.numpy as jnp
import numpy as np
from jax import lax
from jax.experimental import pallas as pl
from jax.experimental.pallas import tpu as pltpu
from jax.sharding import PartitionSpec as P

N1 = 256
N2 = 256
BF16 = jnp.bfloat16
F32 = jnp.float32
EARLY = 3
HALF = 144
VMEM = 26 << 20

two_pi = 6.283185307179586
smart_weight = 2.0


def tables():
    ids = np.arange(N1)
    phase = (ids[:, None] * ids[None, :] % N1) * (two_pi / N1)
    cos_table, sin_table = np.cos(phase), np.sin(phase)
    split_rows = np.concatenate([cos_table[:HALF], -sin_table[:HALF]], 0)
    forward_table = np.block([[cos_table, -sin_table], [sin_table, cos_table]])
    weight = np.where(ids[: N1 // 2] == 0, 1.0, 2.0) / (N1 * N2)
    join_rows = np.concatenate([cos_table[:, : N1 // 2] * weight, -sin_table[:, : N1 // 2] * weight], 1)
    mirror_rows = np.zeros((HALF, N1))
    mirror_rows[ids[:HALF], -ids[:HALF] % N1] = 1
    mirror_cols = np.eye(N2)[::-1]
    angle = (ids[:HALF, None] * ids[None, :]) * (two_pi / (N1 * N2))
    twiddle = np.stack([np.cos(angle), np.sin(angle)], 0)
    small = (split_rows, forward_table, join_rows, mirror_rows, mirror_cols)
    small = [jnp.asarray(t.astype(jnp.bfloat16)) for t in small]
    return (*small, jnp.asarray(twiddle.astype(np.float32)))


def dot(a, b):
    return jnp.dot(a, b, preferred_element_type=F32)


def place(plane):
    c = lax.axis_index("ctx")
    return lax.axis_index("dp"), c // plane, c % plane


def peer(here, j, hop, plane):
    return here[0] ^ (j // plane), (here[1] ^ hop) * plane + (here[2] ^ (j % plane))


def owner(here, j, hop, plane):
    d, c = peer(here, j, hop, plane)
    return c * lax.axis_size("dp") + d


def forward(signals, split_ref, fwd_ref, tw_cos, tw_sin):
    halves = []
    for x in signals:
        part = dot(split_ref[...], x)
        part_real, part_imag = part[:HALF], part[HALF:]
        out_real = part_real * tw_cos + part_imag * tw_sin
        out_imag = part_imag * tw_cos - part_real * tw_sin
        halves.append(jnp.concatenate([out_real.astype(BF16), out_imag.astype(BF16)], 1))
    spectra = dot(jnp.concatenate(halves, 0), fwd_ref[...])
    return [spectra[i * HALF : (i + 1) * HALF] for i in range(len(signals))]


def hermitian_part(filter_real, filter_imag, mirror_rows, mirror_cols):
    rows = dot(mirror_rows, jnp.concatenate([filter_real, filter_imag], 1)).astype(BF16)
    flipped = dot(jnp.concatenate([rows[:, :N2], rows[:, N2:]], 0), mirror_cols)
    out = []
    for part, other, sign in ((filter_real, flipped[:HALF], 0.5), (filter_imag, flipped[HALF:], -0.5)):
        top = other[:8]
        row = lax.broadcasted_iota(jnp.int32, top.shape, 0)
        top = jnp.where(row == 0, pltpu.roll(top, 1, 1), top)
        other = jnp.concatenate([top, other[8:]], 0)
        out.append(0.5 * part[:HALF].astype(F32) + sign * other)
    return out


def gradient(err_spectra, spectra):
    total_real = total_imag = 0.0
    for err_spec, spec in zip(err_spectra, spectra):
        err_real, err_imag = err_spec[:, :N2], err_spec[:, N2:]
        real, imag = spec[:, :N2], spec[:, N2:]
        total_real += err_real * real + err_imag * imag
        total_imag += err_imag * real - err_real * imag
    return total_real, total_imag


def conv_kernel(
    gain_ref, recv_ref, split_ref, fwd_ref, join_ref, mirror_ref, cols_ref, tw_ref,
    gap_ref, spec_ref, part_ref, *refs, early,
):
    *refs, y_rows = refs
    ctx, count = recv_ref.shape[:2]
    step = pl.program_id(0)
    q = step if early else step + EARLY
    if early:
        held_refs, early_refs = refs[:3], refs[3:]

        @pl.when(step == 0)
        def _():
            for held_ref, table_ref in zip(held_refs, (split_ref, fwd_ref, tw_ref)):
                held_ref[...] = table_ref[...]

    tw_cos, tw_sin = tw_ref[0], tw_ref[1]
    signals = []
    for d in range(count):
        clean = recv_ref[:, d, 0, q].reshape(N1, N2)
        perturb = recv_ref[:, d, 1, q].reshape(N1, N2)
        signals += [clean, (clean.astype(F32) + perturb.astype(F32)).astype(BF16)]
    spectra = forward(signals, split_ref, fwd_ref, tw_cos, tw_sin)
    filter_real, filter_imag = hermitian_part(
        recv_ref[:, 0, 2, q].reshape(N1, N2), recv_ref[:, 1, 2, q].reshape(N1, N2), mirror_ref[...], cols_ref[...]
    )
    products = []
    for spec in spectra:
        real, imag = spec[:, :N2], spec[:, N2:]
        prod_real = (filter_real * real - filter_imag * imag).astype(BF16)
        minus_imag = (-filter_real * imag - filter_imag * real).astype(BF16)
        products.append(jnp.concatenate([prod_real, minus_imag], 1))
    back = dot(jnp.concatenate(products, 0), fwd_ref[...])
    mixed, middle = [], []
    for i in range(2 * count):
        back_real, minus_imag = back[i * HALF : (i + 1) * HALF, :N2], back[i * HALF : (i + 1) * HALF, N2:]
        mixed_real = (back_real * tw_cos + minus_imag * tw_sin).astype(BF16)
        mixed_imag = (back_real * tw_sin - minus_imag * tw_cos).astype(BF16)
        mixed.append(jnp.concatenate([mixed_real[: N1 // 2], mixed_imag[: N1 // 2]], 0))
        middle.append(mixed_real[N1 // 2 :].astype(F32)[:1])
    conv = dot(join_ref[...], jnp.concatenate(mixed, 1))
    parity = lax.broadcasted_iota(jnp.int32, (N1, N2), 0) % 2
    alternate = (1 - 2 * parity).astype(F32) * (1.0 / (N1 * N2))
    gain = gain_ref[q]
    errors = []
    for d in range(count):
        pair = []
        for i in range(2):
            k = 2 * d + i
            wide = signals[k].astype(F32)
            filtered = conv[:, k * N2 : (k + 1) * N2] + alternate * middle[k]
            pair.append((wide, wide * filtered.astype(BF16).astype(F32) + gain * wide))
        (clean, clean_y), (shifted, shifted_y) = pair
        y_rows[d * ctx : (d + 1) * ctx] = clean_y.astype(BF16).reshape(ctx, -1, N2)
        gap = smart_weight * (shifted_y - clean_y)
        gap_ref[step, d] = gap
        spec_ref[step, d] = spectra[2 * d]
        errors.append((shifted * gap).astype(BF16))
    total_real, total_imag = gradient(forward(errors, split_ref, fwd_ref, tw_cos, tw_sin), spectra[1::2])
    part_ref[step, 0] = total_real
    part_ref[step, 1] = total_imag
    if early:
        near_count = early_refs[0].shape[0]
        here = place(near_count // count)
        for hop, early_ref in enumerate(early_refs):
            for j in range(near_count):
                side, block = peer(here, j, hop, near_count // count)
                early_ref[j, step] = y_rows[side * ctx + block]
    else:
        (send_ref,) = refs
        for d in range(count):
            send_ref[:, d, step] = y_rows[d * ctx : (d + 1) * ctx]


def grad_kernel(recv_ref, *refs, hops):
    first, second, refs = refs[:3], refs[3:6], refs[6:]
    cot_refs, refs = refs[:hops], refs[hops:]
    split_ref, fwd_ref, tw_ref, y_ref, send_ref, cot_rows, ready_ref, sems = refs
    copies = [pltpu.make_async_copy(y_ref, send_ref.at[:, :, pl.ds(0, y_ref.shape[2])], sems.at[0])]
    copies[0].start()
    ctx, count = recv_ref.shape[:2]
    near = cot_refs[0].shape[0]
    plane = near // count
    here = place(plane)
    per = recv_ref.shape[3]
    for hop, cot_ref in enumerate(cot_refs):
        for j in range(near):
            side, block = peer(here, j, hop, plane)
            cot_rows[side * ctx + block] = cot_ref[j]
    kept = [(first, q) if q < EARLY else (second, q - EARLY) for q in range(per)]
    errors = []
    for q, ((gap_ref, _, _), i) in enumerate(kept):
        for d in range(count):
            clean = recv_ref[:, d, 0, q].reshape(N1, N2).astype(F32)
            cot = cot_rows[d * ctx : (d + 1) * ctx, q].reshape(N1, N2).astype(F32)
            errors.append((clean * (cot - gap_ref[i, d])).astype(BF16))
    err_spectra = forward(errors, split_ref, fwd_ref, tw_ref[0], tw_ref[1])
    for q, ((_, spec_ref, part_ref), i) in enumerate(kept):
        spectra = [spec_ref[i, d] for d in range(count)]
        total = gradient(err_spectra[q * count : (q + 1) * count], spectra)
        fill_grad(ready_ref, q, *[t + part_ref[i, p] for p, t in enumerate(total)])
        copies.append(pltpu.make_async_copy(ready_ref.at[q], send_ref.at[:, :, per - EARLY + q], sems.at[1 + q]))
        copies[1 + q].start()
    for copy in copies:
        copy.wait()


def fill_grad(ready_ref, q, total_real, total_imag):
    _, ctx, count, rows, _ = ready_ref.shape
    total = jnp.concatenate([total_real, total_imag], 1) * (1.0 / (N1 * N2))
    upper, after = total[: N1 // 2], total[rows : N1 // 2 + rows]
    first = lax.broadcasted_iota(jnp.int32, upper.shape, 0) % rows == 0
    lower = jnp.where(first, after, upper).astype(BF16)
    upper = upper.astype(BF16)
    width = N2 // count
    for i in range(count):
        for half, x, side in ((0, upper, i), (1, lower, count - 1 - i)):
            cols = slice(side * width, (side + 1) * width)
            pair = jnp.concatenate([x[:, :N2][:, cols], x[:, N2:][:, cols]], 1)
            for block in range(ctx // 2):
                target = ctx - 1 - block if half else block
                ready_ref[q, target, i] = pair[block * rows : (block + 1) * rows]


def whole(x):
    return pl.BlockSpec(x.shape, lambda *_: (0,) * x.ndim)


def near(x):
    return pltpu.with_memory_space_constraint(x, pltpu.VMEM)


def far(x):
    return pltpu.with_memory_space_constraint(x, pltpu.HBM)


def conv_call(gain, received, tabs, plane, early):
    ctx, dp, _, per, rows, _ = received.shape
    split_rows, forward_table, *_, twiddle = tabs
    steps = EARLY if early else per - EARLY
    here = pl.BlockSpec(memory_space=pltpu.VMEM)
    if early:
        tabs, specs = [far(t) for t in tabs], [whole(t) for t in tabs]
        held = [pltpu.VMEM(t.shape, t.dtype) for t in (split_rows, forward_table, twiddle)]
        more = [*held, *[pltpu.VMEM((dp * plane, EARLY, rows, N2), BF16)] * (ctx // plane)]
    else:
        inside = (True, True, False, False, False, True)
        specs = [here if held else whole(t) for t, held in zip(tabs, inside)]
        tabs = [near(t) if held else far(t) for t, held in zip(tabs, inside)]
        more = [pltpu.VMEM((ctx, dp, steps, rows, N2), BF16)]
    return pl.pallas_call(
        functools.partial(conv_kernel, early=early),
        grid=(steps,),
        in_specs=[pl.BlockSpec(memory_space=pltpu.SMEM), here, *specs],
        out_specs=[here] * (3 + len(more)),
        out_shape=[
            pltpu.VMEM((steps, dp, N1, N2), F32),
            pltpu.VMEM((steps, dp, HALF, 2 * N2), F32),
            pltpu.VMEM((steps, 2, HALF, N2), F32),
            *more,
        ],
        scratch_shapes=[pltpu.VMEM((dp * ctx, rows, N2), BF16)],
        compiler_params=pltpu.CompilerParams(vmem_limit_bytes=VMEM),
        cost_estimate=pl.CostEstimate(flops=steps * dp * 5 * 6 * N1**3, bytes_accessed=4 << 20, transcendentals=0),
        name="conv_early" if early else "conv_late",
    )(gain, received, *tabs)


def grad_call(received, kept, cots, send):
    ctx, dp, _, per, rows, _ = received.shape
    *kept, split_rows, forward_table, twiddle = [near(x) for x in kept]
    operands = (received, *kept, *[near(x) for x in cots], split_rows, forward_table, twiddle, near(send))
    return pl.pallas_call(
        functools.partial(grad_kernel, hops=len(cots)),
        grid=(1,),
        in_specs=[pl.BlockSpec(memory_space=pltpu.VMEM)] * len(operands),
        out_specs=pl.BlockSpec(memory_space=pl.ANY),
        out_shape=pltpu.HBM((ctx, dp, 2 * per - EARLY, rows, N2), BF16),
        scratch_shapes=[
            pltpu.VMEM((dp * ctx, per, rows, N2), BF16),
            pltpu.VMEM((per, ctx, dp, rows, N2), BF16),
            pltpu.SemaphoreType.DMA((1 + per,)),
        ],
        compiler_params=pltpu.CompilerParams(vmem_limit_bytes=VMEM),
        cost_estimate=pl.CostEstimate(flops=per * dp * 6 * N1**3, bytes_accessed=8 << 20, transcendentals=0),
        name="grad",
    )(*operands)


def outward_kernel(*refs, count):
    in_refs, refs = refs[:count], refs[count:]
    out_ref, refs = refs[0], refs[1:]
    held_refs, (rows_ref, ready_ref, load_sems, store_sems) = refs[:count], refs[count:]
    devices, _, per, rows, _ = out_ref.shape
    pitch = rows_ref.shape[1] // (devices * per)
    width = rows_ref.shape[2]
    loads, stores = [], []
    for t, (in_ref, held_ref) in enumerate(zip(in_refs, held_refs)):
        source = in_ref.at[lax.axis_index("dp") if in_ref.shape[0] > 1 else 0]
        loads.append(pltpu.make_async_copy(source, held_ref, load_sems.at[t]))
        loads[t].start()
    for t, held_ref in enumerate(held_refs):
        loads[t].wait()
        for h in range(N2 // width):
            lanes = slice(h * width, (h + 1) * width)
            for r in range(rows):
                block = held_ref[r, lanes].astype(BF16).T.astype(F32)
                rows_ref[h, pl.ds(r, devices * per, stride=pitch), :] = block
            block = rows_ref[h].reshape(devices, per, pitch, width)[:, :, :rows].astype(BF16)
            ready_ref[t, :, :, :, lanes] = block
        stores.append(pltpu.make_async_copy(ready_ref.at[t], out_ref.at[:, t], store_sems.at[t]))
        stores[t].start()
    for store in stores:
        store.wait()


def outward(arrays, devices):
    _, rows, _, channels = arrays[0].shape
    count, per, width, pitch = len(arrays), channels // devices, 128, rows + 8
    shape = (devices, count, per, rows, N2)
    return pl.pallas_call(
        functools.partial(outward_kernel, count=count),
        in_specs=[pl.BlockSpec(memory_space=pl.ANY)] * count,
        out_specs=pl.BlockSpec(memory_space=pl.ANY),
        out_shape=pltpu.HBM(shape, BF16),
        scratch_shapes=[
            *[pltpu.VMEM(a.shape[1:], a.dtype) for a in arrays],
            pltpu.VMEM((N2 // width, channels * pitch, width), F32),
            pltpu.VMEM((count, devices, per, rows, N2), BF16),
            pltpu.SemaphoreType.DMA((count,)),
            pltpu.SemaphoreType.DMA((count,)),
        ],
        compiler_params=pltpu.CompilerParams(vmem_limit_bytes=VMEM),
        cost_estimate=pl.CostEstimate(flops=0, bytes_accessed=7 << 20, transcendentals=0),
        name="outward",
    )(*arrays)


def outward_near_kernel(in_ref, *refs, hops, plane):
    here = place(plane)
    *out_refs, rows_ref = refs
    _, per, rows, width = out_refs[0].shape
    channels = in_ref.shape[3]
    pitch = rows_ref.shape[0] // channels
    for r in range(rows):
        rows_ref[pl.ds(r, channels, stride=pitch), :] = in_ref[0, r].T.astype(F32)
    for j, out_ref in enumerate(out_refs):
        for hop in range(hops):
            block = owner(here, j, hop, plane) * (per * pitch)
            rows_here = rows_ref[pl.ds(pl.multiple_of(block, per * pitch), per * pitch), :]
            out_ref[hop] = rows_here.reshape(per, pitch, width)[:, :rows].astype(BF16)


def outward_near(x, count, hops, plane):
    _, rows, _, channels = x.shape
    per = channels // count
    width = 128
    return pl.pallas_call(
        functools.partial(outward_near_kernel, hops=hops, plane=plane),
        grid=(N2 // width,),
        in_specs=[pl.BlockSpec((1, rows, width, channels), lambda h: (0, 0, h, 0))],
        out_specs=[pl.BlockSpec((hops, per, rows, width), lambda h: (0, 0, 0, h))] * (count // hops),
        out_shape=[jax.ShapeDtypeStruct((hops, per, rows, N2), BF16)] * (count // hops),
        scratch_shapes=[pltpu.VMEM((channels * (rows + 8), width), F32)],
        compiler_params=pltpu.CompilerParams(vmem_limit_bytes=VMEM),
        cost_estimate=pl.CostEstimate(flops=0, bytes_accessed=2 << 20, transcendentals=0),
        name="outward_near",
    )(x)


def regroup_kernel(*refs, count):
    for i, in_ref in enumerate(refs[:count]):
        for j, out_ref in enumerate(refs[count:]):
            out_ref[i] = in_ref[j]


def regroup(arrays):
    hops, *block = arrays[0].shape
    return pl.pallas_call(
        functools.partial(regroup_kernel, count=len(arrays)),
        out_shape=[jax.ShapeDtypeStruct((len(arrays), *block), BF16)] * hops,
        compiler_params=pltpu.CompilerParams(vmem_limit_bytes=VMEM),
        cost_estimate=pl.CostEstimate(flops=0, bytes_accessed=2 << 20, transcendentals=0),
        name="regroup",
    )(*arrays)


def homeward_kernel(last_ref, *refs, per):
    *early_refs, y_ref, grad_ref, rows_ref = refs
    count, _, rows, _ = last_ref.shape
    hops = early_refs[0].shape[0]
    plane = count // hops // 2
    here = place(plane)
    width = rows_ref.shape[2]
    pitch = rows_ref.shape[1] // (count * per)
    h = pl.program_id(0)
    lanes = pl.ds(pl.multiple_of(h * width, width), width)
    lower = lax.axis_index("ctx") >= lax.axis_size("ctx") // 2
    row = lax.broadcasted_iota(jnp.int32, (width, width), 0)
    col = lax.broadcasted_iota(jnp.int32, (width, width), 1)
    turn = (col == jnp.where(lower, width - 1 - row, row)).astype(F32)
    turn = (turn * jnp.where(lower, (1 - 2 * h).astype(F32), 1.0)).astype(BF16)
    y_rows = rows_ref.at[0].reshape(count, per, pitch, width)
    grad_rows = rows_ref.at[1].reshape(count, per, pitch, width)
    for j, early_ref in enumerate(early_refs):
        for hop in range(hops):
            y_rows[owner(here, j, hop, plane), :EARLY, :rows] = early_ref[hop, :, :, lanes].astype(F32)
    y_rows[:, EARLY:, :rows] = last_ref[:, : per - EARLY, :, lanes].astype(F32)
    block = last_ref[:, per - EARLY :, :, lanes]
    grad_rows[:, :, :rows] = dot(block.reshape(count * per * rows, width), turn).reshape(block.shape)
    for r in range(rows):
        y_ref[r] = rows_ref[0, pl.ds(r, count * per, stride=pitch), :].astype(BF16).T
    for r in range(rows):
        target = jnp.where(lower, (rows - r) % rows, r)
        grad_ref[0, target] = rows_ref[1, pl.ds(r, count * per, stride=pitch), :].T


def homeward(last, early):
    count, slots, rows, _ = last.shape
    per = (slots + EARLY) // 2
    channels, width, pitch = count * per, 128, rows + 8
    return pl.pallas_call(
        functools.partial(homeward_kernel, per=per),
        grid=(N2 // width,),
        in_specs=[pl.BlockSpec(memory_space=pltpu.VMEM)] * (1 + len(early)),
        out_specs=[
            pl.BlockSpec((rows, width, channels), lambda h: (0, h, 0)),
            pl.BlockSpec((1, rows, width, channels), lambda h: (h, 0, 0, 0)),
        ],
        out_shape=[
            jax.ShapeDtypeStruct((rows, N2, channels), BF16),
            jax.ShapeDtypeStruct((2, rows, width, channels), F32),
        ],
        scratch_shapes=[pltpu.VMEM((2, channels * pitch, width), F32)],
        compiler_params=pltpu.CompilerParams(vmem_limit_bytes=VMEM),
        cost_estimate=pl.CostEstimate(flops=0, bytes_accessed=5 << 20, transcendentals=0),
        name="homeward",
    )(near(last), *[near(x) for x in early])


def by_channel_body(embeds, perturb, cotangent, filter_spectrum, skip_gain):
    dp, ctx = lax.axis_size("dp"), lax.axis_size("ctx")
    d, c = lax.axis_index("dp"), lax.axis_index("ctx")
    axes, order = ("dp", "ctx"), ("ctx", "dp")
    count = dp * ctx
    channels = embeds.shape[2]
    rows = N1 // ctx
    per = channels // count
    plane = 4
    hops = ctx // plane
    tabs = tables()

    def matrix(x):
        return far(x.reshape(1, rows, N2, channels))

    def exchange(x, mask):
        return lax.ppermute(x, axes, [(i, i ^ mask) for i in range(count)]) if mask else x

    first = outward([matrix(embeds), matrix(perturb), far(filter_spectrum)], count)
    received = lax.all_to_all(first, order, 0, 0, tiled=True).reshape(ctx, dp, 3, per, rows, N2)
    cots = outward_near(matrix(cotangent), count, hops, plane)
    cots = regroup([exchange(x, j // plane * ctx + j % plane) for j, x in enumerate(cots)])
    received = near(received)
    *early, late = cots
    late, received = lax.optimization_barrier((late, received))
    cots = [exchange(x, hop * plane) for hop, x in enumerate([*early, late])]
    gain = lax.dynamic_slice(skip_gain, ((c * dp + d) * per,), (per,))
    outs = conv_call(gain, received, tabs, plane, True)
    kept, held, early = outs[:3], outs[3:6], outs[6:]
    early = [exchange(x, hop * plane) for hop, x in enumerate(early)]
    *kept_late, send = conv_call(gain, received, [*held[:2], *tabs[2:5], held[2]], plane, False)
    send = grad_call(received, [*kept, *kept_late, *held], cots, send)
    send, *early = lax.optimization_barrier((send, *early))
    send, *early = lax.optimization_barrier((send, *regroup(early)))
    last = lax.all_to_all(send.reshape(count, *send.shape[2:]), order, 0, 0, tiled=True)
    early = [exchange(x, j // plane * ctx + j % plane) for j, x in enumerate(early)]
    y, grad = homeward(last, early)
    return y.reshape(1, rows * N2, channels), grad


def trig_table(period):
    row_ids = jnp.arange(period, dtype=jnp.int32)
    exponent = row_ids[:, None] * row_ids[None, :] % period
    phase_angle = exponent.astype(jnp.float32) * (two_pi / period)
    return (jnp.cos(phase_angle).astype(jnp.bfloat16), jnp.sin(phase_angle).astype(jnp.bfloat16))


def twiddle(row_first, row_count, col_first, col_count):
    row_ids = row_first + jnp.arange(row_count, dtype=jnp.int32)
    col_ids = col_first + jnp.arange(col_count, dtype=jnp.int32)
    exponent = row_ids[:, None] * col_ids[None, :] % (N1 * N2)
    phase_angle = exponent.astype(jnp.float32) * (two_pi / (N1 * N2))
    return (jnp.cos(phase_angle)[:, :, None], jnp.sin(phase_angle)[:, :, None])


def first_section(values, col_start):
    cos_table, sin_table = trig_table(N1)
    part_real = jnp.einsum("kn,snmc->skmc", cos_table, values, preferred_element_type=jnp.float32)
    part_imag = -jnp.einsum("kn,snmc->skmc", sin_table, values, preferred_element_type=jnp.float32)
    tw_cos, tw_sin = twiddle(0, N1, col_start, values.shape[2])
    out_real = part_real * tw_cos + part_imag * tw_sin
    out_imag = part_imag * tw_cos - part_real * tw_sin
    return jnp.stack([out_real, out_imag], 1).astype(jnp.bfloat16)


def second_section(section_rows):
    cos_table, sin_table = trig_table(N2)
    with_cos = jnp.einsum(
        "sprnc,kn->sprkc", section_rows, cos_table, preferred_element_type=jnp.float32
    )
    with_sin = jnp.einsum(
        "sprnc,kn->sprkc", section_rows, sin_table, preferred_element_type=jnp.float32
    )
    return jnp.stack([with_cos[:, 0] + with_sin[:, 1], with_cos[:, 1] - with_sin[:, 0]], 1)


def spectral_inverse(product, row_start):
    cos_table, sin_table = trig_table(N2)
    with_cos = jnp.einsum("sprkc,nk->sprnc", product, cos_table, preferred_element_type=jnp.float32)
    with_sin = jnp.einsum("sprkc,nk->sprnc", product, sin_table, preferred_element_type=jnp.float32)
    part_real = with_cos[:, 0] - with_sin[:, 1]
    part_imag = with_cos[:, 1] + with_sin[:, 0]
    tw_cos, tw_sin = twiddle(row_start, product.shape[2], 0, N2)
    out_real = part_real * tw_cos - part_imag * tw_sin
    out_imag = part_imag * tw_cos + part_real * tw_sin
    return jnp.stack([out_real, out_imag], 1).astype(jnp.bfloat16)


def column_inverse(mixed_cols):
    cos_table, sin_table = trig_table(N1)
    with_cos = jnp.einsum(
        "nk,skmc->snmc", cos_table, mixed_cols[:, 0], preferred_element_type=jnp.float32
    )
    with_sin = jnp.einsum(
        "nk,skmc->snmc", sin_table, mixed_cols[:, 1], preferred_element_type=jnp.float32
    )
    return ((with_cos - with_sin) * (1.0 / (N1 * N2))).astype(jnp.bfloat16)


def to_spectrum(section_cols):
    return second_section(
        lax.all_to_all(section_cols, "ctx", split_axis=2, concat_axis=3, tiled=True)
    )


def error_terms(signal, filtered, skip_gain, cotangent_view):
    signal_wide = signal.astype(jnp.float32)
    filtered_wide = lax.optimization_barrier(filtered).astype(jnp.float32)
    outputs = signal_wide * filtered_wide + skip_gain * signal_wide
    clean_y = outputs[0]
    smooth_gap = outputs[1] - clean_y
    err_clean = signal_wide[0] * (cotangent_view.astype(jnp.float32) - smart_weight * smooth_gap)
    err_shift = signal_wide[1] * (smart_weight * smooth_gap)
    return (clean_y, jnp.stack([err_clean, err_shift], 0).astype(jnp.bfloat16))


def body(embeds, perturb, cotangent, filter_spectrum, skip_gain):
    ctx_size = lax.axis_size("ctx")
    ctx_index = lax.axis_index("ctx")
    channels = embeds.shape[2]
    row_count = N1 // ctx_size
    col_count = N2 // ctx_size
    row_start = ctx_index * row_count
    col_start = ctx_index * col_count
    clean_rows = embeds[0].reshape(row_count, N2, channels)
    perturb_rows = perturb[0].reshape(row_count, N2, channels)
    shifted = (clean_rows.astype(jnp.float32) + perturb_rows.astype(jnp.float32)).astype(
        jnp.bfloat16
    )
    inputs = jnp.stack([clean_rows, shifted], 0)
    signal_cols = lax.all_to_all(inputs, "ctx", split_axis=2, concat_axis=1, tiled=True)
    section_cols, signal_cols = (first_section(signal_cols, col_start), signal_cols)
    spectra = to_spectrum(section_cols)
    filter_real = filter_spectrum[0]
    filter_imag = filter_spectrum[1]
    spectrum_real = spectra[:, 0]
    spectrum_imag = spectra[:, 1]
    product = jnp.stack(
        [
            filter_real * spectrum_real - filter_imag * spectrum_imag,
            filter_real * spectrum_imag + filter_imag * spectrum_real,
        ],
        1,
    ).astype(jnp.bfloat16)
    mixed_rows = spectral_inverse(product, row_start)
    filtered = column_inverse(
        lax.all_to_all(mixed_rows, "ctx", split_axis=3, concat_axis=2, tiled=True)
    )
    cotangent_rows = cotangent[0].reshape(row_count, N2, channels)
    filtered_rows = lax.all_to_all(filtered, "ctx", split_axis=1, concat_axis=2, tiled=True)
    clean_y, errors = error_terms(inputs, filtered_rows, skip_gain, cotangent_rows)
    clean_output = clean_y.astype(jnp.bfloat16)
    error_section = first_section(
        lax.all_to_all(errors, "ctx", split_axis=2, concat_axis=1, tiled=True), col_start
    )
    error_spec = to_spectrum(error_section)
    error_real = error_spec[:, 0]
    error_imag = error_spec[:, 1]
    term_real = error_real * spectrum_real + error_imag * spectrum_imag
    term_imag = error_imag * spectrum_real - error_real * spectrum_imag
    local_grad = jnp.stack([term_real[0] + term_real[1], term_imag[0] + term_imag[1]], 0) * (
        1.0 / (N1 * N2)
    )
    grad_shard = lax.psum_scatter(
        local_grad.astype(jnp.bfloat16), "dp", scatter_dimension=2, tiled=True
    ).astype(jnp.float32)
    return (clean_output.reshape(1, row_count * N2, channels), grad_shard)


def solution(mesh):
    dp, ctx = mesh.shape["dp"], mesh.shape["ctx"]

    def run(embeds, *rest):
        apart = dp == 2 and embeds.shape[2] % (dp * ctx) == 0 and N1 // ctx == 16 and embeds.shape[2] // (dp * ctx) > 1
        return jax.shard_map(
            by_channel_body if apart else body,
            mesh=mesh,
            in_specs=(
                P("dp", "ctx", None),
                P("dp", "ctx", None),
                P("dp", "ctx", None),
                P(None, "ctx", None, None),
                P(),
            ),
            out_specs=(P("dp", "ctx", None), P(None, "ctx", "dp", None)),
            check_vma=False,
        )(embeds, *rest)

    return run
```

```python
import functools

import jax
import jax.numpy as jnp
import numpy as np
from jax import lax
from jax.experimental import pallas as pl
from jax.experimental.pallas import tpu as pltpu
from jax.sharding import PartitionSpec as P

N1 = 256
N2 = 256
BF16 = jnp.bfloat16
F32 = jnp.float32
EARLY = 3
HALF = 144
VMEM = 26 << 20

two_pi = 6.283185307179586
smart_weight = 2.0


def tables():
    ids = np.arange(N1)
    phase = (ids[:, None] * ids[None, :] % N1) * (two_pi / N1)
    cos_table, sin_table = np.cos(phase), np.sin(phase)
    split_rows = np.concatenate([cos_table[:HALF], -sin_table[:HALF]], 0)
    forward_table = np.block([[cos_table, -sin_table], [sin_table, cos_table]])
    weight = np.where(ids[: N1 // 2] == 0, 1.0, 2.0) / (N1 * N2)
    join_rows = np.concatenate([cos_table[:, : N1 // 2] * weight, -sin_table[:, : N1 // 2] * weight], 1)
    mirror_rows = np.zeros((HALF, N1))
    mirror_rows[ids[:HALF], -ids[:HALF] % N1] = 1
    mirror_cols = np.eye(N2)[::-1]
    angle = (ids[:HALF, None] * ids[None, :]) * (two_pi / (N1 * N2))
    twiddle = np.stack([np.cos(angle), np.sin(angle)], 0)
    small = (split_rows, forward_table, join_rows, mirror_rows, mirror_cols)
    small = [jnp.asarray(t.astype(jnp.bfloat16)) for t in small]
    return (*small, jnp.asarray(twiddle.astype(np.float32)))


def dot(a, b):
    return jnp.dot(a, b, preferred_element_type=F32)


def place(plane):
    c = lax.axis_index("ctx")
    return lax.axis_index("dp"), c // plane, c % plane


def peer(here, j, hop, plane):
    return here[0] ^ (j // plane), (here[1] ^ hop) * plane + (here[2] ^ (j % plane))


def owner(here, j, hop, plane):
    d, c = peer(here, j, hop, plane)
    return c * lax.axis_size("dp") + d


def forward(signals, split_ref, fwd_ref, tw_cos, tw_sin):
    halves = []
    for x in signals:
        part = dot(split_ref[...], x)
        part_real, part_imag = part[:HALF], part[HALF:]
        out_real = part_real * tw_cos + part_imag * tw_sin
        out_imag = part_imag * tw_cos - part_real * tw_sin
        halves.append(jnp.concatenate([out_real.astype(BF16), out_imag.astype(BF16)], 1))
    spectra = dot(jnp.concatenate(halves, 0), fwd_ref[...])
    return [spectra[i * HALF : (i + 1) * HALF] for i in range(len(signals))]


def hermitian_part(filter_real, filter_imag, mirror_rows, mirror_cols):
    rows = dot(mirror_rows, jnp.concatenate([filter_real, filter_imag], 1)).astype(BF16)
    flipped = dot(jnp.concatenate([rows[:, :N2], rows[:, N2:]], 0), mirror_cols)
    out = []
    for part, other, sign in ((filter_real, flipped[:HALF], 0.5), (filter_imag, flipped[HALF:], -0.5)):
        top = other[:8]
        row = lax.broadcasted_iota(jnp.int32, top.shape, 0)
        top = jnp.where(row == 0, pltpu.roll(top, 1, 1), top)
        other = jnp.concatenate([top, other[8:]], 0)
        out.append(0.5 * part[:HALF].astype(F32) + sign * other)
    return out


def gradient(err_spectra, spectra):
    total_real = total_imag = 0.0
    for err_spec, spec in zip(err_spectra, spectra):
        err_real, err_imag = err_spec[:, :N2], err_spec[:, N2:]
        real, imag = spec[:, :N2], spec[:, N2:]
        total_real += err_real * real + err_imag * imag
        total_imag += err_imag * real - err_real * imag
    return total_real, total_imag


def conv_kernel(
    gain_ref, recv_ref, split_ref, fwd_ref, join_ref, mirror_ref, cols_ref, tw_ref,
    gap_ref, spec_ref, part_ref, *refs, early,
):
    *refs, y_rows = refs
    ctx, count = recv_ref.shape[:2]
    step = pl.program_id(0)
    q = step if early else step + EARLY
    if early:
        held_refs, early_refs = refs[:3], refs[3:]

        @pl.when(step == 0)
        def _():
            for held_ref, table_ref in zip(held_refs, (split_ref, fwd_ref, tw_ref)):
                held_ref[...] = table_ref[...]

    tw_cos, tw_sin = tw_ref[0], tw_ref[1]
    signals = []
    for d in range(count):
        clean = recv_ref[:, d, 0, q].reshape(N1, N2)
        perturb = recv_ref[:, d, 1, q].reshape(N1, N2)
        signals += [clean, (clean.astype(F32) + perturb.astype(F32)).astype(BF16)]
    spectra = forward(signals, split_ref, fwd_ref, tw_cos, tw_sin)
    filter_real, filter_imag = hermitian_part(
        recv_ref[:, 0, 2, q].reshape(N1, N2), recv_ref[:, 1, 2, q].reshape(N1, N2), mirror_ref[...], cols_ref[...]
    )
    products = []
    for spec in spectra:
        real, imag = spec[:, :N2], spec[:, N2:]
        prod_real = (filter_real * real - filter_imag * imag).astype(BF16)
        minus_imag = (-filter_real * imag - filter_imag * real).astype(BF16)
        products.append(jnp.concatenate([prod_real, minus_imag], 1))
    back = dot(jnp.concatenate(products, 0), fwd_ref[...])
    mixed, middle = [], []
    for i in range(2 * count):
        back_real, minus_imag = back[i * HALF : (i + 1) * HALF, :N2], back[i * HALF : (i + 1) * HALF, N2:]
        mixed_real = (back_real * tw_cos + minus_imag * tw_sin).astype(BF16)
        mixed_imag = (back_real * tw_sin - minus_imag * tw_cos).astype(BF16)
        mixed.append(jnp.concatenate([mixed_real[: N1 // 2], mixed_imag[: N1 // 2]], 0))
        middle.append(mixed_real[N1 // 2 :].astype(F32)[:1])
    conv = dot(join_ref[...], jnp.concatenate(mixed, 1))
    parity = lax.broadcasted_iota(jnp.int32, (N1, N2), 0) % 2
    alternate = (1 - 2 * parity).astype(F32) * (1.0 / (N1 * N2))
    gain = gain_ref[q]
    errors = []
    for d in range(count):
        pair = []
        for i in range(2):
            k = 2 * d + i
            wide = signals[k].astype(F32)
            filtered = conv[:, k * N2 : (k + 1) * N2] + alternate * middle[k]
            pair.append((wide, wide * filtered.astype(BF16).astype(F32) + gain * wide))
        (clean, clean_y), (shifted, shifted_y) = pair
        y_rows[d * ctx : (d + 1) * ctx] = clean_y.astype(BF16).reshape(ctx, -1, N2)
        gap = smart_weight * (shifted_y - clean_y)
        gap_ref[step, d] = gap
        spec_ref[step, d] = spectra[2 * d]
        errors.append((shifted * gap).astype(BF16))
    total_real, total_imag = gradient(forward(errors, split_ref, fwd_ref, tw_cos, tw_sin), spectra[1::2])
    part_ref[step, 0] = total_real
    part_ref[step, 1] = total_imag
    if early:
        near_count = early_refs[0].shape[0]
        here = place(near_count // count)
        for hop, early_ref in enumerate(early_refs):
            for j in range(near_count):
                side, block = peer(here, j, hop, near_count // count)
                early_ref[j, step] = y_rows[side * ctx + block]
    else:
        (send_ref,) = refs
        for d in range(count):
            send_ref[:, d, step] = y_rows[d * ctx : (d + 1) * ctx]


def grad_kernel(recv_ref, *refs, hops):
    first, second, refs = refs[:3], refs[3:6], refs[6:]
    cot_refs, refs = refs[:hops], refs[hops:]
    split_ref, fwd_ref, tw_ref, y_ref, send_ref, cot_rows, ready_ref, sems = refs
    copies = [pltpu.make_async_copy(y_ref, send_ref.at[:, :, pl.ds(0, y_ref.shape[2])], sems.at[0])]
    copies[0].start()
    ctx, count = recv_ref.shape[:2]
    near = cot_refs[0].shape[0]
    plane = near // count
    here = place(plane)
    per = recv_ref.shape[3]
    for hop, cot_ref in enumerate(cot_refs):
        for j in range(near):
            side, block = peer(here, j, hop, plane)
            cot_rows[side * ctx + block] = cot_ref[j]
    kept = [(first, q) if q < EARLY else (second, q - EARLY) for q in range(per)]
    errors = []
    for q, ((gap_ref, _, _), i) in enumerate(kept):
        for d in range(count):
            clean = recv_ref[:, d, 0, q].reshape(N1, N2).astype(F32)
            cot = cot_rows[d * ctx : (d + 1) * ctx, q].reshape(N1, N2).astype(F32)
            errors.append((clean * (cot - gap_ref[i, d])).astype(BF16))
    err_spectra = forward(errors, split_ref, fwd_ref, tw_ref[0], tw_ref[1])
    for q, ((_, spec_ref, part_ref), i) in enumerate(kept):
        spectra = [spec_ref[i, d] for d in range(count)]
        total = gradient(err_spectra[q * count : (q + 1) * count], spectra)
        fill_grad(ready_ref, q, *[t + part_ref[i, p] for p, t in enumerate(total)])
        copies.append(pltpu.make_async_copy(ready_ref.at[q], send_ref.at[:, :, per - EARLY + q], sems.at[1 + q]))
        copies[1 + q].start()
    for copy in copies:
        copy.wait()


def fill_grad(ready_ref, q, total_real, total_imag):
    _, ctx, count, rows, _ = ready_ref.shape
    total = jnp.concatenate([total_real, total_imag], 1) * (1.0 / (N1 * N2))
    upper, after = total[: N1 // 2], total[rows : N1 // 2 + rows]
    first = lax.broadcasted_iota(jnp.int32, upper.shape, 0) % rows == 0
    lower = jnp.where(first, after, upper).astype(BF16)
    upper = upper.astype(BF16)
    width = N2 // count
    for i in range(count):
        for half, x, side in ((0, upper, i), (1, lower, count - 1 - i)):
            cols = slice(side * width, (side + 1) * width)
            pair = jnp.concatenate([x[:, :N2][:, cols], x[:, N2:][:, cols]], 1)
            for block in range(ctx // 2):
                target = ctx - 1 - block if half else block
                ready_ref[q, target, i] = pair[block * rows : (block + 1) * rows]


def whole(x):
    return pl.BlockSpec(x.shape, lambda *_: (0,) * x.ndim)


def near(x):
    return pltpu.with_memory_space_constraint(x, pltpu.VMEM)


def far(x):
    return pltpu.with_memory_space_constraint(x, pltpu.HBM)


def conv_call(gain, received, tabs, plane, early):
    ctx, dp, _, per, rows, _ = received.shape
    split_rows, forward_table, *_, twiddle = tabs
    steps = EARLY if early else per - EARLY
    here = pl.BlockSpec(memory_space=pltpu.VMEM)
    if early:
        tabs, specs = [far(t) for t in tabs], [whole(t) for t in tabs]
        held = [pltpu.VMEM(t.shape, t.dtype) for t in (split_rows, forward_table, twiddle)]
        more = [*held, *[pltpu.VMEM((dp * plane, EARLY, rows, N2), BF16)] * (ctx // plane)]
    else:
        inside = (True, True, False, False, False, True)
        specs = [here if held else whole(t) for t, held in zip(tabs, inside)]
        tabs = [near(t) if held else far(t) for t, held in zip(tabs, inside)]
        more = [pltpu.VMEM((ctx, dp, steps, rows, N2), BF16)]
    return pl.pallas_call(
        functools.partial(conv_kernel, early=early),
        grid=(steps,),
        in_specs=[pl.BlockSpec(memory_space=pltpu.SMEM), here, *specs],
        out_specs=[here] * (3 + len(more)),
        out_shape=[
            pltpu.VMEM((steps, dp, N1, N2), F32),
            pltpu.VMEM((steps, dp, HALF, 2 * N2), F32),
            pltpu.VMEM((steps, 2, HALF, N2), F32),
            *more,
        ],
        scratch_shapes=[pltpu.VMEM((dp * ctx, rows, N2), BF16)],
        compiler_params=pltpu.CompilerParams(vmem_limit_bytes=VMEM),
        cost_estimate=pl.CostEstimate(flops=steps * dp * 5 * 6 * N1**3, bytes_accessed=4 << 20, transcendentals=0),
        name="conv_early" if early else "conv_late",
    )(gain, received, *tabs)


def grad_call(received, kept, cots, send):
    ctx, dp, _, per, rows, _ = received.shape
    *kept, split_rows, forward_table, twiddle = [near(x) for x in kept]
    operands = (received, *kept, *[near(x) for x in cots], split_rows, forward_table, twiddle, near(send))
    return pl.pallas_call(
        functools.partial(grad_kernel, hops=len(cots)),
        grid=(1,),
        in_specs=[pl.BlockSpec(memory_space=pltpu.VMEM)] * len(operands),
        out_specs=pl.BlockSpec(memory_space=pl.ANY),
        out_shape=pltpu.HBM((ctx, dp, 2 * per - EARLY, rows, N2), BF16),
        scratch_shapes=[
            pltpu.VMEM((dp * ctx, per, rows, N2), BF16),
            pltpu.VMEM((per, ctx, dp, rows, N2), BF16),
            pltpu.SemaphoreType.DMA((1 + per,)),
        ],
        compiler_params=pltpu.CompilerParams(vmem_limit_bytes=VMEM),
        cost_estimate=pl.CostEstimate(flops=per * dp * 6 * N1**3, bytes_accessed=8 << 20, transcendentals=0),
        name="grad",
    )(*operands)


def outward_kernel(*refs, count):
    in_refs, refs = refs[:count], refs[count:]
    out_ref, refs = refs[0], refs[1:]
    held_refs, (rows_ref, ready_ref, load_sems, store_sems) = refs[:count], refs[count:]
    devices, _, per, rows, _ = out_ref.shape
    pitch = rows_ref.shape[1] // (devices * per)
    width = rows_ref.shape[2]
    loads, stores = [], []
    for t, (in_ref, held_ref) in enumerate(zip(in_refs, held_refs)):
        source = in_ref.at[lax.axis_index("dp") if in_ref.shape[0] > 1 else 0]
        loads.append(pltpu.make_async_copy(source, held_ref, load_sems.at[t]))
        loads[t].start()
    for t, held_ref in enumerate(held_refs):
        loads[t].wait()
        for h in range(N2 // width):
            lanes = slice(h * width, (h + 1) * width)
            for r in range(rows):
                block = held_ref[r, lanes].astype(BF16).T.astype(F32)
                rows_ref[h, pl.ds(r, devices * per, stride=pitch), :] = block
            block = rows_ref[h].reshape(devices, per, pitch, width)[:, :, :rows].astype(BF16)
            ready_ref[t, :, :, :, lanes] = block
        stores.append(pltpu.make_async_copy(ready_ref.at[t], out_ref.at[:, t], store_sems.at[t]))
        stores[t].start()
    for store in stores:
        store.wait()


def outward(arrays, devices):
    _, rows, _, channels = arrays[0].shape
    count, per, width, pitch = len(arrays), channels // devices, 128, rows + 8
    shape = (devices, count, per, rows, N2)
    return pl.pallas_call(
        functools.partial(outward_kernel, count=count),
        in_specs=[pl.BlockSpec(memory_space=pl.ANY)] * count,
        out_specs=pl.BlockSpec(memory_space=pl.ANY),
        out_shape=pltpu.HBM(shape, BF16),
        scratch_shapes=[
            *[pltpu.VMEM(a.shape[1:], a.dtype) for a in arrays],
            pltpu.VMEM((N2 // width, channels * pitch, width), F32),
            pltpu.VMEM((count, devices, per, rows, N2), BF16),
            pltpu.SemaphoreType.DMA((count,)),
            pltpu.SemaphoreType.DMA((count,)),
        ],
        compiler_params=pltpu.CompilerParams(vmem_limit_bytes=VMEM),
        cost_estimate=pl.CostEstimate(flops=0, bytes_accessed=7 << 20, transcendentals=0),
        name="outward",
    )(*arrays)


def outward_near_kernel(in_ref, *refs, hops, plane):
    here = place(plane)
    *out_refs, rows_ref = refs
    _, per, rows, width = out_refs[0].shape
    channels = in_ref.shape[3]
    pitch = rows_ref.shape[0] // channels
    for r in range(rows):
        rows_ref[pl.ds(r, channels, stride=pitch), :] = in_ref[0, r].T.astype(F32)
    for j, out_ref in enumerate(out_refs):
        for hop in range(hops):
            block = owner(here, j, hop, plane) * (per * pitch)
            rows_here = rows_ref[pl.ds(pl.multiple_of(block, per * pitch), per * pitch), :]
            out_ref[hop] = rows_here.reshape(per, pitch, width)[:, :rows].astype(BF16)


def outward_near(x, count, hops, plane):
    _, rows, _, channels = x.shape
    per = channels // count
    width = 128
    return pl.pallas_call(
        functools.partial(outward_near_kernel, hops=hops, plane=plane),
        grid=(N2 // width,),
        in_specs=[pl.BlockSpec((1, rows, width, channels), lambda h: (0, 0, h, 0))],
        out_specs=[pl.BlockSpec((hops, per, rows, width), lambda h: (0, 0, 0, h))] * (count // hops),
        out_shape=[jax.ShapeDtypeStruct((hops, per, rows, N2), BF16)] * (count // hops),
        scratch_shapes=[pltpu.VMEM((channels * (rows + 8), width), F32)],
        compiler_params=pltpu.CompilerParams(vmem_limit_bytes=VMEM),
        cost_estimate=pl.CostEstimate(flops=0, bytes_accessed=2 << 20, transcendentals=0),
        name="outward_near",
    )(x)


def regroup_kernel(*refs, count):
    for i, in_ref in enumerate(refs[:count]):
        for j, out_ref in enumerate(refs[count:]):
            out_ref[i] = in_ref[j]


def regroup(arrays):
    hops, *block = arrays[0].shape
    return pl.pallas_call(
        functools.partial(regroup_kernel, count=len(arrays)),
        out_shape=[jax.ShapeDtypeStruct((len(arrays), *block), BF16)] * hops,
        compiler_params=pltpu.CompilerParams(vmem_limit_bytes=VMEM),
        cost_estimate=pl.CostEstimate(flops=0, bytes_accessed=2 << 20, transcendentals=0),
        name="regroup",
    )(*arrays)


def homeward_kernel(last_ref, *refs, per):
    *early_refs, y_ref, grad_ref, rows_ref = refs
    count, _, rows, _ = last_ref.shape
    hops = early_refs[0].shape[0]
    plane = count // hops // 2
    here = place(plane)
    width = rows_ref.shape[2]
    pitch = rows_ref.shape[1] // (count * per)
    h = pl.program_id(0)
    lanes = pl.ds(pl.multiple_of(h * width, width), width)
    lower = lax.axis_index("ctx") >= lax.axis_size("ctx") // 2
    row = lax.broadcasted_iota(jnp.int32, (width, width), 0)
    col = lax.broadcasted_iota(jnp.int32, (width, width), 1)
    turn = (col == jnp.where(lower, width - 1 - row, row)).astype(F32)
    turn = (turn * jnp.where(lower, (1 - 2 * h).astype(F32), 1.0)).astype(BF16)
    y_rows = rows_ref.at[0].reshape(count, per, pitch, width)
    grad_rows = rows_ref.at[1].reshape(count, per, pitch, width)
    for j, early_ref in enumerate(early_refs):
        for hop in range(hops):
            y_rows[owner(here, j, hop, plane), :EARLY, :rows] = early_ref[hop, :, :, lanes].astype(F32)
    y_rows[:, EARLY:, :rows] = last_ref[:, : per - EARLY, :, lanes].astype(F32)
    block = last_ref[:, per - EARLY :, :, lanes]
    grad_rows[:, :, :rows] = dot(block.reshape(count * per * rows, width), turn).reshape(block.shape)
    for r in range(rows):
        y_ref[r] = rows_ref[0, pl.ds(r, count * per, stride=pitch), :].astype(BF16).T
    for r in range(rows):
        target = jnp.where(lower, (rows - r) % rows, r)
        grad_ref[0, target] = rows_ref[1, pl.ds(r, count * per, stride=pitch), :].T


def homeward(last, early):
    count, slots, rows, _ = last.shape
    per = (slots + EARLY) // 2
    channels, width, pitch = count * per, 128, rows + 8
    return pl.pallas_call(
        functools.partial(homeward_kernel, per=per),
        grid=(N2 // width,),
        in_specs=[pl.BlockSpec(memory_space=pltpu.VMEM)] * (1 + len(early)),
        out_specs=[
            pl.BlockSpec((rows, width, channels), lambda h: (0, h, 0)),
            pl.BlockSpec((1, rows, width, channels), lambda h: (h, 0, 0, 0)),
        ],
        out_shape=[
            jax.ShapeDtypeStruct((rows, N2, channels), BF16),
            jax.ShapeDtypeStruct((2, rows, width, channels), F32),
        ],
        scratch_shapes=[pltpu.VMEM((2, channels * pitch, width), F32)],
        compiler_params=pltpu.CompilerParams(vmem_limit_bytes=VMEM),
        cost_estimate=pl.CostEstimate(flops=0, bytes_accessed=5 << 20, transcendentals=0),
        name="homeward",
    )(near(last), *[near(x) for x in early])


def by_channel_body(embeds, perturb, cotangent, filter_spectrum, skip_gain):
    dp, ctx = lax.axis_size("dp"), lax.axis_size("ctx")
    d, c = lax.axis_index("dp"), lax.axis_index("ctx")
    axes, order = ("dp", "ctx"), ("ctx", "dp")
    count = dp * ctx
    channels = embeds.shape[2]
    rows = N1 // ctx
    per = channels // count
    plane = 4
    hops = ctx // plane
    tabs = tables()

    def matrix(x):
        return far(x.reshape(1, rows, N2, channels))

    def exchange(x, mask):
        return lax.ppermute(x, axes, [(i, i ^ mask) for i in range(count)]) if mask else x

    first = outward([matrix(embeds), matrix(perturb), far(filter_spectrum)], count)
    received = lax.all_to_all(first, order, 0, 0, tiled=True).reshape(ctx, dp, 3, per, rows, N2)
    cots = outward_near(matrix(cotangent), count, hops, plane)
    cots = regroup([exchange(x, j // plane * ctx + j % plane) for j, x in enumerate(cots)])
    received = near(received)
    cots = list(cots)
    cots[1] = exchange(cots[1], plane)
    cots[1], cots[2] = lax.optimization_barrier((cots[1], cots[2]))
    cots[3], received = lax.optimization_barrier((cots[3], received))
    cots[2:] = [exchange(x, (2 + i) * plane) for i, x in enumerate(cots[2:])]
    gain = lax.dynamic_slice(skip_gain, ((c * dp + d) * per,), (per,))
    outs = conv_call(gain, received, tabs, plane, True)
    kept, held, early = outs[:3], outs[3:6], outs[6:]
    early = [exchange(x, hop * plane) for hop, x in enumerate(early)]
    *kept_late, send = conv_call(gain, received, [*held[:2], *tabs[2:5], held[2]], plane, False)
    send = grad_call(received, [*kept, *kept_late, *held], cots, send)
    send, *early = lax.optimization_barrier((send, *early))
    send, *early = lax.optimization_barrier((send, *regroup(early)))
    last = lax.all_to_all(send.reshape(count, *send.shape[2:]), order, 0, 0, tiled=True)
    early = [exchange(x, j // plane * ctx + j % plane) for j, x in enumerate(early)]
    y, grad = homeward(last, early)
    return y.reshape(1, rows * N2, channels), grad


def trig_table(period):
    row_ids = jnp.arange(period, dtype=jnp.int32)
    exponent = row_ids[:, None] * row_ids[None, :] % period
    phase_angle = exponent.astype(jnp.float32) * (two_pi / period)
    return (jnp.cos(phase_angle).astype(jnp.bfloat16), jnp.sin(phase_angle).astype(jnp.bfloat16))


def twiddle(row_first, row_count, col_first, col_count):
    row_ids = row_first + jnp.arange(row_count, dtype=jnp.int32)
    col_ids = col_first + jnp.arange(col_count, dtype=jnp.int32)
    exponent = row_ids[:, None] * col_ids[None, :] % (N1 * N2)
    phase_angle = exponent.astype(jnp.float32) * (two_pi / (N1 * N2))
    return (jnp.cos(phase_angle)[:, :, None], jnp.sin(phase_angle)[:, :, None])


def first_section(values, col_start):
    cos_table, sin_table = trig_table(N1)
    part_real = jnp.einsum("kn,snmc->skmc", cos_table, values, preferred_element_type=jnp.float32)
    part_imag = -jnp.einsum("kn,snmc->skmc", sin_table, values, preferred_element_type=jnp.float32)
    tw_cos, tw_sin = twiddle(0, N1, col_start, values.shape[2])
    out_real = part_real * tw_cos + part_imag * tw_sin
    out_imag = part_imag * tw_cos - part_real * tw_sin
    return jnp.stack([out_real, out_imag], 1).astype(jnp.bfloat16)


def second_section(section_rows):
    cos_table, sin_table = trig_table(N2)
    with_cos = jnp.einsum(
        "sprnc,kn->sprkc", section_rows, cos_table, preferred_element_type=jnp.float32
    )
    with_sin = jnp.einsum(
        "sprnc,kn->sprkc", section_rows, sin_table, preferred_element_type=jnp.float32
    )
    return jnp.stack([with_cos[:, 0] + with_sin[:, 1], with_cos[:, 1] - with_sin[:, 0]], 1)


def spectral_inverse(product, row_start):
    cos_table, sin_table = trig_table(N2)
    with_cos = jnp.einsum("sprkc,nk->sprnc", product, cos_table, preferred_element_type=jnp.float32)
    with_sin = jnp.einsum("sprkc,nk->sprnc", product, sin_table, preferred_element_type=jnp.float32)
    part_real = with_cos[:, 0] - with_sin[:, 1]
    part_imag = with_cos[:, 1] + with_sin[:, 0]
    tw_cos, tw_sin = twiddle(row_start, product.shape[2], 0, N2)
    out_real = part_real * tw_cos - part_imag * tw_sin
    out_imag = part_imag * tw_cos + part_real * tw_sin
    return jnp.stack([out_real, out_imag], 1).astype(jnp.bfloat16)


def column_inverse(mixed_cols):
    cos_table, sin_table = trig_table(N1)
    with_cos = jnp.einsum(
        "nk,skmc->snmc", cos_table, mixed_cols[:, 0], preferred_element_type=jnp.float32
    )
    with_sin = jnp.einsum(
        "nk,skmc->snmc", sin_table, mixed_cols[:, 1], preferred_element_type=jnp.float32
    )
    return ((with_cos - with_sin) * (1.0 / (N1 * N2))).astype(jnp.bfloat16)


def to_spectrum(section_cols):
    return second_section(
        lax.all_to_all(section_cols, "ctx", split_axis=2, concat_axis=3, tiled=True)
    )


def error_terms(signal, filtered, skip_gain, cotangent_view):
    signal_wide = signal.astype(jnp.float32)
    filtered_wide = lax.optimization_barrier(filtered).astype(jnp.float32)
    outputs = signal_wide * filtered_wide + skip_gain * signal_wide
    clean_y = outputs[0]
    smooth_gap = outputs[1] - clean_y
    err_clean = signal_wide[0] * (cotangent_view.astype(jnp.float32) - smart_weight * smooth_gap)
    err_shift = signal_wide[1] * (smart_weight * smooth_gap)
    return (clean_y, jnp.stack([err_clean, err_shift], 0).astype(jnp.bfloat16))


def body(embeds, perturb, cotangent, filter_spectrum, skip_gain):
    ctx_size = lax.axis_size("ctx")
    ctx_index = lax.axis_index("ctx")
    channels = embeds.shape[2]
    row_count = N1 // ctx_size
    col_count = N2 // ctx_size
    row_start = ctx_index * row_count
    col_start = ctx_index * col_count
    clean_rows = embeds[0].reshape(row_count, N2, channels)
    perturb_rows = perturb[0].reshape(row_count, N2, channels)
    shifted = (clean_rows.astype(jnp.float32) + perturb_rows.astype(jnp.float32)).astype(
        jnp.bfloat16
    )
    inputs = jnp.stack([clean_rows, shifted], 0)
    signal_cols = lax.all_to_all(inputs, "ctx", split_axis=2, concat_axis=1, tiled=True)
    section_cols, signal_cols = (first_section(signal_cols, col_start), signal_cols)
    spectra = to_spectrum(section_cols)
    filter_real = filter_spectrum[0]
    filter_imag = filter_spectrum[1]
    spectrum_real = spectra[:, 0]
    spectrum_imag = spectra[:, 1]
    product = jnp.stack(
        [
            filter_real * spectrum_real - filter_imag * spectrum_imag,
            filter_real * spectrum_imag + filter_imag * spectrum_real,
        ],
        1,
    ).astype(jnp.bfloat16)
    mixed_rows = spectral_inverse(product, row_start)
    filtered = column_inverse(
        lax.all_to_all(mixed_rows, "ctx", split_axis=3, concat_axis=2, tiled=True)
    )
    cotangent_rows = cotangent[0].reshape(row_count, N2, channels)
    filtered_rows = lax.all_to_all(filtered, "ctx", split_axis=1, concat_axis=2, tiled=True)
    clean_y, errors = error_terms(inputs, filtered_rows, skip_gain, cotangent_rows)
    clean_output = clean_y.astype(jnp.bfloat16)
    error_section = first_section(
        lax.all_to_all(errors, "ctx", split_axis=2, concat_axis=1, tiled=True), col_start
    )
    error_spec = to_spectrum(error_section)
    error_real = error_spec[:, 0]
    error_imag = error_spec[:, 1]
    term_real = error_real * spectrum_real + error_imag * spectrum_imag
    term_imag = error_imag * spectrum_real - error_real * spectrum_imag
    local_grad = jnp.stack([term_real[0] + term_real[1], term_imag[0] + term_imag[1]], 0) * (
        1.0 / (N1 * N2)
    )
    grad_shard = lax.psum_scatter(
        local_grad.astype(jnp.bfloat16), "dp", scatter_dimension=2, tiled=True
    ).astype(jnp.float32)
    return (clean_output.reshape(1, row_count * N2, channels), grad_shard)


def solution(mesh):
    dp, ctx = mesh.shape["dp"], mesh.shape["ctx"]

    def run(embeds, *rest):
        apart = dp == 2 and embeds.shape[2] % (dp * ctx) == 0 and N1 // ctx == 16 and embeds.shape[2] // (dp * ctx) > 1
        return jax.shard_map(
            by_channel_body if apart else body,
            mesh=mesh,
            in_specs=(
                P("dp", "ctx", None),
                P("dp", "ctx", None),
                P("dp", "ctx", None),
                P(None, "ctx", None, None),
                P(),
            ),
            out_specs=(P("dp", "ctx", None), P(None, "ctx", "dp", None)),
            check_vma=False,
        )(embeds, *rest)

    return run
```

```python
import functools

import jax
import jax.numpy as jnp
import numpy as np
from jax import lax
from jax.experimental import pallas as pl
from jax.experimental.pallas import tpu as pltpu
from jax.sharding import PartitionSpec as P

N1 = 256
N2 = 256
BF16 = jnp.bfloat16
F32 = jnp.float32
EARLY = 3
HALF = 144
VMEM = 26 << 20

two_pi = 6.283185307179586
smart_weight = 2.0


def tables():
    ids = np.arange(N1)
    phase = (ids[:, None] * ids[None, :] % N1) * (two_pi / N1)
    cos_table, sin_table = np.cos(phase), np.sin(phase)
    split_rows = np.concatenate([cos_table[:HALF], -sin_table[:HALF]], 0)
    forward_table = np.block([[cos_table, -sin_table], [sin_table, cos_table]])
    weight = np.where(ids[: N1 // 2] == 0, 1.0, 2.0) / (N1 * N2)
    join_rows = np.concatenate([cos_table[:, : N1 // 2] * weight, -sin_table[:, : N1 // 2] * weight], 1)
    mirror_rows = np.zeros((HALF, N1))
    mirror_rows[ids[:HALF], -ids[:HALF] % N1] = 1
    mirror_cols = np.eye(N2)[::-1]
    angle = (ids[:HALF, None] * ids[None, :]) * (two_pi / (N1 * N2))
    twiddle = np.stack([np.cos(angle), np.sin(angle)], 0)
    small = (split_rows, forward_table, join_rows, mirror_rows, mirror_cols)
    small = [jnp.asarray(t.astype(jnp.bfloat16)) for t in small]
    return (*small, jnp.asarray(twiddle.astype(np.float32)))


def dot(a, b):
    return jnp.dot(a, b, preferred_element_type=F32)


def place(plane):
    c = lax.axis_index("ctx")
    return lax.axis_index("dp"), c // plane, c % plane


def peer(here, j, hop, plane):
    return here[0] ^ (j // plane), (here[1] ^ hop) * plane + (here[2] ^ (j % plane))


def owner(here, j, hop, plane):
    d, c = peer(here, j, hop, plane)
    return c * lax.axis_size("dp") + d


def forward(signals, split_ref, fwd_ref, tw_cos, tw_sin):
    halves = []
    for x in signals:
        part = dot(split_ref[...], x)
        part_real, part_imag = part[:HALF], part[HALF:]
        out_real = part_real * tw_cos + part_imag * tw_sin
        out_imag = part_imag * tw_cos - part_real * tw_sin
        halves.append(jnp.concatenate([out_real.astype(BF16), out_imag.astype(BF16)], 1))
    spectra = dot(jnp.concatenate(halves, 0), fwd_ref[...])
    return [spectra[i * HALF : (i + 1) * HALF] for i in range(len(signals))]


def hermitian_part(filter_real, filter_imag, mirror_rows, mirror_cols):
    rows = dot(mirror_rows, jnp.concatenate([filter_real, filter_imag], 1)).astype(BF16)
    flipped = dot(jnp.concatenate([rows[:, :N2], rows[:, N2:]], 0), mirror_cols)
    out = []
    for part, other, sign in ((filter_real, flipped[:HALF], 0.5), (filter_imag, flipped[HALF:], -0.5)):
        top = other[:8]
        row = lax.broadcasted_iota(jnp.int32, top.shape, 0)
        top = jnp.where(row == 0, pltpu.roll(top, 1, 1), top)
        other = jnp.concatenate([top, other[8:]], 0)
        out.append(0.5 * part[:HALF].astype(F32) + sign * other)
    return out


def gradient(err_spectra, spectra):
    total_real = total_imag = 0.0
    for err_spec, spec in zip(err_spectra, spectra):
        err_real, err_imag = err_spec[:, :N2], err_spec[:, N2:]
        real, imag = spec[:, :N2], spec[:, N2:]
        total_real += err_real * real + err_imag * imag
        total_imag += err_imag * real - err_real * imag
    return total_real, total_imag


def conv_kernel(
    gain_ref, recv_ref, split_ref, fwd_ref, join_ref, mirror_ref, cols_ref, tw_ref,
    gap_ref, spec_ref, part_ref, *refs, early,
):
    *refs, y_rows = refs
    ctx, count = recv_ref.shape[:2]
    step = pl.program_id(0)
    q = step if early else step + EARLY
    if early:
        held_refs, early_refs = refs[:3], refs[3:]

        @pl.when(step == 0)
        def _():
            for held_ref, table_ref in zip(held_refs, (split_ref, fwd_ref, tw_ref)):
                held_ref[...] = table_ref[...]

    tw_cos, tw_sin = tw_ref[0], tw_ref[1]
    signals = []
    for d in range(count):
        clean = recv_ref[:, d, 0, q].reshape(N1, N2)
        perturb = recv_ref[:, d, 1, q].reshape(N1, N2)
        signals += [clean, (clean.astype(F32) + perturb.astype(F32)).astype(BF16)]
    spectra = forward(signals, split_ref, fwd_ref, tw_cos, tw_sin)
    filter_real, filter_imag = hermitian_part(
        recv_ref[:, 0, 2, q].reshape(N1, N2), recv_ref[:, 1, 2, q].reshape(N1, N2), mirror_ref[...], cols_ref[...]
    )
    products = []
    for spec in spectra:
        real, imag = spec[:, :N2], spec[:, N2:]
        prod_real = (filter_real * real - filter_imag * imag).astype(BF16)
        minus_imag = (-filter_real * imag - filter_imag * real).astype(BF16)
        products.append(jnp.concatenate([prod_real, minus_imag], 1))
    back = dot(jnp.concatenate(products, 0), fwd_ref[...])
    mixed, middle = [], []
    for i in range(2 * count):
        back_real, minus_imag = back[i * HALF : (i + 1) * HALF, :N2], back[i * HALF : (i + 1) * HALF, N2:]
        mixed_real = (back_real * tw_cos + minus_imag * tw_sin).astype(BF16)
        mixed_imag = (back_real * tw_sin - minus_imag * tw_cos).astype(BF16)
        mixed.append(jnp.concatenate([mixed_real[: N1 // 2], mixed_imag[: N1 // 2]], 0))
        middle.append(mixed_real[N1 // 2 :].astype(F32)[:1])
    conv = dot(join_ref[...], jnp.concatenate(mixed, 1))
    parity = lax.broadcasted_iota(jnp.int32, (N1, N2), 0) % 2
    alternate = (1 - 2 * parity).astype(F32) * (1.0 / (N1 * N2))
    gain = gain_ref[q]
    errors = []
    for d in range(count):
        pair = []
        for i in range(2):
            k = 2 * d + i
            wide = signals[k].astype(F32)
            filtered = conv[:, k * N2 : (k + 1) * N2] + alternate * middle[k]
            pair.append((wide, wide * filtered.astype(BF16).astype(F32) + gain * wide))
        (clean, clean_y), (shifted, shifted_y) = pair
        y_rows[d * ctx : (d + 1) * ctx] = clean_y.astype(BF16).reshape(ctx, -1, N2)
        gap = smart_weight * (shifted_y - clean_y)
        gap_ref[step, d] = gap
        spec_ref[step, d] = spectra[2 * d]
        errors.append((shifted * gap).astype(BF16))
    total_real, total_imag = gradient(forward(errors, split_ref, fwd_ref, tw_cos, tw_sin), spectra[1::2])
    part_ref[step, 0] = total_real
    part_ref[step, 1] = total_imag
    if early:
        near_count = early_refs[0].shape[0]
        here = place(near_count // count)
        for hop, early_ref in enumerate(early_refs):
            for j in range(near_count):
                side, block = peer(here, j, hop, near_count // count)
                early_ref[j, step] = y_rows[side * ctx + block]
    else:
        (send_ref,) = refs
        for d in range(count):
            send_ref[:, d, step] = y_rows[d * ctx : (d + 1) * ctx]


def grad_kernel(recv_ref, *refs, hops):
    first, second, refs = refs[:3], refs[3:6], refs[6:]
    cot_refs, refs = refs[:hops], refs[hops:]
    split_ref, fwd_ref, tw_ref, y_ref, send_ref, cot_rows, ready_ref, sems = refs
    copies = [pltpu.make_async_copy(y_ref, send_ref.at[:, :, pl.ds(0, y_ref.shape[2])], sems.at[0])]
    copies[0].start()
    ctx, count = recv_ref.shape[:2]
    near = cot_refs[0].shape[0]
    plane = near // count
    here = place(plane)
    per = recv_ref.shape[3]
    for hop, cot_ref in enumerate(cot_refs):
        for j in range(near):
            side, block = peer(here, j, hop, plane)
            cot_rows[side * ctx + block] = cot_ref[j]
    kept = [(first, q) if q < EARLY else (second, q - EARLY) for q in range(per)]
    errors = []
    for q, ((gap_ref, _, _), i) in enumerate(kept):
        for d in range(count):
            clean = recv_ref[:, d, 0, q].reshape(N1, N2).astype(F32)
            cot = cot_rows[d * ctx : (d + 1) * ctx, q].reshape(N1, N2).astype(F32)
            errors.append((clean * (cot - gap_ref[i, d])).astype(BF16))
    err_spectra = forward(errors, split_ref, fwd_ref, tw_ref[0], tw_ref[1])
    for q, ((_, spec_ref, part_ref), i) in enumerate(kept):
        spectra = [spec_ref[i, d] for d in range(count)]
        total = gradient(err_spectra[q * count : (q + 1) * count], spectra)
        fill_grad(ready_ref, q, *[t + part_ref[i, p] for p, t in enumerate(total)])
        copies.append(pltpu.make_async_copy(ready_ref.at[q], send_ref.at[:, :, per - EARLY + q], sems.at[1 + q]))
        copies[1 + q].start()
    for copy in copies:
        copy.wait()


def fill_grad(ready_ref, q, total_real, total_imag):
    _, ctx, count, rows, _ = ready_ref.shape
    total = jnp.concatenate([total_real, total_imag], 1) * (1.0 / (N1 * N2))
    upper, after = total[: N1 // 2], total[rows : N1 // 2 + rows]
    first = lax.broadcasted_iota(jnp.int32, upper.shape, 0) % rows == 0
    lower = jnp.where(first, after, upper).astype(BF16)
    upper = upper.astype(BF16)
    width = N2 // count
    for i in range(count):
        for half, x, side in ((0, upper, i), (1, lower, count - 1 - i)):
            cols = slice(side * width, (side + 1) * width)
            pair = jnp.concatenate([x[:, :N2][:, cols], x[:, N2:][:, cols]], 1)
            for block in range(ctx // 2):
                target = ctx - 1 - block if half else block
                ready_ref[q, target, i] = pair[block * rows : (block + 1) * rows]


def whole(x):
    return pl.BlockSpec(x.shape, lambda *_: (0,) * x.ndim)


def near(x):
    return pltpu.with_memory_space_constraint(x, pltpu.VMEM)


def far(x):
    return pltpu.with_memory_space_constraint(x, pltpu.HBM)


def conv_call(gain, received, tabs, plane, early):
    ctx, dp, _, per, rows, _ = received.shape
    split_rows, forward_table, *_, twiddle = tabs
    steps = EARLY if early else per - EARLY
    here = pl.BlockSpec(memory_space=pltpu.VMEM)
    if early:
        tabs, specs = [far(t) for t in tabs], [whole(t) for t in tabs]
        held = [pltpu.VMEM(t.shape, t.dtype) for t in (split_rows, forward_table, twiddle)]
        more = [*held, *[pltpu.VMEM((dp * plane, EARLY, rows, N2), BF16)] * (ctx // plane)]
    else:
        inside = (True, True, False, False, False, True)
        specs = [here if held else whole(t) for t, held in zip(tabs, inside)]
        tabs = [near(t) if held else far(t) for t, held in zip(tabs, inside)]
        more = [pltpu.VMEM((ctx, dp, steps, rows, N2), BF16)]
    return pl.pallas_call(
        functools.partial(conv_kernel, early=early),
        grid=(steps,),
        in_specs=[here, here, *specs],
        out_specs=[here] * (3 + len(more)),
        out_shape=[
            pltpu.VMEM((steps, dp, N1, N2), F32),
            pltpu.VMEM((steps, dp, HALF, 2 * N2), F32),
            pltpu.VMEM((steps, 2, HALF, N2), F32),
            *more,
        ],
        scratch_shapes=[pltpu.VMEM((dp * ctx, rows, N2), BF16)],
        compiler_params=pltpu.CompilerParams(vmem_limit_bytes=VMEM),
        cost_estimate=pl.CostEstimate(flops=steps * dp * 5 * 6 * N1**3, bytes_accessed=4 << 20, transcendentals=0),
        name="conv_early" if early else "conv_late",
    )(near(gain), received, *tabs)


def grad_call(received, kept, cots, send):
    ctx, dp, _, per, rows, _ = received.shape
    *kept, split_rows, forward_table, twiddle = [near(x) for x in kept]
    operands = (received, *kept, *[near(x) for x in cots], split_rows, forward_table, twiddle, near(send))
    return pl.pallas_call(
        functools.partial(grad_kernel, hops=len(cots)),
        grid=(1,),
        in_specs=[pl.BlockSpec(memory_space=pltpu.VMEM)] * len(operands),
        out_specs=pl.BlockSpec(memory_space=pl.ANY),
        out_shape=pltpu.HBM((ctx, dp, 2 * per - EARLY, rows, N2), BF16),
        scratch_shapes=[
            pltpu.VMEM((dp * ctx, per, rows, N2), BF16),
            pltpu.VMEM((per, ctx, dp, rows, N2), BF16),
            pltpu.SemaphoreType.DMA((1 + per,)),
        ],
        compiler_params=pltpu.CompilerParams(vmem_limit_bytes=VMEM),
        cost_estimate=pl.CostEstimate(flops=per * dp * 6 * N1**3, bytes_accessed=8 << 20, transcendentals=0),
        name="grad",
    )(*operands)


def outward_kernel(*refs, count):
    in_refs, refs = refs[:count], refs[count:]
    out_ref, refs = refs[0], refs[1:]
    held_refs, (rows_ref, ready_ref, load_sems, store_sems) = refs[:count], refs[count:]
    devices, _, per, rows, _ = out_ref.shape
    pitch = rows_ref.shape[1] // (devices * per)
    width = rows_ref.shape[2]
    loads, stores = [], []
    for t, (in_ref, held_ref) in enumerate(zip(in_refs, held_refs)):
        source = in_ref.at[lax.axis_index("dp") if in_ref.shape[0] > 1 else 0]
        loads.append(pltpu.make_async_copy(source, held_ref, load_sems.at[t]))
        loads[t].start()
    for t, held_ref in enumerate(held_refs):
        loads[t].wait()
        for h in range(N2 // width):
            lanes = slice(h * width, (h + 1) * width)
            for r in range(rows):
                block = held_ref[r, lanes].astype(BF16).T.astype(F32)
                rows_ref[h, pl.ds(r, devices * per, stride=pitch), :] = block
            block = rows_ref[h].reshape(devices, per, pitch, width)[:, :, :rows].astype(BF16)
            ready_ref[t, :, :, :, lanes] = block
        stores.append(pltpu.make_async_copy(ready_ref.at[t], out_ref.at[:, t], store_sems.at[t]))
        stores[t].start()
    for store in stores:
        store.wait()


def outward(arrays, devices):
    _, rows, _, channels = arrays[0].shape
    count, per, width, pitch = len(arrays), channels // devices, 128, rows + 8
    shape = (devices, count, per, rows, N2)
    return pl.pallas_call(
        functools.partial(outward_kernel, count=count),
        in_specs=[pl.BlockSpec(memory_space=pl.ANY)] * count,
        out_specs=pl.BlockSpec(memory_space=pl.ANY),
        out_shape=pltpu.HBM(shape, BF16),
        scratch_shapes=[
            *[pltpu.VMEM(a.shape[1:], a.dtype) for a in arrays],
            pltpu.VMEM((N2 // width, channels * pitch, width), F32),
            pltpu.VMEM((count, devices, per, rows, N2), BF16),
            pltpu.SemaphoreType.DMA((count,)),
            pltpu.SemaphoreType.DMA((count,)),
        ],
        compiler_params=pltpu.CompilerParams(vmem_limit_bytes=VMEM),
        cost_estimate=pl.CostEstimate(flops=0, bytes_accessed=7 << 20, transcendentals=0),
        name="outward",
    )(*arrays)


def outward_near_kernel(in_ref, *refs, hops, plane):
    here = place(plane)
    *out_refs, rows_ref = refs
    _, per, rows, width = out_refs[0].shape
    channels = in_ref.shape[3]
    pitch = rows_ref.shape[0] // channels
    for r in range(rows):
        rows_ref[pl.ds(r, channels, stride=pitch), :] = in_ref[0, r].T.astype(F32)
    for j, out_ref in enumerate(out_refs):
        for hop in range(hops):
            block = owner(here, j, hop, plane) * (per * pitch)
            rows_here = rows_ref[pl.ds(pl.multiple_of(block, per * pitch), per * pitch), :]
            out_ref[hop] = rows_here.reshape(per, pitch, width)[:, :rows].astype(BF16)


def outward_near(x, count, hops, plane):
    _, rows, _, channels = x.shape
    per = channels // count
    width = 128
    return pl.pallas_call(
        functools.partial(outward_near_kernel, hops=hops, plane=plane),
        grid=(N2 // width,),
        in_specs=[pl.BlockSpec((1, rows, width, channels), lambda h: (0, 0, h, 0))],
        out_specs=[pl.BlockSpec((hops, per, rows, width), lambda h: (0, 0, 0, h))] * (count // hops),
        out_shape=[jax.ShapeDtypeStruct((hops, per, rows, N2), BF16)] * (count // hops),
        scratch_shapes=[pltpu.VMEM((channels * (rows + 8), width), F32)],
        compiler_params=pltpu.CompilerParams(vmem_limit_bytes=VMEM),
        cost_estimate=pl.CostEstimate(flops=0, bytes_accessed=2 << 20, transcendentals=0),
        name="outward_near",
    )(x)


def regroup_kernel(*refs, count):
    for i, in_ref in enumerate(refs[:count]):
        for j, out_ref in enumerate(refs[count:]):
            out_ref[i] = in_ref[j]


def regroup(arrays):
    hops, *block = arrays[0].shape
    return pl.pallas_call(
        functools.partial(regroup_kernel, count=len(arrays)),
        out_shape=[jax.ShapeDtypeStruct((len(arrays), *block), BF16)] * hops,
        compiler_params=pltpu.CompilerParams(vmem_limit_bytes=VMEM),
        cost_estimate=pl.CostEstimate(flops=0, bytes_accessed=2 << 20, transcendentals=0),
        name="regroup",
    )(*arrays)


def homeward_kernel(last_ref, *refs, per):
    *early_refs, y_ref, grad_ref, rows_ref = refs
    count, _, rows, _ = last_ref.shape
    hops = early_refs[0].shape[0]
    plane = count // hops // 2
    here = place(plane)
    width = rows_ref.shape[2]
    pitch = rows_ref.shape[1] // (count * per)
    h = pl.program_id(0)
    lanes = pl.ds(pl.multiple_of(h * width, width), width)
    lower = lax.axis_index("ctx") >= lax.axis_size("ctx") // 2
    row = lax.broadcasted_iota(jnp.int32, (width, width), 0)
    col = lax.broadcasted_iota(jnp.int32, (width, width), 1)
    turn = (col == jnp.where(lower, width - 1 - row, row)).astype(F32)
    turn = (turn * jnp.where(lower, (1 - 2 * h).astype(F32), 1.0)).astype(BF16)
    y_rows = rows_ref.at[0].reshape(count, per, pitch, width)
    grad_rows = rows_ref.at[1].reshape(count, per, pitch, width)
    for j, early_ref in enumerate(early_refs):
        for hop in range(hops):
            y_rows[owner(here, j, hop, plane), :EARLY, :rows] = early_ref[hop, :, :, lanes].astype(F32)
    y_rows[:, EARLY:, :rows] = last_ref[:, : per - EARLY, :, lanes].astype(F32)
    block = last_ref[:, per - EARLY :, :, lanes]
    grad_rows[:, :, :rows] = dot(block.reshape(count * per * rows, width), turn).reshape(block.shape)
    for r in range(rows):
        y_ref[r] = rows_ref[0, pl.ds(r, count * per, stride=pitch), :].astype(BF16).T
    for r in range(rows):
        target = jnp.where(lower, (rows - r) % rows, r)
        grad_ref[0, target] = rows_ref[1, pl.ds(r, count * per, stride=pitch), :].T


def homeward(last, early):
    count, slots, rows, _ = last.shape
    per = (slots + EARLY) // 2
    channels, width, pitch = count * per, 128, rows + 8
    return pl.pallas_call(
        functools.partial(homeward_kernel, per=per),
        grid=(N2 // width,),
        in_specs=[pl.BlockSpec(memory_space=pltpu.VMEM)] * (1 + len(early)),
        out_specs=[
            pl.BlockSpec((rows, width, channels), lambda h: (0, h, 0)),
            pl.BlockSpec((1, rows, width, channels), lambda h: (h, 0, 0, 0)),
        ],
        out_shape=[
            jax.ShapeDtypeStruct((rows, N2, channels), BF16),
            jax.ShapeDtypeStruct((2, rows, width, channels), F32),
        ],
        scratch_shapes=[pltpu.VMEM((2, channels * pitch, width), F32)],
        compiler_params=pltpu.CompilerParams(vmem_limit_bytes=VMEM),
        cost_estimate=pl.CostEstimate(flops=0, bytes_accessed=5 << 20, transcendentals=0),
        name="homeward",
    )(near(last), *[near(x) for x in early])


def by_channel_body(embeds, perturb, cotangent, filter_spectrum, skip_gain):
    dp, ctx = lax.axis_size("dp"), lax.axis_size("ctx")
    d, c = lax.axis_index("dp"), lax.axis_index("ctx")
    axes, order = ("dp", "ctx"), ("ctx", "dp")
    count = dp * ctx
    channels = embeds.shape[2]
    rows = N1 // ctx
    per = channels // count
    plane = 4
    hops = ctx // plane
    tabs = tables()

    def matrix(x):
        return far(x.reshape(1, rows, N2, channels))

    def exchange(x, mask):
        return lax.ppermute(x, axes, [(i, i ^ mask) for i in range(count)]) if mask else x

    first = outward([matrix(embeds), matrix(perturb), far(filter_spectrum)], count)
    received = lax.all_to_all(first, order, 0, 0, tiled=True).reshape(ctx, dp, 3, per, rows, N2)
    cots = outward_near(matrix(cotangent), count, hops, plane)
    cots = regroup([exchange(x, j // plane * ctx + j % plane) for j, x in enumerate(cots)])
    received = near(received)
    *early, late = cots
    late, received = lax.optimization_barrier((late, received))
    cots = [exchange(x, hop * plane) for hop, x in enumerate([*early, late])]
    gain = lax.dynamic_slice(skip_gain, ((c * dp + d) * per,), (per,))
    gain = jnp.broadcast_to(gain[:, None, None], (per, 1, N2))
    outs = conv_call(gain, received, tabs, plane, True)
    kept, held, early = outs[:3], outs[3:6], outs[6:]
    early = [exchange(x, hop * plane) for hop, x in enumerate(early)]
    *kept_late, send = conv_call(gain, received, [*held[:2], *tabs[2:5], held[2]], plane, False)
    send = grad_call(received, [*kept, *kept_late, *held], cots, send)
    send, *early = lax.optimization_barrier((send, *early))
    send, *early = lax.optimization_barrier((send, *regroup(early)))
    last = lax.all_to_all(send.reshape(count, *send.shape[2:]), order, 0, 0, tiled=True)
    early = [exchange(x, j // plane * ctx + j % plane) for j, x in enumerate(early)]
    y, grad = homeward(last, early)
    return y.reshape(1, rows * N2, channels), grad


def trig_table(period):
    row_ids = jnp.arange(period, dtype=jnp.int32)
    exponent = row_ids[:, None] * row_ids[None, :] % period
    phase_angle = exponent.astype(jnp.float32) * (two_pi / period)
    return (jnp.cos(phase_angle).astype(jnp.bfloat16), jnp.sin(phase_angle).astype(jnp.bfloat16))


def twiddle(row_first, row_count, col_first, col_count):
    row_ids = row_first + jnp.arange(row_count, dtype=jnp.int32)
    col_ids = col_first + jnp.arange(col_count, dtype=jnp.int32)
    exponent = row_ids[:, None] * col_ids[None, :] % (N1 * N2)
    phase_angle = exponent.astype(jnp.float32) * (two_pi / (N1 * N2))
    return (jnp.cos(phase_angle)[:, :, None], jnp.sin(phase_angle)[:, :, None])


def first_section(values, col_start):
    cos_table, sin_table = trig_table(N1)
    part_real = jnp.einsum("kn,snmc->skmc", cos_table, values, preferred_element_type=jnp.float32)
    part_imag = -jnp.einsum("kn,snmc->skmc", sin_table, values, preferred_element_type=jnp.float32)
    tw_cos, tw_sin = twiddle(0, N1, col_start, values.shape[2])
    out_real = part_real * tw_cos + part_imag * tw_sin
    out_imag = part_imag * tw_cos - part_real * tw_sin
    return jnp.stack([out_real, out_imag], 1).astype(jnp.bfloat16)


def second_section(section_rows):
    cos_table, sin_table = trig_table(N2)
    with_cos = jnp.einsum(
        "sprnc,kn->sprkc", section_rows, cos_table, preferred_element_type=jnp.float32
    )
    with_sin = jnp.einsum(
        "sprnc,kn->sprkc", section_rows, sin_table, preferred_element_type=jnp.float32
    )
    return jnp.stack([with_cos[:, 0] + with_sin[:, 1], with_cos[:, 1] - with_sin[:, 0]], 1)


def spectral_inverse(product, row_start):
    cos_table, sin_table = trig_table(N2)
    with_cos = jnp.einsum("sprkc,nk->sprnc", product, cos_table, preferred_element_type=jnp.float32)
    with_sin = jnp.einsum("sprkc,nk->sprnc", product, sin_table, preferred_element_type=jnp.float32)
    part_real = with_cos[:, 0] - with_sin[:, 1]
    part_imag = with_cos[:, 1] + with_sin[:, 0]
    tw_cos, tw_sin = twiddle(row_start, product.shape[2], 0, N2)
    out_real = part_real * tw_cos - part_imag * tw_sin
    out_imag = part_imag * tw_cos + part_real * tw_sin
    return jnp.stack([out_real, out_imag], 1).astype(jnp.bfloat16)


def column_inverse(mixed_cols):
    cos_table, sin_table = trig_table(N1)
    with_cos = jnp.einsum(
        "nk,skmc->snmc", cos_table, mixed_cols[:, 0], preferred_element_type=jnp.float32
    )
    with_sin = jnp.einsum(
        "nk,skmc->snmc", sin_table, mixed_cols[:, 1], preferred_element_type=jnp.float32
    )
    return ((with_cos - with_sin) * (1.0 / (N1 * N2))).astype(jnp.bfloat16)


def to_spectrum(section_cols):
    return second_section(
        lax.all_to_all(section_cols, "ctx", split_axis=2, concat_axis=3, tiled=True)
    )


def error_terms(signal, filtered, skip_gain, cotangent_view):
    signal_wide = signal.astype(jnp.float32)
    filtered_wide = lax.optimization_barrier(filtered).astype(jnp.float32)
    outputs = signal_wide * filtered_wide + skip_gain * signal_wide
    clean_y = outputs[0]
    smooth_gap = outputs[1] - clean_y
    err_clean = signal_wide[0] * (cotangent_view.astype(jnp.float32) - smart_weight * smooth_gap)
    err_shift = signal_wide[1] * (smart_weight * smooth_gap)
    return (clean_y, jnp.stack([err_clean, err_shift], 0).astype(jnp.bfloat16))


def body(embeds, perturb, cotangent, filter_spectrum, skip_gain):
    ctx_size = lax.axis_size("ctx")
    ctx_index = lax.axis_index("ctx")
    channels = embeds.shape[2]
    row_count = N1 // ctx_size
    col_count = N2 // ctx_size
    row_start = ctx_index * row_count
    col_start = ctx_index * col_count
    clean_rows = embeds[0].reshape(row_count, N2, channels)
    perturb_rows = perturb[0].reshape(row_count, N2, channels)
    shifted = (clean_rows.astype(jnp.float32) + perturb_rows.astype(jnp.float32)).astype(
        jnp.bfloat16
    )
    inputs = jnp.stack([clean_rows, shifted], 0)
    signal_cols = lax.all_to_all(inputs, "ctx", split_axis=2, concat_axis=1, tiled=True)
    section_cols, signal_cols = (first_section(signal_cols, col_start), signal_cols)
    spectra = to_spectrum(section_cols)
    filter_real = filter_spectrum[0]
    filter_imag = filter_spectrum[1]
    spectrum_real = spectra[:, 0]
    spectrum_imag = spectra[:, 1]
    product = jnp.stack(
        [
            filter_real * spectrum_real - filter_imag * spectrum_imag,
            filter_real * spectrum_imag + filter_imag * spectrum_real,
        ],
        1,
    ).astype(jnp.bfloat16)
    mixed_rows = spectral_inverse(product, row_start)
    filtered = column_inverse(
        lax.all_to_all(mixed_rows, "ctx", split_axis=3, concat_axis=2, tiled=True)
    )
    cotangent_rows = cotangent[0].reshape(row_count, N2, channels)
    filtered_rows = lax.all_to_all(filtered, "ctx", split_axis=1, concat_axis=2, tiled=True)
    clean_y, errors = error_terms(inputs, filtered_rows, skip_gain, cotangent_rows)
    clean_output = clean_y.astype(jnp.bfloat16)
    error_section = first_section(
        lax.all_to_all(errors, "ctx", split_axis=2, concat_axis=1, tiled=True), col_start
    )
    error_spec = to_spectrum(error_section)
    error_real = error_spec[:, 0]
    error_imag = error_spec[:, 1]
    term_real = error_real * spectrum_real + error_imag * spectrum_imag
    term_imag = error_imag * spectrum_real - error_real * spectrum_imag
    local_grad = jnp.stack([term_real[0] + term_real[1], term_imag[0] + term_imag[1]], 0) * (
        1.0 / (N1 * N2)
    )
    grad_shard = lax.psum_scatter(
        local_grad.astype(jnp.bfloat16), "dp", scatter_dimension=2, tiled=True
    ).astype(jnp.float32)
    return (clean_output.reshape(1, row_count * N2, channels), grad_shard)


def solution(mesh):
    dp, ctx = mesh.shape["dp"], mesh.shape["ctx"]

    def run(embeds, *rest):
        apart = dp == 2 and embeds.shape[2] % (dp * ctx) == 0 and N1 // ctx == 16 and embeds.shape[2] // (dp * ctx) > 1
        return jax.shard_map(
            by_channel_body if apart else body,
            mesh=mesh,
            in_specs=(
                P("dp", "ctx", None),
                P("dp", "ctx", None),
                P("dp", "ctx", None),
                P(None, "ctx", None, None),
                P(),
            ),
            out_specs=(P("dp", "ctx", None), P(None, "ctx", "dp", None)),
            check_vma=False,
        )(embeds, *rest)

    return run
```

```python
import functools

import jax
import jax.numpy as jnp
import numpy as np
from jax import lax
from jax.experimental import pallas as pl
from jax.experimental.pallas import tpu as pltpu
from jax.sharding import PartitionSpec as P

N1 = 256
N2 = 256
BF16 = jnp.bfloat16
F32 = jnp.float32
EARLY = 3
HALF = 144
VMEM = 26 << 20

two_pi = 6.283185307179586
smart_weight = 2.0


def tables():
    ids = np.arange(N1)
    phase = (ids[:, None] * ids[None, :] % N1) * (two_pi / N1)
    cos_table, sin_table = np.cos(phase), np.sin(phase)
    split_rows = np.concatenate([cos_table[:HALF], -sin_table[:HALF]], 0)
    forward_table = np.block([[cos_table, -sin_table], [sin_table, cos_table]])
    weight = np.where(ids[: N1 // 2] == 0, 1.0, 2.0) / (N1 * N2)
    join_rows = np.concatenate([cos_table[:, : N1 // 2] * weight, -sin_table[:, : N1 // 2] * weight], 1)
    mirror_rows = np.zeros((HALF, N1))
    mirror_rows[ids[:HALF], -ids[:HALF] % N1] = 1
    mirror_cols = np.eye(N2)[::-1]
    angle = (ids[:HALF, None] * ids[None, :]) * (two_pi / (N1 * N2))
    twiddle = np.stack([np.cos(angle), np.sin(angle)], 0)
    small = (split_rows, forward_table, join_rows, mirror_rows, mirror_cols)
    small = [jnp.asarray(t.astype(jnp.bfloat16)) for t in small]
    return (*small, jnp.asarray(twiddle.astype(np.float32)))


def dot(a, b):
    return jnp.dot(a, b, preferred_element_type=F32)


def place(plane):
    c = lax.axis_index("ctx")
    return lax.axis_index("dp"), c // plane, c % plane


def peer(here, j, hop, plane):
    return here[0] ^ (j // plane), (here[1] ^ hop) * plane + (here[2] ^ (j % plane))


def owner(here, j, hop, plane):
    d, c = peer(here, j, hop, plane)
    return c * lax.axis_size("dp") + d


def forward(signals, split_ref, fwd_ref, tw_cos, tw_sin):
    halves = []
    for x in signals:
        part = dot(split_ref[...], x)
        part_real, part_imag = part[:HALF], part[HALF:]
        out_real = part_real * tw_cos + part_imag * tw_sin
        out_imag = part_imag * tw_cos - part_real * tw_sin
        halves.append(jnp.concatenate([out_real.astype(BF16), out_imag.astype(BF16)], 1))
    spectra = dot(jnp.concatenate(halves, 0), fwd_ref[...])
    return [spectra[i * HALF : (i + 1) * HALF] for i in range(len(signals))]


def hermitian_part(filter_real, filter_imag, mirror_rows, mirror_cols):
    rows = dot(mirror_rows, jnp.concatenate([filter_real, filter_imag], 1)).astype(BF16)
    flipped = dot(jnp.concatenate([rows[:, :N2], rows[:, N2:]], 0), mirror_cols)
    out = []
    for part, other, sign in ((filter_real, flipped[:HALF], 0.5), (filter_imag, flipped[HALF:], -0.5)):
        top = other[:8]
        row = lax.broadcasted_iota(jnp.int32, top.shape, 0)
        top = jnp.where(row == 0, pltpu.roll(top, 1, 1), top)
        other = jnp.concatenate([top, other[8:]], 0)
        out.append(0.5 * part[:HALF].astype(F32) + sign * other)
    return out


def gradient(err_spectra, spectra):
    total_real = total_imag = 0.0
    for err_spec, spec in zip(err_spectra, spectra):
        err_real, err_imag = err_spec[:, :N2], err_spec[:, N2:]
        real, imag = spec[:, :N2], spec[:, N2:]
        total_real += err_real * real + err_imag * imag
        total_imag += err_imag * real - err_real * imag
    return total_real, total_imag


def conv_kernel(
    gain_ref, recv_ref, split_ref, fwd_ref, join_ref, mirror_ref, cols_ref, tw_ref,
    gap_ref, spec_ref, part_ref, *refs, early,
):
    *refs, y_rows = refs
    ctx, count = recv_ref.shape[:2]
    step = pl.program_id(0)
    q = step if early else step + EARLY
    if early:
        held_refs, early_refs = refs[:3], refs[3:]

        @pl.when(step == 0)
        def _():
            for held_ref, table_ref in zip(held_refs, (split_ref, fwd_ref, tw_ref)):
                held_ref[...] = table_ref[...]

    tw_cos, tw_sin = tw_ref[0], tw_ref[1]
    signals = []
    for d in range(count):
        clean = recv_ref[:, d, 0, q].reshape(N1, N2)
        perturb = recv_ref[:, d, 1, q].reshape(N1, N2)
        signals += [clean, (clean.astype(F32) + perturb.astype(F32)).astype(BF16)]
    spectra = forward(signals, split_ref, fwd_ref, tw_cos, tw_sin)
    filter_real, filter_imag = hermitian_part(
        recv_ref[:, 0, 2, q].reshape(N1, N2), recv_ref[:, 1, 2, q].reshape(N1, N2), mirror_ref[...], cols_ref[...]
    )
    products = []
    for spec in spectra:
        real, imag = spec[:, :N2], spec[:, N2:]
        prod_real = (filter_real * real - filter_imag * imag).astype(BF16)
        minus_imag = (-filter_real * imag - filter_imag * real).astype(BF16)
        products.append(jnp.concatenate([prod_real, minus_imag], 1))
    back = dot(jnp.concatenate(products, 0), fwd_ref[...])
    mixed, middle = [], []
    for i in range(2 * count):
        back_real, minus_imag = back[i * HALF : (i + 1) * HALF, :N2], back[i * HALF : (i + 1) * HALF, N2:]
        mixed_real = (back_real * tw_cos + minus_imag * tw_sin).astype(BF16)
        mixed_imag = (back_real * tw_sin - minus_imag * tw_cos).astype(BF16)
        mixed.append(jnp.concatenate([mixed_real[: N1 // 2], mixed_imag[: N1 // 2]], 0))
        middle.append(mixed_real[N1 // 2 :].astype(F32)[:1])
    conv = dot(join_ref[...], jnp.concatenate(mixed, 1))
    parity = lax.broadcasted_iota(jnp.int32, (N1, N2), 0) % 2
    alternate = (1 - 2 * parity).astype(F32) * (1.0 / (N1 * N2))
    gain = gain_ref[q]
    errors = []
    for d in range(count):
        pair = []
        for i in range(2):
            k = 2 * d + i
            wide = signals[k].astype(F32)
            filtered = conv[:, k * N2 : (k + 1) * N2] + alternate * middle[k]
            pair.append((wide, wide * filtered.astype(BF16).astype(F32) + gain * wide))
        (clean, clean_y), (shifted, shifted_y) = pair
        y_rows[d * ctx : (d + 1) * ctx] = clean_y.astype(BF16).reshape(ctx, -1, N2)
        gap = smart_weight * (shifted_y - clean_y)
        gap_ref[step, d] = gap
        spec_ref[step, d] = spectra[2 * d]
        errors.append((shifted * gap).astype(BF16))
    total_real, total_imag = gradient(forward(errors, split_ref, fwd_ref, tw_cos, tw_sin), spectra[1::2])
    part_ref[step, 0] = total_real
    part_ref[step, 1] = total_imag
    if early:
        near_count = early_refs[0].shape[0]
        here = place(near_count // count)
        for hop, early_ref in enumerate(early_refs):
            for j in range(near_count):
                side, block = peer(here, j, hop, near_count // count)
                early_ref[j, step] = y_rows[side * ctx + block]
    else:
        (send_ref,) = refs
        for d in range(count):
            send_ref[:, d, step] = y_rows[d * ctx : (d + 1) * ctx]


def grad_kernel(recv_ref, *refs, hops):
    first, second, refs = refs[:3], refs[3:6], refs[6:]
    cot_refs, refs = refs[:hops], refs[hops:]
    split_ref, fwd_ref, tw_ref, y_ref, send_ref, cot_rows, ready_ref, sems = refs
    copies = [pltpu.make_async_copy(y_ref, send_ref.at[:, :, pl.ds(0, y_ref.shape[2])], sems.at[0])]
    copies[0].start()
    ctx, count = recv_ref.shape[:2]
    near = cot_refs[0].shape[0]
    plane = near // count
    here = place(plane)
    per = recv_ref.shape[3]
    for hop, cot_ref in enumerate(cot_refs):
        for j in range(near):
            side, block = peer(here, j, hop, plane)
            cot_rows[side * ctx + block] = cot_ref[j]
    kept = [(first, q) if q < EARLY else (second, q - EARLY) for q in range(per)]
    errors = []
    for q, ((gap_ref, _, _), i) in enumerate(kept):
        for d in range(count):
            clean = recv_ref[:, d, 0, q].reshape(N1, N2).astype(F32)
            cot = cot_rows[d * ctx : (d + 1) * ctx, q].reshape(N1, N2).astype(F32)
            errors.append((clean * (cot - gap_ref[i, d])).astype(BF16))
    err_spectra = forward(errors, split_ref, fwd_ref, tw_ref[0], tw_ref[1])
    for q, ((_, spec_ref, part_ref), i) in enumerate(kept):
        spectra = [spec_ref[i, d] for d in range(count)]
        total = gradient(err_spectra[q * count : (q + 1) * count], spectra)
        fill_grad(ready_ref, q, *[t + part_ref[i, p] for p, t in enumerate(total)])
        copies.append(pltpu.make_async_copy(ready_ref.at[q], send_ref.at[:, :, per - EARLY + q], sems.at[1 + q]))
        copies[1 + q].start()
    for copy in copies:
        copy.wait()


def fill_grad(ready_ref, q, total_real, total_imag):
    _, ctx, count, rows, _ = ready_ref.shape
    total = jnp.concatenate([total_real, total_imag], 1) * (1.0 / (N1 * N2))
    upper, after = total[: N1 // 2], total[rows : N1 // 2 + rows]
    first = lax.broadcasted_iota(jnp.int32, upper.shape, 0) % rows == 0
    lower = jnp.where(first, after, upper).astype(BF16)
    upper = upper.astype(BF16)
    width = N2 // count
    for i in range(count):
        for half, x, side in ((0, upper, i), (1, lower, count - 1 - i)):
            cols = slice(side * width, (side + 1) * width)
            pair = jnp.concatenate([x[:, :N2][:, cols], x[:, N2:][:, cols]], 1)
            for block in range(ctx // 2):
                target = ctx - 1 - block if half else block
                ready_ref[q, target, i] = pair[block * rows : (block + 1) * rows]


def whole(x):
    return pl.BlockSpec(x.shape, lambda *_: (0,) * x.ndim)


def near(x):
    return pltpu.with_memory_space_constraint(x, pltpu.VMEM)


def far(x):
    return pltpu.with_memory_space_constraint(x, pltpu.HBM)


def conv_call(gain, received, tabs, plane, early):
    ctx, dp, _, per, rows, _ = received.shape
    split_rows, forward_table, *_, twiddle = tabs
    steps = EARLY if early else per - EARLY
    here = pl.BlockSpec(memory_space=pltpu.VMEM)
    if early:
        tabs, specs = [far(t) for t in tabs], [whole(t) for t in tabs]
        held = [pltpu.VMEM(t.shape, t.dtype) for t in (split_rows, forward_table, twiddle)]
        more = [*held, *[pltpu.VMEM((dp * plane, EARLY, rows, N2), BF16)] * (ctx // plane)]
    else:
        inside = (True, True, False, False, False, True)
        specs = [here if held else whole(t) for t, held in zip(tabs, inside)]
        tabs = [near(t) if held else far(t) for t, held in zip(tabs, inside)]
        more = [pltpu.VMEM((ctx, dp, steps, rows, N2), BF16)]
    return pl.pallas_call(
        functools.partial(conv_kernel, early=early),
        grid=(steps,),
        in_specs=[here, here, *specs],
        out_specs=[here] * (3 + len(more)),
        out_shape=[
            pltpu.VMEM((steps, dp, N1, N2), F32),
            pltpu.VMEM((steps, dp, HALF, 2 * N2), F32),
            pltpu.VMEM((steps, 2, HALF, N2), F32),
            *more,
        ],
        scratch_shapes=[pltpu.VMEM((dp * ctx, rows, N2), BF16)],
        compiler_params=pltpu.CompilerParams(vmem_limit_bytes=VMEM),
        cost_estimate=pl.CostEstimate(flops=steps * dp * 5 * 6 * N1**3, bytes_accessed=4 << 20, transcendentals=0),
        name="conv_early" if early else "conv_late",
    )(near(gain), received, *tabs)


def grad_call(received, kept, cots, send):
    ctx, dp, _, per, rows, _ = received.shape
    *kept, split_rows, forward_table, twiddle = [near(x) for x in kept]
    operands = (received, *kept, *[near(x) for x in cots], split_rows, forward_table, twiddle, near(send))
    return pl.pallas_call(
        functools.partial(grad_kernel, hops=len(cots)),
        grid=(1,),
        in_specs=[pl.BlockSpec(memory_space=pltpu.VMEM)] * len(operands),
        out_specs=pl.BlockSpec(memory_space=pl.ANY),
        out_shape=pltpu.HBM((ctx, dp, 2 * per - EARLY, rows, N2), BF16),
        scratch_shapes=[
            pltpu.VMEM((dp * ctx, per, rows, N2), BF16),
            pltpu.VMEM((per, ctx, dp, rows, N2), BF16),
            pltpu.SemaphoreType.DMA((1 + per,)),
        ],
        compiler_params=pltpu.CompilerParams(vmem_limit_bytes=VMEM),
        cost_estimate=pl.CostEstimate(flops=per * dp * 6 * N1**3, bytes_accessed=8 << 20, transcendentals=0),
        name="grad",
    )(*operands)


def outward_kernel(*refs, count):
    in_refs, refs = refs[:count], refs[count:]
    out_ref, refs = refs[0], refs[1:]
    held_refs, (rows_ref, ready_ref, load_sems, store_sems) = refs[:count], refs[count:]
    devices, _, per, rows, _ = out_ref.shape
    pitch = rows_ref.shape[1] // (devices * per)
    width = rows_ref.shape[2]
    loads, stores = [], []
    for t, (in_ref, held_ref) in enumerate(zip(in_refs, held_refs)):
        source = in_ref.at[lax.axis_index("dp") if in_ref.shape[0] > 1 else 0]
        loads.append(pltpu.make_async_copy(source, held_ref, load_sems.at[t]))
        loads[t].start()
    for t, held_ref in enumerate(held_refs):
        loads[t].wait()
        for h in range(N2 // width):
            lanes = slice(h * width, (h + 1) * width)
            for r in range(rows):
                block = held_ref[r, lanes].astype(BF16).T.astype(F32)
                rows_ref[h, pl.ds(r, devices * per, stride=pitch), :] = block
            block = rows_ref[h].reshape(devices, per, pitch, width)[:, :, :rows].astype(BF16)
            ready_ref[t, :, :, :, lanes] = block
        stores.append(pltpu.make_async_copy(ready_ref.at[t], out_ref.at[:, t], store_sems.at[t]))
        stores[t].start()
    for store in stores:
        store.wait()


def outward(arrays, devices):
    _, rows, _, channels = arrays[0].shape
    count, per, width, pitch = len(arrays), channels // devices, 128, rows + 8
    shape = (devices, count, per, rows, N2)
    return pl.pallas_call(
        functools.partial(outward_kernel, count=count),
        in_specs=[pl.BlockSpec(memory_space=pl.ANY)] * count,
        out_specs=pl.BlockSpec(memory_space=pl.ANY),
        out_shape=pltpu.HBM(shape, BF16),
        scratch_shapes=[
            *[pltpu.VMEM(a.shape[1:], a.dtype) for a in arrays],
            pltpu.VMEM((N2 // width, channels * pitch, width), F32),
            pltpu.VMEM((count, devices, per, rows, N2), BF16),
            pltpu.SemaphoreType.DMA((count,)),
            pltpu.SemaphoreType.DMA((count,)),
        ],
        compiler_params=pltpu.CompilerParams(vmem_limit_bytes=VMEM),
        cost_estimate=pl.CostEstimate(flops=0, bytes_accessed=7 << 20, transcendentals=0),
        name="outward",
    )(*arrays)


def outward_near_kernel(in_ref, *refs, hops, plane):
    here = place(plane)
    *out_refs, rows_ref = refs
    _, per, rows, width = out_refs[0].shape
    channels = in_ref.shape[3]
    pitch = rows_ref.shape[0] // channels
    for r in range(rows):
        rows_ref[pl.ds(r, channels, stride=pitch), :] = in_ref[0, r].T.astype(F32)
    for j, out_ref in enumerate(out_refs):
        for hop in range(hops):
            block = owner(here, j, hop, plane) * (per * pitch)
            rows_here = rows_ref[pl.ds(pl.multiple_of(block, per * pitch), per * pitch), :]
            out_ref[hop] = rows_here.reshape(per, pitch, width)[:, :rows].astype(BF16)


def outward_near(x, count, hops, plane):
    _, rows, _, channels = x.shape
    per = channels // count
    width = 128
    return pl.pallas_call(
        functools.partial(outward_near_kernel, hops=hops, plane=plane),
        grid=(N2 // width,),
        in_specs=[pl.BlockSpec((1, rows, width, channels), lambda h: (0, 0, h, 0))],
        out_specs=[pl.BlockSpec((hops, per, rows, width), lambda h: (0, 0, 0, h))] * (count // hops),
        out_shape=[jax.ShapeDtypeStruct((hops, per, rows, N2), BF16)] * (count // hops),
        scratch_shapes=[pltpu.VMEM((channels * (rows + 8), width), F32)],
        compiler_params=pltpu.CompilerParams(vmem_limit_bytes=VMEM),
        cost_estimate=pl.CostEstimate(flops=0, bytes_accessed=2 << 20, transcendentals=0),
        name="outward_near",
    )(x)


def regroup_kernel(*refs, count):
    for i, in_ref in enumerate(refs[:count]):
        for j, out_ref in enumerate(refs[count:]):
            out_ref[i] = in_ref[j]


def regroup(arrays):
    hops, *block = arrays[0].shape
    return pl.pallas_call(
        functools.partial(regroup_kernel, count=len(arrays)),
        out_shape=[jax.ShapeDtypeStruct((len(arrays), *block), BF16)] * hops,
        compiler_params=pltpu.CompilerParams(vmem_limit_bytes=VMEM),
        cost_estimate=pl.CostEstimate(flops=0, bytes_accessed=2 << 20, transcendentals=0),
        name="regroup",
    )(*arrays)


def homeward_kernel(last_ref, *refs, per):
    *early_refs, y_ref, grad_ref, rows_ref = refs
    count, _, rows, _ = last_ref.shape
    hops = early_refs[0].shape[0]
    plane = count // hops // 2
    here = place(plane)
    width = rows_ref.shape[2]
    pitch = rows_ref.shape[1] // (count * per)
    h = pl.program_id(0)
    lanes = pl.ds(pl.multiple_of(h * width, width), width)
    lower = lax.axis_index("ctx") >= lax.axis_size("ctx") // 2
    row = lax.broadcasted_iota(jnp.int32, (width, width), 0)
    col = lax.broadcasted_iota(jnp.int32, (width, width), 1)
    turn = (col == jnp.where(lower, width - 1 - row, row)).astype(F32)
    turn = (turn * jnp.where(lower, (1 - 2 * h).astype(F32), 1.0)).astype(BF16)
    y_rows = rows_ref.at[0].reshape(count, per, pitch, width)
    grad_rows = rows_ref.at[1].reshape(count, per, pitch, width)
    for j, early_ref in enumerate(early_refs):
        for hop in range(hops):
            y_rows[owner(here, j, hop, plane), :EARLY, :rows] = early_ref[hop, :, :, lanes].astype(F32)
    y_rows[:, EARLY:, :rows] = last_ref[:, : per - EARLY, :, lanes].astype(F32)
    block = last_ref[:, per - EARLY :, :, lanes]
    grad_rows[:, :, :rows] = dot(block.reshape(count * per * rows, width), turn).reshape(block.shape)
    for r in range(rows):
        y_ref[r] = rows_ref[0, pl.ds(r, count * per, stride=pitch), :].astype(BF16).T
    for r in range(rows):
        target = jnp.where(lower, (rows - r) % rows, r)
        grad_ref[0, target] = rows_ref[1, pl.ds(r, count * per, stride=pitch), :].T


def homeward(last, early):
    count, slots, rows, _ = last.shape
    per = (slots + EARLY) // 2
    channels, width, pitch = count * per, 128, rows + 8
    return pl.pallas_call(
        functools.partial(homeward_kernel, per=per),
        grid=(N2 // width,),
        in_specs=[pl.BlockSpec(memory_space=pltpu.VMEM)] * (1 + len(early)),
        out_specs=[
            pl.BlockSpec((rows, width, channels), lambda h: (0, h, 0)),
            pl.BlockSpec((1, rows, width, channels), lambda h: (h, 0, 0, 0)),
        ],
        out_shape=[
            jax.ShapeDtypeStruct((rows, N2, channels), BF16),
            jax.ShapeDtypeStruct((2, rows, width, channels), F32),
        ],
        scratch_shapes=[pltpu.VMEM((2, channels * pitch, width), F32)],
        compiler_params=pltpu.CompilerParams(vmem_limit_bytes=VMEM),
        cost_estimate=pl.CostEstimate(flops=0, bytes_accessed=5 << 20, transcendentals=0),
        name="homeward",
    )(near(last), *[near(x) for x in early])


def by_channel_body(embeds, perturb, cotangent, filter_spectrum, skip_gain):
    dp, ctx = lax.axis_size("dp"), lax.axis_size("ctx")
    d, c = lax.axis_index("dp"), lax.axis_index("ctx")
    axes, order = ("dp", "ctx"), ("ctx", "dp")
    count = dp * ctx
    channels = embeds.shape[2]
    rows = N1 // ctx
    per = channels // count
    plane = 4
    hops = ctx // plane
    tabs = tables()

    def matrix(x):
        return far(x.reshape(1, rows, N2, channels))

    def exchange(x, mask):
        return lax.ppermute(x, axes, [(i, i ^ mask) for i in range(count)]) if mask else x

    first = outward([matrix(embeds), matrix(perturb), far(filter_spectrum)], count)
    received = lax.all_to_all(first, order, 0, 0, tiled=True).reshape(ctx, dp, 3, per, rows, N2)
    cots = outward_near(matrix(cotangent), count, hops, plane)
    cots = regroup([exchange(x, j // plane * ctx + j % plane) for j, x in enumerate(cots)])
    received = near(received)
    cots = list(cots)
    cots[1] = exchange(cots[1], plane)
    cots[1], cots[2] = lax.optimization_barrier((cots[1], cots[2]))
    cots[3], received = lax.optimization_barrier((cots[3], received))
    cots[2:] = [exchange(x, (2 + i) * plane) for i, x in enumerate(cots[2:])]
    gain = lax.dynamic_slice(skip_gain, ((c * dp + d) * per,), (per,))
    gain = jnp.broadcast_to(gain[:, None, None], (per, 1, N2))
    outs = conv_call(gain, received, tabs, plane, True)
    kept, held, early = outs[:3], outs[3:6], outs[6:]
    early = [exchange(x, hop * plane) for hop, x in enumerate(early)]
    *kept_late, send = conv_call(gain, received, [*held[:2], *tabs[2:5], held[2]], plane, False)
    send = grad_call(received, [*kept, *kept_late, *held], cots, send)
    send, *early = lax.optimization_barrier((send, *early))
    send, *early = lax.optimization_barrier((send, *regroup(early)))
    last = lax.all_to_all(send.reshape(count, *send.shape[2:]), order, 0, 0, tiled=True)
    early = [exchange(x, j // plane * ctx + j % plane) for j, x in enumerate(early)]
    y, grad = homeward(last, early)
    return y.reshape(1, rows * N2, channels), grad


def trig_table(period):
    row_ids = jnp.arange(period, dtype=jnp.int32)
    exponent = row_ids[:, None] * row_ids[None, :] % period
    phase_angle = exponent.astype(jnp.float32) * (two_pi / period)
    return (jnp.cos(phase_angle).astype(jnp.bfloat16), jnp.sin(phase_angle).astype(jnp.bfloat16))


def twiddle(row_first, row_count, col_first, col_count):
    row_ids = row_first + jnp.arange(row_count, dtype=jnp.int32)
    col_ids = col_first + jnp.arange(col_count, dtype=jnp.int32)
    exponent = row_ids[:, None] * col_ids[None, :] % (N1 * N2)
    phase_angle = exponent.astype(jnp.float32) * (two_pi / (N1 * N2))
    return (jnp.cos(phase_angle)[:, :, None], jnp.sin(phase_angle)[:, :, None])


def first_section(values, col_start):
    cos_table, sin_table = trig_table(N1)
    part_real = jnp.einsum("kn,snmc->skmc", cos_table, values, preferred_element_type=jnp.float32)
    part_imag = -jnp.einsum("kn,snmc->skmc", sin_table, values, preferred_element_type=jnp.float32)
    tw_cos, tw_sin = twiddle(0, N1, col_start, values.shape[2])
    out_real = part_real * tw_cos + part_imag * tw_sin
    out_imag = part_imag * tw_cos - part_real * tw_sin
    return jnp.stack([out_real, out_imag], 1).astype(jnp.bfloat16)


def second_section(section_rows):
    cos_table, sin_table = trig_table(N2)
    with_cos = jnp.einsum(
        "sprnc,kn->sprkc", section_rows, cos_table, preferred_element_type=jnp.float32
    )
    with_sin = jnp.einsum(
        "sprnc,kn->sprkc", section_rows, sin_table, preferred_element_type=jnp.float32
    )
    return jnp.stack([with_cos[:, 0] + with_sin[:, 1], with_cos[:, 1] - with_sin[:, 0]], 1)


def spectral_inverse(product, row_start):
    cos_table, sin_table = trig_table(N2)
    with_cos = jnp.einsum("sprkc,nk->sprnc", product, cos_table, preferred_element_type=jnp.float32)
    with_sin = jnp.einsum("sprkc,nk->sprnc", product, sin_table, preferred_element_type=jnp.float32)
    part_real = with_cos[:, 0] - with_sin[:, 1]
    part_imag = with_cos[:, 1] + with_sin[:, 0]
    tw_cos, tw_sin = twiddle(row_start, product.shape[2], 0, N2)
    out_real = part_real * tw_cos - part_imag * tw_sin
    out_imag = part_imag * tw_cos + part_real * tw_sin
    return jnp.stack([out_real, out_imag], 1).astype(jnp.bfloat16)


def column_inverse(mixed_cols):
    cos_table, sin_table = trig_table(N1)
    with_cos = jnp.einsum(
        "nk,skmc->snmc", cos_table, mixed_cols[:, 0], preferred_element_type=jnp.float32
    )
    with_sin = jnp.einsum(
        "nk,skmc->snmc", sin_table, mixed_cols[:, 1], preferred_element_type=jnp.float32
    )
    return ((with_cos - with_sin) * (1.0 / (N1 * N2))).astype(jnp.bfloat16)


def to_spectrum(section_cols):
    return second_section(
        lax.all_to_all(section_cols, "ctx", split_axis=2, concat_axis=3, tiled=True)
    )


def error_terms(signal, filtered, skip_gain, cotangent_view):
    signal_wide = signal.astype(jnp.float32)
    filtered_wide = lax.optimization_barrier(filtered).astype(jnp.float32)
    outputs = signal_wide * filtered_wide + skip_gain * signal_wide
    clean_y = outputs[0]
    smooth_gap = outputs[1] - clean_y
    err_clean = signal_wide[0] * (cotangent_view.astype(jnp.float32) - smart_weight * smooth_gap)
    err_shift = signal_wide[1] * (smart_weight * smooth_gap)
    return (clean_y, jnp.stack([err_clean, err_shift], 0).astype(jnp.bfloat16))


def body(embeds, perturb, cotangent, filter_spectrum, skip_gain):
    ctx_size = lax.axis_size("ctx")
    ctx_index = lax.axis_index("ctx")
    channels = embeds.shape[2]
    row_count = N1 // ctx_size
    col_count = N2 // ctx_size
    row_start = ctx_index * row_count
    col_start = ctx_index * col_count
    clean_rows = embeds[0].reshape(row_count, N2, channels)
    perturb_rows = perturb[0].reshape(row_count, N2, channels)
    shifted = (clean_rows.astype(jnp.float32) + perturb_rows.astype(jnp.float32)).astype(
        jnp.bfloat16
    )
    inputs = jnp.stack([clean_rows, shifted], 0)
    signal_cols = lax.all_to_all(inputs, "ctx", split_axis=2, concat_axis=1, tiled=True)
    section_cols, signal_cols = (first_section(signal_cols, col_start), signal_cols)
    spectra = to_spectrum(section_cols)
    filter_real = filter_spectrum[0]
    filter_imag = filter_spectrum[1]
    spectrum_real = spectra[:, 0]
    spectrum_imag = spectra[:, 1]
    product = jnp.stack(
        [
            filter_real * spectrum_real - filter_imag * spectrum_imag,
            filter_real * spectrum_imag + filter_imag * spectrum_real,
        ],
        1,
    ).astype(jnp.bfloat16)
    mixed_rows = spectral_inverse(product, row_start)
    filtered = column_inverse(
        lax.all_to_all(mixed_rows, "ctx", split_axis=3, concat_axis=2, tiled=True)
    )
    cotangent_rows = cotangent[0].reshape(row_count, N2, channels)
    filtered_rows = lax.all_to_all(filtered, "ctx", split_axis=1, concat_axis=2, tiled=True)
    clean_y, errors = error_terms(inputs, filtered_rows, skip_gain, cotangent_rows)
    clean_output = clean_y.astype(jnp.bfloat16)
    error_section = first_section(
        lax.all_to_all(errors, "ctx", split_axis=2, concat_axis=1, tiled=True), col_start
    )
    error_spec = to_spectrum(error_section)
    error_real = error_spec[:, 0]
    error_imag = error_spec[:, 1]
    term_real = error_real * spectrum_real + error_imag * spectrum_imag
    term_imag = error_imag * spectrum_real - error_real * spectrum_imag
    local_grad = jnp.stack([term_real[0] + term_real[1], term_imag[0] + term_imag[1]], 0) * (
        1.0 / (N1 * N2)
    )
    grad_shard = lax.psum_scatter(
        local_grad.astype(jnp.bfloat16), "dp", scatter_dimension=2, tiled=True
    ).astype(jnp.float32)
    return (clean_output.reshape(1, row_count * N2, channels), grad_shard)


def solution(mesh):
    dp, ctx = mesh.shape["dp"], mesh.shape["ctx"]

    def run(embeds, *rest):
        apart = dp == 2 and embeds.shape[2] % (dp * ctx) == 0 and N1 // ctx == 16 and embeds.shape[2] // (dp * ctx) > 1
        return jax.shard_map(
            by_channel_body if apart else body,
            mesh=mesh,
            in_specs=(
                P("dp", "ctx", None),
                P("dp", "ctx", None),
                P("dp", "ctx", None),
                P(None, "ctx", None, None),
                P(),
            ),
            out_specs=(P("dp", "ctx", None), P(None, "ctx", "dp", None)),
            check_vma=False,
        )(embeds, *rest)

    return run
```
